32 devices in a mesh: mem: 8 (over y, x, core), tile: 4 (over z).
Axes of the slice: x: 2, y: 2, z: 4, core: 2. Of those that a mesh axis runs over, the one named last changes fastest.
Arguments:
- background: float32 [256, 128, 256], P('mem', 'tile'), may hold values from -6 to 6
- diffusion: float32 [256], replicated, may hold values from 0.05 to 0.2
- advection: float32 [256], replicated, may hold values from -0.25 to 0.25
- obs_where: int32 [4, 32, 512], P('tile'), may hold values from 0 to 255
- obs_count: int32 [4, 32], P('tile'), may hold values from 256 to 512
- obs_value: float32 [4, 32, 512], P('tile'), may hold values from -6 to 6
- obs_rinv: float32 [4, 32, 512], P('tile'), may hold values from 1 to 1000
Outputs:
- analysis: float32 [256, 128, 256], P('mem', 'tile')
The draws below stay inside these ranges and needn't reach their ends.
Inputs may be any that keep to these rules, and one draw needn't show every extreme that they name: `obs_where`: each slot reads one entry of its column's 4 * 64 state entries. A column uses its first obs_count slots.
All inputs are finite; a program needn't handle non-finite values.
Results may differ from the reference program's by a relative error of at most 0.0003.
Values sent between devices are 32-bit elements; how exact they have to be, the bound alone decides.
No kernel may reach another device: no remote copies, remote signals or barrier semaphores. Data moves between devices by JAX's collectives and lax.ppermute only.
A program may use at most 64 MiB of HBM per device.

```python
import math
import jax
import jax.numpy as jnp
from jax import lax

MEMBERS = 256
LEVELS = 64
VARS = 4
OBS_MAX = 512
ITERS = 12
COLS_TILE = 32
TILES = 4
COLS = 128


def plant(values, stream_key, smallest, high):
    extent = values.shape
    index_at = [jax.random.randint(jax.random.fold_in(stream_key, axis), (), 0, extent[axis]) for axis in range(len(extent))]
    values = values.at[tuple(index_at)].set(smallest)
    longest = extent.index(max(extent))
    index_at[longest] = (index_at[longest] + 1) % extent[longest]
    return values.at[tuple(index_at)].set(high)


def block_levels(rng, shape, cuts, least, top_value):
    gain, own = 1.0, jax.random.fold_in(rng, 6)
    for position, shards_of in cuts:
        steps = jnp.exp(jax.random.uniform(jax.random.fold_in(own, position), (shards_of,), jnp.float32, least / len(cuts), top_value / len(cuts)))
        gain = gain * jnp.repeat(steps, shape[position] // shards_of).reshape([-1 if axis == position else 1 for axis in range(len(shape))])
    return gain


def scatter_about(rng, extent, spread, bound, shards=(), kind=jnp.bfloat16):
    array = spread * jax.random.normal(rng, extent, jnp.float32)
    if shards:
        array = array * block_levels(rng, extent, shards, -0.22, 0.18)
    return jnp.clip(array, -bound, bound).astype(kind)


def setup_inputs(seed: int = 0) -> dict:
    keys = jax.random.split(jax.random.key(seed), 8)
    background = scatter_about(keys[0], (MEMBERS, COLS, VARS * LEVELS), 1.0, 6.0, ((0, 8), (1, 4)), jnp.float32)
    diffusion = jnp.clip(jax.random.uniform(keys[1], (VARS * LEVELS,), jnp.float32, 0.05, 0.2), 0.05, 0.2)
    advection = jnp.clip(jax.random.uniform(keys[2], (VARS * LEVELS,), jnp.float32, -0.25, 0.25), -0.25, 0.25)
    obs_where = plant(jax.random.randint(keys[3], (TILES, COLS_TILE, OBS_MAX), 0, VARS * LEVELS), jax.random.fold_in(keys[3], 1), 0, (VARS * LEVELS) - 1).astype(jnp.int32)
    obs_count = plant(jax.random.randint(keys[4], (TILES, COLS_TILE), OBS_MAX // 2, OBS_MAX + 1), jax.random.fold_in(keys[4], 1), OBS_MAX // 2, OBS_MAX).astype(jnp.int32)
    obs_value = scatter_about(keys[5], (TILES, COLS_TILE, OBS_MAX), 1.0, 6.0, ((0, 4),), jnp.float32)
    obs_rinv = jnp.clip(jnp.exp(math.log(1000.0) - 6.9077553 * jax.random.uniform(keys[6], (TILES, COLS_TILE, OBS_MAX), jnp.float32) ** block_levels(keys[6], (TILES, COLS_TILE, OBS_MAX), ((0, 4),), -0.2, 0.2)), 1.0, 1000.0)
    return {"background": background, "diffusion": diffusion, "advection": advection, "obs_where": obs_where, "obs_count": obs_count, "obs_value": obs_value, "obs_rinv": obs_rinv}


HIGH = lax.Precision.HIGHEST

def analyse(states, where, count, value, rinv):
    members = states.shape[0]
    entries = states.shape[2]
    slots = where.shape[1]
    mean = lax.optimization_barrier(jnp.mean(states, axis=0))
    anomaly = states - mean[None]
    mask = (jnp.arange(slots, dtype=jnp.int32)[None, :] < count[:, None]).astype(jnp.float32)
    onehot = (where[:, :, None] == jnp.arange(entries, dtype=jnp.int32)[None, None, :]).astype(jnp.float32) * mask[:, :, None]
    yb = jnp.einsum('npv,knv->npk', onehot, anomaly, precision=HIGH)
    innov = value - jnp.einsum('npv,nv->np', onehot, mean, precision=HIGH)
    weight_obs = rinv * mask
    eye = jnp.eye(members, dtype=jnp.float32)
    gram = (members - 1.0) * eye[None] + jnp.einsum('npk,npl->nkl', yb * weight_obs[:, :, None], yb, precision=HIGH)
    scale = jnp.sqrt(lax.optimization_barrier(jnp.sum(gram * gram, axis=(1, 2))))
    start_y = gram / scale[:, None, None]
    start_z = jnp.broadcast_to(eye[None], gram.shape)

    def newton(step, carry):
        iter_y, iter_z = carry
        middle = 1.5 * eye[None] - 0.5 * jnp.einsum('nij,njk->nik', iter_z, iter_y, precision=HIGH)
        return (jnp.einsum('nij,njk->nik', iter_y, middle, precision=HIGH), jnp.einsum('nij,njk->nik', middle, iter_z, precision=HIGH))
    final_y, final_z = lax.fori_loop(0, ITERS, newton, (start_y, start_z))
    weights = jnp.sqrt(members - 1.0) * final_z / jnp.sqrt(scale)[:, None, None]
    project = jnp.einsum('npk,np->nk', yb, weight_obs * innov, precision=HIGH)
    inner = jnp.einsum('nkl,nl->nk', final_z, project, precision=HIGH)
    wmean = jnp.einsum('nkl,nl->nk', final_z, inner, precision=HIGH) / scale[:, None]
    trans = weights + wmean[:, :, None]
    return mean[None] + jnp.einsum('nij,inv->jnv', trans, anomaly, precision=HIGH)

def advance(state, diffusion, advection):
    left = jnp.roll(state, 1, axis=1)
    right = jnp.roll(state, -1, axis=1)
    return state + diffusion * (left - 2.0 * state + right) + advection * (0.5 * (left - right))

def reference(background, diffusion, advection, obs_where, obs_count, obs_value, obs_rinv):
    state = background
    for step in range(2):
        state = advance(state, diffusion, advection)
    columns = jnp.transpose(state, (1, 0, 2))
    total = columns.shape[0]
    where = obs_where.reshape(total, -1)
    count = obs_count.reshape(total)
    value = obs_value.reshape(total, -1)
    rinv = obs_rinv.reshape(total, -1)

    def one_column(items):
        column, col_where, col_count, col_value, col_rinv = items
        result = analyse(column[:, None, :], col_where[None], col_count[None], col_value[None], col_rinv[None])
        return result[:, 0, :]
    result = lax.map(one_column, (columns, where, count, value, rinv))
    return jnp.transpose(result, (1, 0, 2))
```

```python
import jax
import jax.numpy as jnp
from jax import lax
from jax.experimental import pallas as pl
from jax.experimental.pallas import tpu as pltpu
from jax.sharding import PartitionSpec as P

PAIRS = 6
VMEM_BYTES = 48 * 1024 * 1024


def call(kernel, out_shape, flops, moved, **options):
    return pl.pallas_call(
        kernel,
        out_shape=out_shape,
        compiler_params=pltpu.CompilerParams(vmem_limit_bytes=VMEM_BYTES),
        cost_estimate=pl.CostEstimate(flops=flops, bytes_accessed=moved, transcendentals=0),
        **options,
    )


def split(x, parts):
    out = []
    for _ in range(parts):
        part = x.astype(jnp.bfloat16)
        out.append(part)
        x = x - part.astype(jnp.float32)
    return out


def dot3(a, b):
    lhs = jnp.concatenate([a[0], a[1], a[0]], axis=1)
    rhs = jnp.concatenate([b[0], b[0], b[1]], axis=0)
    return jnp.dot(lhs, rhs, preferred_element_type=jnp.float32)


def square_by_rows(parts):
    p0, p1, p2 = parts
    lhs = jnp.concatenate([p2, p0, p1, p1, p0, p0], axis=1)
    rhs = jnp.concatenate([p0, p2, p1, p0, p1, p0], axis=1)
    return lax.dot_general(lhs, rhs, (((1,), (1,)), ((), ())), preferred_element_type=jnp.float32)


def stencil(padded, diffusion, advection):
    middle = padded[1:-1]
    left = padded[:-2]
    right = padded[2:]
    return middle + diffusion * (left - 2.0 * middle + right) + advection * (0.5 * (left - right))


def inner_kernel(state_ref, diff_ref, adv_ref, out_ref):
    columns = state_ref.shape[1]
    quarter = columns // 4
    x = jnp.swapaxes(state_ref[...], 0, 1)[quarter - 2 : columns - quarter + 2]
    diffusion = diff_ref[...][None]
    advection = adv_ref[...][None]
    x = stencil(stencil(x, diffusion, advection), diffusion, advection)
    out_ref[...] = x.reshape(out_ref.shape)


def outer_kernel(state_ref, before_ref, after_ref, diff_ref, adv_ref, out_ref):
    columns = state_ref.shape[1]
    quarter = columns // 4
    x = jnp.swapaxes(state_ref[...], 0, 1)
    diffusion = diff_ref[...][None]
    advection = adv_ref[...][None]
    low = jnp.concatenate([before_ref[...], x[: quarter + 2]], axis=0)
    high = jnp.concatenate([x[columns - quarter - 2 :], after_ref[...]], axis=0)
    low = stencil(stencil(low, diffusion, advection), diffusion, advection)
    high = stencil(stencil(high, diffusion, advection), diffusion, advection)
    out_ref[...] = jnp.concatenate([low, high], axis=0).reshape(out_ref.shape)


def join_kernel(inner_ref, outer_ref, out_ref):
    members, columns, entries = out_ref.shape
    quarter = columns // 4
    inner = inner_ref[...].reshape(columns - 2 * quarter, members, entries)
    outer = outer_ref[...].reshape(2 * quarter, members, entries)
    x = jnp.concatenate([outer[:quarter], inner, outer[quarter:]], axis=0)
    out_ref[...] = jnp.swapaxes(x, 0, 1)


def observe_kernel(count_ref, where_ref, value_ref, rinv_ref, out_ref):
    columns, _, entries = out_ref.shape
    slots = where_ref.shape[1]
    slot = lax.broadcasted_iota(jnp.int32, (1, slots), 1)
    row = lax.broadcasted_iota(jnp.int32, (16, slots), 0)
    entry = lax.broadcasted_iota(jnp.int32, (entries, slots), 0)
    for c in range(columns):
        weight = jnp.where(slot < count_ref[c], rinv_ref[c : c + 1, :], 0.0)
        lhs = jnp.zeros((16, slots), jnp.float32)
        for first, source in ((0, weight), (3, weight * value_ref[c : c + 1, :])):
            for k, part in enumerate(split(source, 3)):
                lhs = jnp.where(row == first + k, part.astype(jnp.float32), lhs)
        onehot = (entry == where_ref[c : c + 1, :]).astype(jnp.float32).astype(jnp.bfloat16)
        sums = lax.dot_general(
            lhs.astype(jnp.bfloat16), onehot, (((1,), (1,)), ((), ())), preferred_element_type=jnp.float32
        )
        total = sums[0:1] + (sums[1:2] + sums[2:3])
        weighted = sums[3:4] + (sums[4:5] + sums[5:6])
        out_ref[c, 0:1] = total
        out_ref[c, 1:2] = weighted


def analyse_kernel(states_ref, obs_ref, out_ref, root_ref, ahead_ref):
    groups, columns, local, entries = states_ref.shape
    members = groups * local
    spread = members - 1.0
    rows = lax.broadcasted_iota(jnp.int32, (members, members), 0)
    cols = lax.broadcasted_iota(jnp.int32, (members, members), 1)
    means, forces, scales = [], [], []
    for c in range(columns):
        x = states_ref[:, c].reshape(members, entries)
        mean = jnp.sum(x, axis=0, keepdims=True) * (1.0 / members)
        anomaly = x - mean
        total = obs_ref[c, 0:1]
        forces.append(obs_ref[c, 1:2] - total * mean)
        gram = square_by_rows(split(anomaly * jnp.sqrt(total), 3))
        gram = gram + jnp.where(rows == cols, spread, 0.0)
        norm = jnp.sum(jnp.sum(gram * gram, axis=0, keepdims=True), axis=1, keepdims=True)
        scale = jnp.sqrt(norm)
        root_ref[c] = gram * (1.0 / scale)
        ahead_ref[c] = anomaly
        means.append(mean)
        scales.append(scale)

    def factor(c):
        s = root_ref[c]
        s_parts = split(s, 2)
        p = dot3(s_parts, s_parts)
        return 1.6875 * p - 2.4375 * s + dot3(split(p, 2), split(0.0625 * p - 0.5625 * s, 2))

    def pair(step, carry):
        for c in range(columns):
            r = split(factor(c), 2)
            s, w = root_ref[c], ahead_ref[c]
            ahead_ref[c] = 2.25 * w + dot3(r, split(w, 2))
            t = 2.25 * s + dot3(r, split(s, 2))
            root_ref[c] = 2.25 * t + dot3(r, split(t, 2))
        return carry

    lax.fori_loop(0, PAIRS - 1, pair, 0)
    for c in range(columns):
        r = split(factor(c), 2)
        w = ahead_ref[c]
        w = 2.25 * w + dot3(r, split(w, 2))
        inner = jnp.sum(w * forces[c], axis=1, keepdims=True)
        shift = jnp.sum(w * inner, axis=0, keepdims=True) / scales[c]
        result = means[c] + shift + w * jnp.sqrt(spread / scales[c])
        out_ref[:, c] = result.reshape(groups, local, entries)


def analyse(states, obs):
    groups, columns, local, entries = states.shape
    members = groups * local
    return call(
        analyse_kernel,
        jax.ShapeDtypeStruct(states.shape, jnp.float32),
        columns * 90 * 2 * members * members * entries,
        8 * states.size,
        scratch_shapes=[
            pltpu.VMEM((columns, members, members), jnp.float32),
            pltpu.VMEM((columns, members, entries), jnp.float32),
        ],
    )(states, obs)


def body(background, diffusion, advection, obs_where, obs_count, obs_value, obs_rinv):
    local, columns, entries = background.shape
    groups = lax.axis_size("mem")
    tiles = lax.axis_size("tile")
    half = columns // groups // 2
    quarter = columns // 4
    block = jax.ShapeDtypeStruct((groups, half, local, entries), jnp.float32)
    diffusion, advection = diffusion[None], advection[None]

    before = lax.ppermute(
        jnp.swapaxes(background[:, -2:], 0, 1), "tile", [(i, (i + 1) % tiles) for i in range(tiles)]
    )
    after = lax.ppermute(
        jnp.swapaxes(background[:, :2], 0, 1), "tile", [((i + 1) % tiles, i) for i in range(tiles)]
    )
    moved = 4 * background.size
    inner = call(inner_kernel, block, 20 * background.size, 2 * moved)(background, diffusion, advection)
    inner = lax.all_to_all(inner, "mem", split_axis=0, concat_axis=0, tiled=True)
    outer = call(outer_kernel, block, 20 * background.size, 2 * moved)(
        background, before, after, diffusion, advection
    )
    outer = lax.all_to_all(outer, "mem", split_axis=0, concat_axis=0, tiled=True)

    place = lax.axis_index("mem") * half
    starts = (quarter + place, jnp.where(place < quarter, place, place + 2 * quarter))

    def owned(array):
        return jnp.concatenate([lax.dynamic_slice_in_dim(array[0], start, half, 0) for start in starts], axis=0)

    obs = call(
        observe_kernel,
        jax.ShapeDtypeStruct((2 * half, 8, entries), jnp.float32),
        2 * half * 2 * 16 * obs_where.shape[2] * entries,
        2 * half * 3 * 4 * obs_where.shape[2],
        in_specs=[pl.BlockSpec(memory_space=pltpu.SMEM)] + [pl.BlockSpec(memory_space=pltpu.VMEM)] * 3,
    )(owned(obs_count), owned(obs_where), owned(obs_value), owned(obs_rinv))

    inner = analyse(inner, obs[:half])
    inner = lax.all_to_all(inner, "mem", split_axis=0, concat_axis=0, tiled=True)
    outer = analyse(outer, obs[half:])
    outer = lax.all_to_all(outer, "mem", split_axis=0, concat_axis=0, tiled=True)
    return call(join_kernel, jax.ShapeDtypeStruct(background.shape, jnp.float32), background.size, 2 * moved)(inner, outer)


def solution(mesh):
    return jax.shard_map(
        body,
        mesh=mesh,
        in_specs=(
            P("mem", "tile", None),
            P(),
            P(),
            P("tile", None, None),
            P("tile", None),
            P("tile", None, None),
            P("tile", None, None),
        ),
        out_specs=P("mem", "tile", None),
        check_vma=False,
    )
```

```python
import jax
import jax.numpy as jnp
from jax import lax
from jax.experimental import pallas as pl
from jax.experimental.pallas import tpu as pltpu
from jax.sharding import PartitionSpec as P

PAIRS = 6
VMEM_BYTES = 48 * 1024 * 1024
SMEM = pl.BlockSpec(memory_space=pltpu.SMEM)
VMEM = pl.BlockSpec(memory_space=pltpu.VMEM)
ANY = pl.BlockSpec(memory_space=pl.ANY)


def call(kernel, out_shape, flops, moved, **options):
    return pl.pallas_call(
        kernel,
        out_shape=out_shape,
        compiler_params=pltpu.CompilerParams(vmem_limit_bytes=VMEM_BYTES),
        cost_estimate=pl.CostEstimate(flops=flops, bytes_accessed=moved, transcendentals=0),
        **options,
    )


def owner(me, k, groups):
    if groups & (groups - 1) == 0:
        return me ^ k
    return lax.rem(me + k, groups)


def exchange(blocks, back):
    groups = len(blocks)
    out = [blocks[0]]
    for k in range(1, groups):
        if groups & (groups - 1) == 0:
            pairs = [(i, i ^ k) for i in range(groups)]
        else:
            pairs = [(i, (i + k) % groups) for i in range(groups)]
        if back:
            pairs = [(j, i) for i, j in pairs]
        out.append(lax.ppermute(blocks[k], "mem", pairs))
    return out


def split(x, parts):
    out = []
    for _ in range(parts):
        part = x.astype(jnp.bfloat16)
        out.append(part)
        x = x - part.astype(jnp.float32)
    return out


def dot3(a, b):
    lhs = jnp.concatenate([a[0], a[1], a[0]], axis=1)
    rhs = jnp.concatenate([b[0], b[0], b[1]], axis=0)
    return jnp.dot(lhs, rhs, preferred_element_type=jnp.float32)


def square_by_rows(parts):
    p0, p1, p2 = parts
    lhs = jnp.concatenate([p2, p0, p1, p1, p0, p0], axis=1)
    rhs = jnp.concatenate([p0, p2, p1, p0, p1, p0], axis=1)
    return lax.dot_general(lhs, rhs, (((1,), (1,)), ((), ())), preferred_element_type=jnp.float32)


def stencil(padded, diffusion, advection):
    middle = padded[1:-1]
    left = padded[:-2]
    right = padded[2:]
    return middle + diffusion * (left - 2.0 * middle + right) + advection * (0.5 * (left - right))


def inner_start(place, quarter):
    return place + quarter


def outer_start(place, quarter):
    return jnp.where(place < quarter, place, place + 2 * quarter)


def inner_kernel(me_ref, state_ref, diff_ref, adv_ref, *refs):
    *outs, low_ref, high_ref, held_ref, turned_ref, sems = refs
    groups = len(outs)
    half = outs[0].shape[0]
    members, columns, _ = state_ref.shape
    rows = members // sems.shape[0]
    copies = []
    for i in range(sems.shape[0]):
        copy = pltpu.make_async_copy(
            state_ref.at[pl.ds(i * rows, rows)], held_ref.at[pl.ds(i * rows, rows)], sems.at[i]
        )
        copy.start()
        copies.append(copy)
    for i, copy in enumerate(copies):
        copy.wait()
        turned_ref[:, i * rows : (i + 1) * rows] = jnp.swapaxes(held_ref[i * rows : (i + 1) * rows], 0, 1)
    diffusion = diff_ref[...][None]
    advection = adv_ref[...][None]
    for k in range(groups):
        first = inner_start(owner(me_ref[0], k, groups) * half, columns // 4)
        x = turned_ref[pl.ds(first - 2, half + 4)]
        outs[k][...] = stencil(stencil(x, diffusion, advection), diffusion, advection)
    low_ref[...] = turned_ref[:2]
    high_ref[...] = turned_ref[columns - 2 :]


def outer_kernel(me_ref, state_ref, before_ref, after_ref, diff_ref, adv_ref, *refs):
    *outs, turned_ref = refs
    groups = len(outs)
    half = outs[0].shape[0]
    columns = state_ref.shape[1]
    turned_ref[2 : columns + 2] = jnp.swapaxes(state_ref[...], 0, 1)
    turned_ref[:2] = before_ref[...]
    turned_ref[columns + 2 :] = after_ref[...]
    diffusion = diff_ref[...][None]
    advection = adv_ref[...][None]
    for k in range(groups):
        first = outer_start(owner(me_ref[0], k, groups) * half, columns // 4)
        x = turned_ref[pl.ds(first, half + 4)]
        outs[k][...] = stencil(stencil(x, diffusion, advection), diffusion, advection)


def join_kernel(me_ref, *refs):
    *blocks, out_ref, turned_ref = refs
    groups = len(blocks) // 2
    half = blocks[0].shape[0]
    quarter = out_ref.shape[1] // 4
    for k in range(groups):
        place = owner(me_ref[0], k, groups) * half
        turned_ref[pl.ds(inner_start(place, quarter), half)] = blocks[k][...]
        turned_ref[pl.ds(outer_start(place, quarter), half)] = blocks[groups + k][...]
    out_ref[...] = jnp.swapaxes(turned_ref[...], 0, 1)


def observe_kernel(me_ref, count_ref, where_ref, value_ref, rinv_ref, out_ref):
    columns, _, entries = out_ref.shape
    half = columns // 2
    quarter = where_ref.shape[0] // 4
    slots = where_ref.shape[1]
    place = me_ref[0] * half
    slot = lax.broadcasted_iota(jnp.int32, (1, slots), 1)
    row = lax.broadcasted_iota(jnp.int32, (16, slots), 0)
    entry = lax.broadcasted_iota(jnp.int32, (entries, slots), 0)
    for c in range(columns):
        at = inner_start(place, quarter) + c if c < half else outer_start(place, quarter) + c - half
        weight = jnp.where(slot < count_ref[0, at], rinv_ref[pl.ds(at, 1), :], 0.0)
        lhs = jnp.zeros((16, slots), jnp.float32)
        for first, source in ((0, weight), (3, weight * value_ref[pl.ds(at, 1), :])):
            for k, part in enumerate(split(source, 3)):
                lhs = jnp.where(row == first + k, part.astype(jnp.float32), lhs)
        onehot = (entry == where_ref[pl.ds(at, 1), :]).astype(jnp.float32).astype(jnp.bfloat16)
        sums = lax.dot_general(
            lhs.astype(jnp.bfloat16), onehot, (((1,), (1,)), ((), ())), preferred_element_type=jnp.float32
        )
        out_ref[c, 0:1] = sums[0:1] + (sums[1:2] + sums[2:3])
        out_ref[c, 1:2] = sums[3:4] + (sums[4:5] + sums[5:6])


def analyse_kernel(first, obs_ref, *refs):
    *blocks, root_ref, ahead_ref = refs
    groups = len(blocks) // 2
    states, outs = blocks[:groups], blocks[groups:]
    columns, local, entries = states[0].shape
    members = groups * local
    spread = members - 1.0
    every = range(columns)
    rows = lax.broadcasted_iota(jnp.int32, (members, members), 0)
    cols = lax.broadcasted_iota(jnp.int32, (members, members), 1)
    means, forces, scales, grams = [], [], [], []
    for c in every:
        x = jnp.concatenate([ref[c] for ref in states], axis=0)
        mean = jnp.sum(x, axis=0, keepdims=True) * (1.0 / members)
        anomaly = x - mean
        total = obs_ref[first + c, 0:1]
        forces.append(obs_ref[first + c, 1:2] - total * mean)
        means.append(mean)
        ahead_ref[c] = anomaly
        grams.append(square_by_rows(split(anomaly * jnp.sqrt(total), 3)))
    for c in every:
        gram = grams[c] + jnp.where(rows == cols, spread, 0.0)
        norm = jnp.sum(jnp.sum(gram * gram, axis=0, keepdims=True), axis=1, keepdims=True)
        scales.append(jnp.sqrt(norm))
        root_ref[c] = gram * (1.0 / scales[c])

    def factors():
        s = [split(root_ref[c], 2) for c in every]
        p = [dot3(s[c], s[c]) for c in every]
        cubic = [dot3(split(p[c], 2), split(0.0625 * p[c] - 0.5625 * root_ref[c], 2)) for c in every]
        return s, [split(1.6875 * p[c] - 2.4375 * root_ref[c] + cubic[c], 2) for c in every]

    def pair(step, carry):
        s, r = factors()
        t = [2.25 * root_ref[c] + dot3(r[c], s[c]) for c in every]
        for c in every:
            ahead_ref[c] = 2.25 * ahead_ref[c] + dot3(r[c], split(ahead_ref[c], 2))
        for c in every:
            root_ref[c] = 2.25 * t[c] + dot3(r[c], split(t[c], 2))
        return carry

    lax.fori_loop(0, PAIRS - 1, pair, 0)
    _, r = factors()
    ahead = [2.25 * ahead_ref[c] + dot3(r[c], split(ahead_ref[c], 2)) for c in every]
    for c in every:
        w = ahead[c]
        inner = jnp.sum(w * forces[c], axis=1, keepdims=True)
        shift = jnp.sum(w * inner, axis=0, keepdims=True) / scales[c]
        result = means[c] + shift + w * jnp.sqrt(spread / scales[c])
        for k in range(groups):
            outs[k][c] = result[k * local : (k + 1) * local]


def analyse(states, obs, first):
    groups = len(states)
    columns, local, entries = states[0].shape
    members = groups * local

    def kernel(*refs):
        analyse_kernel(first, *refs)

    return call(
        kernel,
        [jax.ShapeDtypeStruct(states[0].shape, jnp.float32)] * groups,
        columns * 90 * 2 * members * members * entries,
        8 * columns * members * entries,
        scratch_shapes=[
            pltpu.VMEM((columns, members, members), jnp.float32),
            pltpu.VMEM((columns, members, entries), jnp.float32),
        ],
    )(obs, *states)


def body(background, diffusion, advection, obs_where, obs_count, obs_value, obs_rinv):
    local, columns, entries = background.shape
    groups = lax.axis_size("mem")
    tiles = lax.axis_size("tile")
    half = columns // groups // 2
    size = background.size
    blocks = [jax.ShapeDtypeStruct((half, local, entries), jnp.float32)] * groups
    edge = jax.ShapeDtypeStruct((2, local, entries), jnp.float32)
    diffusion, advection = diffusion[None], advection[None]
    me = lax.axis_index("mem")[None].astype(jnp.int32)
    pieces = local // 8 if local % 8 == 0 else 1

    *inner, low, high = call(
        inner_kernel,
        blocks + [edge, edge],
        20 * size,
        8 * size,
        in_specs=[SMEM, ANY, VMEM, VMEM],
        scratch_shapes=[
            pltpu.VMEM(background.shape, jnp.float32),
            pltpu.VMEM((columns, local, entries), jnp.float32),
            pltpu.SemaphoreType.DMA((pieces,)),
        ],
    )(me, background, diffusion, advection)
    inner = exchange(inner, False)
    before = lax.ppermute(high, "tile", [(i, (i + 1) % tiles) for i in range(tiles)])
    after = lax.ppermute(low, "tile", [((i + 1) % tiles, i) for i in range(tiles)])
    outer = call(
        outer_kernel,
        blocks,
        20 * size,
        8 * size,
        in_specs=[SMEM] + [VMEM] * 5,
        scratch_shapes=[pltpu.VMEM((columns + 4, local, entries), jnp.float32)],
    )(me, background, before, after, diffusion, advection)
    outer = exchange(outer, False)
    obs = call(
        observe_kernel,
        jax.ShapeDtypeStruct((2 * half, 8, entries), jnp.float32),
        2 * half * 2 * 16 * obs_where.shape[2] * entries,
        12 * obs_where.size,
        in_specs=[SMEM, SMEM] + [VMEM] * 3,
    )(me, obs_count, obs_where[0], obs_value[0], obs_rinv[0])

    inner = exchange(analyse(inner, obs, 0), True)
    outer = exchange(analyse(outer, obs, half), True)
    return call(
        join_kernel,
        jax.ShapeDtypeStruct(background.shape, jnp.float32),
        size,
        8 * size,
        in_specs=[SMEM] + [VMEM] * (2 * groups),
        scratch_shapes=[pltpu.VMEM((columns, local, entries), jnp.float32)],
    )(me, *inner, *outer)


def solution(mesh):
    return jax.shard_map(
        body,
        mesh=mesh,
        in_specs=(
            P("mem", "tile", None),
            P(),
            P(),
            P("tile", None, None),
            P("tile", None),
            P("tile", None, None),
            P("tile", None, None),
        ),
        out_specs=P("mem", "tile", None),
        check_vma=False,
    )
```

```python
import jax
import jax.numpy as jnp
from jax import lax
from jax.experimental import pallas as pl
from jax.experimental.pallas import tpu as pltpu
from jax.sharding import PartitionSpec as P

PAIRS = 6
VMEM_BYTES = 48 * 1024 * 1024
SMEM = pl.BlockSpec(memory_space=pltpu.SMEM)
VMEM = pl.BlockSpec(memory_space=pltpu.VMEM)
HBM = pl.BlockSpec(memory_space=pltpu.HBM)


def call(kernel, out_shape, flops, moved, vmem=VMEM_BYTES, **options):
    return pl.pallas_call(
        kernel,
        out_shape=out_shape,
        compiler_params=pltpu.CompilerParams(vmem_limit_bytes=vmem),
        cost_estimate=pl.CostEstimate(flops=flops, bytes_accessed=moved, transcendentals=0),
        **options,
    )


def owner(me, chip, other):
    return 2 * chip + (me & 1 ^ other)


def exchange(blocks):
    chips = blocks.shape[0]
    same = [[2 * chip + core for chip in range(chips)] for core in range(2)]
    blocks = lax.all_to_all(blocks, "mem", split_axis=0, concat_axis=0, axis_index_groups=same, tiled=True)
    return blocks, lax.ppermute(blocks[:, 1], "mem", [(i, i ^ 1) for i in range(2 * chips)])


def split(x, parts):
    out = []
    for _ in range(parts):
        part = x.astype(jnp.bfloat16)
        out.append(part)
        x = x - part.astype(jnp.float32)
    return out


def dot3(a, b):
    lhs = jnp.concatenate([a[0], a[1], a[0]], axis=1)
    rhs = jnp.concatenate([b[0], b[0], b[1]], axis=0)
    return jnp.dot(lhs, rhs, preferred_element_type=jnp.float32)


def square_by_rows(parts):
    p0, p1, p2 = parts
    lhs = jnp.concatenate([p2, p0, p1, p1, p0, p0], axis=1)
    rhs = jnp.concatenate([p0, p2, p1, p0, p1, p0], axis=1)
    return lax.dot_general(lhs, rhs, (((1,), (1,)), ((), ())), preferred_element_type=jnp.float32)


def stencil(padded, diffusion, advection):
    middle = padded[1:-1]
    left = padded[:-2]
    right = padded[2:]
    return middle + diffusion * (left - 2.0 * middle + right) + advection * (0.5 * (left - right))


def inner_start(place, quarter):
    return place + quarter


def outer_start(place, quarter):
    return jnp.where(place < quarter, place, place + 2 * quarter)


def forecast(me, turned_ref, diffusion, advection, out_ref, start):
    chips, _, half, _, _ = out_ref.shape
    for chip in range(chips):
        for other in range(2):
            x = turned_ref[pl.ds(start(owner(me, chip, other) * half), half + 4)]
            out_ref[chip, other] = stencil(stencil(x, diffusion, advection), diffusion, advection)


def inner_kernel(me_ref, state_ref, diff_ref, adv_ref, out_ref, low_ref, high_ref, held_ref, turned_ref, num_ref, sems):
    members, columns, _ = state_ref.shape
    pieces = sems.shape[0] - 2
    rows = members // pieces
    copies = []
    for i in range(pieces):
        part = pl.ds(i * rows, rows)
        copies.append(pltpu.make_async_copy(state_ref.at[part], held_ref.at[part], sems.at[i]))
    copies.append(pltpu.make_async_copy(diff_ref, num_ref.at[0], sems.at[pieces]))
    copies.append(pltpu.make_async_copy(adv_ref, num_ref.at[1], sems.at[pieces + 1]))
    for copy in copies:
        copy.start()
    for i in range(pieces):
        copies[i].wait()
        turned_ref[:, i * rows : (i + 1) * rows] = jnp.swapaxes(held_ref[i * rows : (i + 1) * rows], 0, 1)
    copies[pieces].wait()
    copies[pieces + 1].wait()
    quarter = columns // 4
    forecast(me_ref[0], turned_ref, num_ref[0:1], num_ref[1:2], out_ref, lambda place: place + (quarter - 2))
    low_ref[...] = turned_ref[:2]
    high_ref[...] = turned_ref[columns - 2 :]


def outer_kernel(me_ref, state_ref, before_ref, after_ref, diff_ref, adv_ref, out_ref, turned_ref):
    columns = state_ref.shape[1]
    turned_ref[2 : columns + 2] = jnp.swapaxes(state_ref[...], 0, 1)
    turned_ref[:2] = before_ref[...]
    turned_ref[columns + 2 :] = after_ref[...]
    quarter = columns // 4
    forecast(
        me_ref[0],
        turned_ref,
        diff_ref[...],
        adv_ref[...],
        out_ref,
        lambda place: outer_start(place, quarter),
    )


def join_kernel(me_ref, inner_ref, inner_other_ref, outer_ref, outer_other_ref, out_ref, turned_ref):
    chips, _, half, _, _ = inner_ref.shape
    quarter = out_ref.shape[1] // 4
    for chip in range(chips):
        for other in range(2):
            place = owner(me_ref[0], chip, other) * half
            for start, pair in ((inner_start, (inner_ref, inner_other_ref)), (outer_start, (outer_ref, outer_other_ref))):
                block = pair[1][chip] if other else pair[0][chip, 0]
                turned_ref[pl.ds(start(place, quarter), half)] = block
    out_ref[...] = jnp.swapaxes(turned_ref[...], 0, 1)


def observe_kernel(me_ref, count_ref, where_ref, value_ref, rinv_ref, out_ref):
    columns, _, entries = out_ref.shape
    half = columns // 2
    quarter = where_ref.shape[0] // 4
    slots = where_ref.shape[1]
    place = me_ref[0] * half
    slot = lax.broadcasted_iota(jnp.int32, (1, slots), 1)
    row = lax.broadcasted_iota(jnp.int32, (16, slots), 0)
    entry = lax.broadcasted_iota(jnp.int32, (entries, slots), 0)
    for c in range(columns):
        at = inner_start(place, quarter) + c if c < half else outer_start(place, quarter) + c - half
        weight = jnp.where(slot < count_ref[0, at], rinv_ref[pl.ds(at, 1), :], 0.0)
        lhs = jnp.zeros((16, slots), jnp.float32)
        for first, source in ((0, weight), (3, weight * value_ref[pl.ds(at, 1), :])):
            for k, part in enumerate(split(source, 3)):
                lhs = jnp.where(row == first + k, part.astype(jnp.float32), lhs)
        onehot = (entry == where_ref[pl.ds(at, 1), :]).astype(jnp.float32).astype(jnp.bfloat16)
        sums = lax.dot_general(
            lhs.astype(jnp.bfloat16), onehot, (((1,), (1,)), ((), ())), preferred_element_type=jnp.float32
        )
        out_ref[c, 0:1] = sums[0:1] + (sums[1:2] + sums[2:3])
        out_ref[c, 1:2] = sums[3:4] + (sums[4:5] + sums[5:6])


def analyse_kernel(first, obs_ref, same_ref, other_ref, out_ref, root_ref, ahead_ref):
    chips, _, columns, local, entries = same_ref.shape
    members = 2 * chips * local
    spread = members - 1.0
    every = range(columns)
    rows = lax.broadcasted_iota(jnp.int32, (members, members), 0)
    cols = lax.broadcasted_iota(jnp.int32, (members, members), 1)
    means, forces, scales, grams = [], [], [], []
    for c in every:
        x = jnp.concatenate([same_ref[k, 0, c] for k in range(chips)] + [other_ref[k, c] for k in range(chips)], axis=0)
        mean = jnp.sum(x, axis=0, keepdims=True) * (1.0 / members)
        anomaly = x - mean
        total = obs_ref[first + c, 0:1]
        forces.append(obs_ref[first + c, 1:2] - total * mean)
        means.append(mean)
        ahead_ref[c] = anomaly.T
        grams.append(square_by_rows(split(anomaly * jnp.sqrt(total), 3)))
    for c in every:
        gram = grams[c] + jnp.where(rows == cols, spread, 0.0)
        norm = jnp.sum(jnp.sum(gram * gram, axis=0, keepdims=True), axis=1, keepdims=True)
        scales.append(jnp.sqrt(norm))
        root_ref[c] = gram * (1.0 / scales[c])

    def factors():
        s = [split(root_ref[c], 2) for c in every]
        p = [dot3(s[c], s[c]) for c in every]
        cubic = [dot3(split(p[c], 2), split(0.0625 * p[c] - 0.5625 * root_ref[c], 2)) for c in every]
        return s, [split(1.6875 * p[c] - 2.4375 * root_ref[c] + cubic[c], 2) for c in every]

    def pair(step, carry):
        s, r = factors()
        t = []
        for c in every:
            w = split(ahead_ref[c], 2)
            both = dot3([jnp.concatenate([s[c][i], w[i]], axis=0) for i in range(2)], r[c])
            t.append(2.25 * root_ref[c] + both[:members])
            ahead_ref[c] = 2.25 * ahead_ref[c] + both[members:]
        for c in every:
            root_ref[c] = 2.25 * t[c] + dot3(split(t[c], 2), r[c])
        return carry

    lax.fori_loop(0, PAIRS - 1, pair, 0)
    _, r = factors()
    ahead = [2.25 * ahead_ref[c] + dot3(split(ahead_ref[c], 2), r[c]) for c in every]
    for c in every:
        w = ahead[c].T
        inner = jnp.sum(w * forces[c], axis=1, keepdims=True)
        shift = jnp.sum(w * inner, axis=0, keepdims=True) / scales[c]
        result = means[c] + shift + w * jnp.sqrt(spread / scales[c])
        for k in range(2 * chips):
            out_ref[k % chips, k // chips, c] = result[k * local : (k + 1) * local]


def analyse(states, obs, first):
    same, other = states
    chips, _, columns, local, entries = same.shape
    members = 2 * chips * local

    def kernel(*refs):
        analyse_kernel(first, *refs)

    return call(
        kernel,
        jax.ShapeDtypeStruct(same.shape, jnp.float32),
        columns * 90 * 2 * members * members * entries,
        8 * columns * members * entries,
        scratch_shapes=[
            pltpu.VMEM((columns, members, members), jnp.float32),
            pltpu.VMEM((columns, entries, members), jnp.float32),
        ],
    )(obs, same, other)


def body(background, diffusion, advection, obs_where, obs_count, obs_value, obs_rinv):
    local, columns, entries = background.shape
    groups = lax.axis_size("mem")
    tiles = lax.axis_size("tile")
    half = columns // groups // 2
    size = background.size
    blocks = jax.ShapeDtypeStruct((groups // 2, 2, half, local, entries), jnp.float32)
    edge = jax.ShapeDtypeStruct((2, local, entries), jnp.float32)
    me = lax.axis_index("mem")[None].astype(jnp.int32)
    pieces = local // 8 if local % 8 == 0 else 1

    inner, low, high = call(
        inner_kernel,
        [blocks, edge, edge],
        20 * size,
        8 * size,
        vmem=61440 * 1024,
        in_specs=[SMEM, HBM, HBM, HBM],
        scratch_shapes=[
            pltpu.VMEM(background.shape, jnp.float32),
            pltpu.VMEM((columns, local, entries), jnp.float32),
            pltpu.VMEM((8, entries), jnp.float32),
            pltpu.SemaphoreType.DMA((pieces + 2,)),
        ],
    )(me, background, diffusion, advection)
    inner = exchange(inner)
    before = lax.ppermute(high, "tile", [(i, (i + 1) % tiles) for i in range(tiles)])
    after = lax.ppermute(low, "tile", [((i + 1) % tiles, i) for i in range(tiles)])
    outer = call(
        outer_kernel,
        blocks,
        20 * size,
        8 * size,
        in_specs=[SMEM] + [VMEM] * 5,
        scratch_shapes=[pltpu.VMEM((columns + 4, local, entries), jnp.float32)],
    )(me, background, before, after, diffusion[None], advection[None])
    outer = exchange(outer)
    obs = call(
        observe_kernel,
        jax.ShapeDtypeStruct((2 * half, 8, entries), jnp.float32),
        2 * half * 2 * 16 * obs_where.shape[2] * entries,
        12 * obs_where.size,
        in_specs=[SMEM, SMEM] + [VMEM] * 3,
    )(me, obs_count, obs_where[0], obs_value[0], obs_rinv[0])

    inner = exchange(analyse(inner, obs, 0))
    outer = exchange(analyse(outer, obs, half))
    return call(
        join_kernel,
        jax.ShapeDtypeStruct(background.shape, jnp.float32),
        size,
        8 * size,
        in_specs=[SMEM] + [VMEM] * 4,
        scratch_shapes=[pltpu.VMEM((columns, local, entries), jnp.float32)],
    )(me, *inner, *outer)


def solution(mesh):
    return jax.shard_map(
        body,
        mesh=mesh,
        in_specs=(
            P("mem", "tile", None),
            P(),
            P(),
            P("tile", None, None),
            P("tile", None),
            P("tile", None, None),
            P("tile", None, None),
        ),
        out_specs=P("mem", "tile", None),
        check_vma=False,
    )
```

```python
import jax
import jax.numpy as jnp
from jax import lax
from jax.experimental import pallas as pl
from jax.experimental.pallas import tpu as pltpu
from jax.sharding import PartitionSpec as P

PAIRS = 6
MIB = 1024 * 1024
SMEM = pl.BlockSpec(memory_space=pltpu.SMEM)
VMEM = pl.BlockSpec(memory_space=pltpu.VMEM)
HBM = pl.BlockSpec(memory_space=pltpu.HBM)


def call(kernel, out_shape, flops, moved, vmem=48 * MIB, **options):
    return pl.pallas_call(
        kernel,
        out_shape=out_shape,
        compiler_params=pltpu.CompilerParams(vmem_limit_bytes=vmem),
        cost_estimate=pl.CostEstimate(flops=flops, bytes_accessed=moved, transcendentals=0),
        **options,
    )


def owner(me, k, groups):
    if groups & (groups - 1) == 0:
        return me ^ k
    return lax.rem(me + k, groups)


def exchange(blocks, back):
    groups = len(blocks)
    out = [blocks[0]]
    for k in range(1, groups):
        if groups & (groups - 1) == 0:
            pairs = [(i, i ^ k) for i in range(groups)]
        else:
            pairs = [(i, (i + k) % groups) for i in range(groups)]
        if back:
            pairs = [(j, i) for i, j in pairs]
        out.append(lax.ppermute(blocks[k], "mem", pairs))
    return out


def split(x, parts):
    out = []
    for _ in range(parts):
        part = x.astype(jnp.bfloat16)
        out.append(part)
        x = x - part.astype(jnp.float32)
    return out


def dot3(a, b):
    lhs = jnp.concatenate([a[0], a[1], a[0]], axis=1)
    rhs = jnp.concatenate([b[0], b[0], b[1]], axis=0)
    middle = lhs.shape[0] // 2
    upper = jnp.dot(lhs[:middle], rhs, preferred_element_type=jnp.float32)
    lower = jnp.dot(lhs[middle:], rhs, preferred_element_type=jnp.float32)
    return jnp.concatenate([upper, lower], axis=0)


def square_by_rows(parts):
    p0, p1, p2 = parts
    lhs = jnp.concatenate([p2, p0, p1, p1, p0, p0], axis=1)
    rhs = jnp.concatenate([p0, p2, p1, p0, p1, p0], axis=1)
    return lax.dot_general(lhs, rhs, (((1,), (1,)), ((), ())), preferred_element_type=jnp.float32)


def stencil(padded, diffusion, advection):
    middle = padded[1:-1]
    left = padded[:-2]
    right = padded[2:]
    return middle + diffusion * (left - 2.0 * middle + right) + advection * (0.5 * (left - right))


def inner_start(place, quarter):
    return place + quarter


def outer_start(place, quarter):
    return jnp.where(place < quarter, place, place + 2 * quarter)


def pieces_of(members):
    rows = 8 if members % 8 == 0 else members
    return [pl.ds(first, rows) for first in range(0, members, rows)]


def inner_kernel(state_ref, diff_ref, adv_ref, out_ref, low_ref, high_ref, held_ref, num_ref, edge_ref, made_ref, sems):
    members, columns, entries = state_ref.shape
    groups, half, _, _ = out_ref.shape
    quarter = columns // 4
    pieces = pieces_of(members)
    count = len(pieces)
    reads = [pltpu.make_async_copy(state_ref.at[part], held_ref.at[part], sems.at[i]) for i, part in enumerate(pieces)]
    reads.append(pltpu.make_async_copy(diff_ref, num_ref.at[0], sems.at[count]))
    reads.append(pltpu.make_async_copy(adv_ref, num_ref.at[1], sems.at[count + 1]))
    for copy in reads[count:] + reads[:count]:
        copy.start()
    reads[count].wait()
    reads[count + 1].wait()
    diffusion = num_ref[0:1][None]
    advection = num_ref[1:2][None]
    writes = []
    for i, part in enumerate(pieces):
        reads[i].wait()
        x = jnp.swapaxes(held_ref[part], 0, 1)
        edge_ref[0, :, part] = x[:2]
        edge_ref[1, :, part] = x[columns - 2 :]
        x = x[quarter - 2 : columns - quarter + 2]
        x = stencil(stencil(x, diffusion, advection), diffusion, advection)
        made_ref[:, :, part] = x.reshape(groups, half, part.size, entries)
        copy = pltpu.make_async_copy(made_ref.at[:, :, part], out_ref.at[:, :, part], sems.at[count + 2 + i])
        copy.start()
        writes.append(copy)
    for i, ref in enumerate((low_ref, high_ref)):
        copy = pltpu.make_async_copy(edge_ref.at[i], ref, sems.at[2 * count + 2 + i])
        copy.start()
        writes.append(copy)
    for copy in writes:
        copy.wait()


def outer_kernel(me_ref, state_ref, before_ref, after_ref, diff_ref, adv_ref, *refs):
    *outs, turned_ref = refs
    groups = len(outs)
    half = outs[0].shape[0]
    columns = state_ref.shape[1]
    turned_ref[2 : columns + 2] = jnp.swapaxes(state_ref[...], 0, 1)
    turned_ref[:2] = before_ref[...]
    turned_ref[columns + 2 :] = after_ref[...]
    diffusion = diff_ref[...][None]
    advection = adv_ref[...][None]
    for k in range(groups):
        first = outer_start(owner(me_ref[0], k, groups) * half, columns // 4)
        x = turned_ref[pl.ds(first, half + 4)]
        outs[k][...] = stencil(stencil(x, diffusion, advection), diffusion, advection)


def join_kernel(me_ref, inner_ref, *refs):
    *outer, out_ref, turned_ref, made_ref, sems = refs
    members, columns, entries = out_ref.shape
    groups, half, _, _ = inner_ref.shape
    quarter = columns // 4
    writes = []
    for i, part in enumerate(pieces_of(members)):
        for k in range(groups):
            place = owner(me_ref[0], k, groups) * half
            turned_ref[pl.ds(outer_start(place, quarter), half), part] = outer[k][:, part]
        turned_ref[quarter : columns - quarter, part] = inner_ref[:, :, part].reshape(groups * half, part.size, entries)
        made_ref[part] = jnp.swapaxes(turned_ref[:, part], 0, 1)
        copy = pltpu.make_async_copy(made_ref.at[part], out_ref.at[part], sems.at[i])
        copy.start()
        writes.append(copy)
    for copy in writes:
        copy.wait()


def observe_kernel(me_ref, count_ref, where_ref, value_ref, rinv_ref, out_ref):
    columns, _, entries = out_ref.shape
    half = columns // 2
    quarter = where_ref.shape[0] // 4
    slots = where_ref.shape[1]
    place = me_ref[0] * half
    slot = lax.broadcasted_iota(jnp.int32, (1, slots), 1)
    row = lax.broadcasted_iota(jnp.int32, (16, slots), 0)
    entry = lax.broadcasted_iota(jnp.int32, (entries, slots), 0)
    for c in range(columns):
        at = inner_start(place, quarter) + c if c < half else outer_start(place, quarter) + c - half
        weight = jnp.where(slot < count_ref[0, at], rinv_ref[pl.ds(at, 1), :], 0.0)
        lhs = jnp.zeros((16, slots), jnp.float32)
        for first, source in ((0, weight), (3, weight * value_ref[pl.ds(at, 1), :])):
            for k, part in enumerate(split(source, 3)):
                lhs = jnp.where(row == first + k, part.astype(jnp.float32), lhs)
        onehot = (entry == where_ref[pl.ds(at, 1), :]).astype(jnp.float32).astype(jnp.bfloat16)
        sums = lax.dot_general(
            lhs.astype(jnp.bfloat16), onehot, (((1,), (1,)), ((), ())), preferred_element_type=jnp.float32
        )
        out_ref[c, 0:1] = sums[0:1] + (sums[1:2] + sums[2:3])
        out_ref[c, 1:2] = sums[3:4] + (sums[4:5] + sums[5:6])


def analyse_kernel(first, groups, obs_ref, *refs):
    *blocks, root_ref, ahead_ref = refs
    if len(blocks) == 2:
        blocks = [ref.at[k] for ref in blocks for k in range(groups)]
    states, outs = blocks[:groups], blocks[groups:]
    columns, local, entries = states[0].shape
    members = groups * local
    spread = members - 1.0
    every = range(columns)
    rows = lax.broadcasted_iota(jnp.int32, (members, members), 0)
    cols = lax.broadcasted_iota(jnp.int32, (members, members), 1)
    means, forces, scales, grams = [], [], [], []
    for c in every:
        x = jnp.concatenate([ref[c] for ref in states], axis=0)
        mean = jnp.sum(x, axis=0, keepdims=True) * (1.0 / members)
        anomaly = x - mean
        total = obs_ref[first + c, 0:1]
        forces.append(obs_ref[first + c, 1:2] - total * mean)
        means.append(mean)
        ahead_ref[c] = anomaly
        grams.append(square_by_rows(split(anomaly * jnp.sqrt(total), 3)))
    for c in every:
        gram = grams[c] + jnp.where(rows == cols, spread, 0.0)
        norm = jnp.sum(jnp.sum(gram * gram, axis=0, keepdims=True), axis=1, keepdims=True)
        scales.append(jnp.sqrt(norm))
        root_ref[c] = gram * (1.0 / scales[c])

    def factors():
        s = [split(root_ref[c], 2) for c in every]
        p = [dot3(s[c], s[c]) for c in every]
        cubic = [dot3(split(0.0625 * p[c] - 0.5625 * root_ref[c], 2), split(p[c], 2)) for c in every]
        return s, [split(1.6875 * p[c] - 2.4375 * root_ref[c] + cubic[c], 2) for c in every]

    def pair(step, carry):
        s, r = factors()
        t = [2.25 * root_ref[c] + dot3(r[c], s[c]) for c in every]
        for c in every:
            ahead_ref[c] = 2.25 * ahead_ref[c] + dot3(r[c], split(ahead_ref[c], 2))
        for c in every:
            root_ref[c] = 2.25 * t[c] + dot3(split(t[c], 2), r[c])
        return carry

    lax.fori_loop(0, PAIRS - 1, pair, 0)
    _, r = factors()
    ahead = [2.25 * ahead_ref[c] + dot3(r[c], split(ahead_ref[c], 2)) for c in every]
    for c in every:
        w = ahead[c]
        inner = jnp.sum(w * forces[c], axis=1, keepdims=True)
        shift = jnp.sum(w * inner, axis=0, keepdims=True) / scales[c]
        result = means[c] + shift + w * jnp.sqrt(spread / scales[c])
        for k in range(groups):
            outs[k][c] = result[k * local : (k + 1) * local]


def analyse(states, obs, first):
    groups = len(states) if isinstance(states, list) else states.shape[0]
    columns, local, entries = states[0].shape
    members = groups * local
    block = jax.ShapeDtypeStruct((columns, local, entries), jnp.float32)

    def kernel(*refs):
        analyse_kernel(first, groups, *refs)

    several = isinstance(states, list)
    return call(
        kernel,
        [block] * groups if several else jax.ShapeDtypeStruct(states.shape, jnp.float32),
        columns * 90 * 2 * members * members * entries,
        8 * columns * members * entries,
        scratch_shapes=[
            pltpu.VMEM((columns, members, members), jnp.float32),
            pltpu.VMEM((columns, members, entries), jnp.float32),
        ],
    )(obs, *(states if several else [states]))


def body(background, diffusion, advection, obs_where, obs_count, obs_value, obs_rinv):
    local, columns, entries = background.shape
    groups = lax.axis_size("mem")
    tiles = lax.axis_size("tile")
    half = columns // groups // 2
    size = background.size
    block = (half, local, entries)
    edge = jax.ShapeDtypeStruct((2, local, entries), jnp.float32)
    me = lax.axis_index("mem")[None].astype(jnp.int32)
    pieces = len(pieces_of(local))

    inner, low, high = call(
        inner_kernel,
        [jax.ShapeDtypeStruct((groups, *block), jnp.float32), edge, edge],
        20 * size,
        8 * size,
        vmem=60 * MIB,
        in_specs=[HBM, HBM, HBM],
        out_specs=[HBM, HBM, HBM],
        scratch_shapes=[
            pltpu.VMEM(background.shape, jnp.float32),
            pltpu.VMEM((8, entries), jnp.float32),
            pltpu.VMEM((2, 2, local, entries), jnp.float32),
            pltpu.VMEM((groups, *block), jnp.float32),
            pltpu.SemaphoreType.DMA((2 * pieces + 4,)),
        ],
    )(background, diffusion, advection)
    inner = lax.all_to_all(inner, "mem", split_axis=0, concat_axis=0, tiled=True)
    before = lax.ppermute(high, "tile", [(i, (i + 1) % tiles) for i in range(tiles)])
    after = lax.ppermute(low, "tile", [((i + 1) % tiles, i) for i in range(tiles)])
    outer = call(
        outer_kernel,
        [jax.ShapeDtypeStruct(block, jnp.float32)] * groups,
        20 * size,
        8 * size,
        in_specs=[SMEM] + [VMEM] * 5,
        scratch_shapes=[pltpu.VMEM((columns + 4, local, entries), jnp.float32)],
    )(me, background, before, after, diffusion[None], advection[None])
    outer = exchange(outer, False)
    obs = call(
        observe_kernel,
        jax.ShapeDtypeStruct((2 * half, 8, entries), jnp.float32),
        2 * half * 2 * 16 * obs_where.shape[2] * entries,
        12 * obs_where.size,
        in_specs=[SMEM, SMEM] + [VMEM] * 3,
    )(me, obs_count, obs_where[0], obs_value[0], obs_rinv[0])

    inner = analyse(inner, obs, 0)
    inner = lax.all_to_all(inner, "mem", split_axis=0, concat_axis=0, tiled=True)
    outer = exchange(analyse(outer, obs, half), True)
    return call(
        join_kernel,
        jax.ShapeDtypeStruct(background.shape, jnp.float32),
        size,
        8 * size,
        in_specs=[SMEM] + [VMEM] * (groups + 1),
        out_specs=HBM,
        scratch_shapes=[
            pltpu.VMEM((columns, local, entries), jnp.float32),
            pltpu.VMEM(background.shape, jnp.float32),
            pltpu.SemaphoreType.DMA((pieces,)),
        ],
    )(me, inner, *outer)


def solution(mesh):
    return jax.shard_map(
        body,
        mesh=mesh,
        in_specs=(
            P("mem", "tile", None),
            P(),
            P(),
            P("tile", None, None),
            P("tile", None),
            P("tile", None, None),
            P("tile", None, None),
        ),
        out_specs=P("mem", "tile", None),
        check_vma=False,
    )
```

```python
import jax
import jax.numpy as jnp
from jax import lax
from jax.experimental import pallas as pl
from jax.experimental.pallas import tpu as pltpu
from jax.sharding import PartitionSpec as P

PAIRS = 6
MIB = 1024 * 1024
SMEM = pl.BlockSpec(memory_space=pltpu.SMEM)
VMEM = pl.BlockSpec(memory_space=pltpu.VMEM)
HBM = pl.BlockSpec(memory_space=pltpu.HBM)


def call(kernel, out_shape, flops, moved, vmem=48 * MIB, **options):
    return pl.pallas_call(
        kernel,
        out_shape=out_shape,
        compiler_params=pltpu.CompilerParams(vmem_limit_bytes=vmem),
        cost_estimate=pl.CostEstimate(flops=flops, bytes_accessed=moved, transcendentals=0),
        **options,
    )


def target(me, k, groups):
    if groups & (groups - 1) == 0:
        return me ^ k
    return lax.rem(me + k, groups)


def source(me, k, groups):
    if groups & (groups - 1) == 0:
        return me ^ k
    return lax.rem(me + groups - k, groups)


def exchange(blocks):
    groups = len(blocks)
    out = [blocks[0]]
    for k in range(1, groups):
        pairs = [(i, i ^ k if groups & (groups - 1) == 0 else (i + k) % groups) for i in range(groups)]
        out.append(lax.ppermute(blocks[k], "mem", pairs))
    return out


def split(x, parts):
    out = []
    for _ in range(parts):
        part = x.astype(jnp.bfloat16)
        out.append(part)
        x = x - part.astype(jnp.float32)
    return out


def dot(a, b):
    return jnp.dot(a, b, precision=lax.Precision.HIGH, preferred_element_type=jnp.float32)


def square_by_rows(parts):
    p0, p1, p2 = parts
    lhs = jnp.concatenate([p2, p0, p1, p1, p0, p0], axis=1)
    rhs = jnp.concatenate([p0, p2, p1, p0, p1, p0], axis=1)
    return lax.dot_general(lhs, rhs, (((1,), (1,)), ((), ())), preferred_element_type=jnp.float32)


def stencil(padded, diffusion, advection):
    middle = padded[1:-1]
    left = padded[:-2]
    right = padded[2:]
    return middle + diffusion * (left - 2.0 * middle + right) + advection * (0.5 * (left - right))


def inner_start(place, quarter):
    return place + quarter


def outer_start(place, quarter):
    return jnp.where(place < quarter, place, place + 2 * quarter)


def pieces_of(members):
    rows = 8 if members % 8 == 0 else members
    return [pl.ds(first, rows) for first in range(0, members, rows)]


def inner_kernel(state_ref, diff_ref, adv_ref, out_ref, low_ref, high_ref, held_ref, num_ref, edge_ref, made_ref, sems):
    members, columns, entries = state_ref.shape
    groups, half, _, _ = out_ref.shape
    quarter = columns // 4
    pieces = pieces_of(members)
    count = len(pieces)
    reads = [pltpu.make_async_copy(state_ref.at[part], held_ref.at[part], sems.at[i]) for i, part in enumerate(pieces)]
    reads.append(pltpu.make_async_copy(diff_ref, num_ref.at[0], sems.at[count]))
    reads.append(pltpu.make_async_copy(adv_ref, num_ref.at[1], sems.at[count + 1]))
    for copy in reads[count:] + reads[:count]:
        copy.start()
    reads[count].wait()
    reads[count + 1].wait()
    diffusion = num_ref[0:1][None]
    advection = num_ref[1:2][None]
    writes = []
    for i, part in enumerate(pieces):
        reads[i].wait()
        x = jnp.swapaxes(held_ref[part], 0, 1)
        edge_ref[0, :, part] = x[:2]
        edge_ref[1, :, part] = x[columns - 2 :]
        x = x[quarter - 2 : columns - quarter + 2]
        x = stencil(stencil(x, diffusion, advection), diffusion, advection)
        made_ref[:, :, part] = x.reshape(groups, half, part.size, entries)
        copy = pltpu.make_async_copy(made_ref.at[:, :, part], out_ref.at[:, :, part], sems.at[count + 2 + i])
        copy.start()
        writes.append(copy)
    for i, ref in enumerate((low_ref, high_ref)):
        copy = pltpu.make_async_copy(edge_ref.at[i], ref, sems.at[2 * count + 2 + i])
        copy.start()
        writes.append(copy)
    for copy in writes:
        copy.wait()


def outer_kernel(obs_ref, state_ref, before_ref, after_ref, diff_ref, adv_ref, out_ref, turned_ref):
    del obs_ref
    columns = state_ref.shape[1]
    quarter = columns // 4
    turned_ref[2 : columns + 2] = jnp.swapaxes(state_ref[...], 0, 1)
    turned_ref[:2] = before_ref[...]
    turned_ref[columns + 2 :] = after_ref[...]
    diffusion = diff_ref[...][None]
    advection = adv_ref[...][None]
    low = turned_ref[: quarter + 4]
    high = turned_ref[columns - quarter :]
    low = stencil(stencil(low, diffusion, advection), diffusion, advection)
    high = stencil(stencil(high, diffusion, advection), diffusion, advection)
    out_ref[...] = jnp.concatenate([low, high], axis=0).reshape(out_ref.shape)


def join_kernel(me_ref, inner_ref, *refs):
    *outer, out_ref, turned_ref, made_ref, sems = refs
    members, columns, entries = out_ref.shape
    groups, half, _, _ = inner_ref.shape
    quarter = columns // 4
    writes = []
    for i, part in enumerate(pieces_of(members)):
        for k in range(groups):
            place = source(me_ref[0], k, groups) * half
            turned_ref[pl.ds(outer_start(place, quarter), half), part] = outer[k][:, part]
        turned_ref[quarter : columns - quarter, part] = inner_ref[:, :, part].reshape(groups * half, part.size, entries)
        made_ref[part] = jnp.swapaxes(turned_ref[:, part], 0, 1)
        copy = pltpu.make_async_copy(made_ref.at[part], out_ref.at[part], sems.at[i])
        copy.start()
        writes.append(copy)
    for copy in writes:
        copy.wait()


def observe_kernel(me_ref, count_ref, where_ref, value_ref, rinv_ref, out_ref):
    columns, _, entries = out_ref.shape
    half = columns // 2
    quarter = where_ref.shape[0] // 4
    slots = where_ref.shape[1]
    place = me_ref[0] * half
    slot = lax.broadcasted_iota(jnp.int32, (1, slots), 1)
    row = lax.broadcasted_iota(jnp.int32, (16, slots), 0)
    entry = lax.broadcasted_iota(jnp.int32, (entries, slots), 0)
    for c in range(columns):
        at = inner_start(place, quarter) + c if c < half else outer_start(place, quarter) + c - half
        weight = jnp.where(slot < count_ref[0, at], rinv_ref[pl.ds(at, 1), :], 0.0)
        lhs = jnp.zeros((16, slots), jnp.float32)
        for first, source in ((0, weight), (3, weight * value_ref[pl.ds(at, 1), :])):
            for k, part in enumerate(split(source, 3)):
                lhs = jnp.where(row == first + k, part.astype(jnp.float32), lhs)
        onehot = (entry == where_ref[pl.ds(at, 1), :]).astype(jnp.float32).astype(jnp.bfloat16)
        sums = lax.dot_general(
            lhs.astype(jnp.bfloat16), onehot, (((1,), (1,)), ((), ())), preferred_element_type=jnp.float32
        )
        out_ref[c, 0:1] = sums[0:1] + (sums[1:2] + sums[2:3])
        out_ref[c, 1:2] = sums[3:4] + (sums[4:5] + sums[5:6])


def analyse_kernel(first, me_ref, after_ref, obs_ref, states_ref, *refs):
    del after_ref
    *outs, done_ref, root_ref, ahead_ref = refs
    done_ref[...] = jnp.zeros_like(done_ref)
    groups = states_ref.shape[0]
    if len(outs) == 1:
        states = [states_ref.at[k] for k in range(groups)]
        outs = [outs[0].at[k] for k in range(groups)]
    else:
        states = [states_ref.at[target(me_ref[0], k, groups)] for k in range(groups)]
    columns, local, entries = states[0].shape
    members = groups * local
    spread = members - 1.0
    every = range(columns)
    rows = lax.broadcasted_iota(jnp.int32, (members, members), 0)
    cols = lax.broadcasted_iota(jnp.int32, (members, members), 1)
    means, forces, scales, grams = [], [], [], []
    for c in every:
        x = jnp.concatenate([ref[c] for ref in states], axis=0)
        mean = jnp.sum(x, axis=0, keepdims=True) * (1.0 / members)
        anomaly = x - mean
        total = obs_ref[first + c, 0:1]
        forces.append(obs_ref[first + c, 1:2] - total * mean)
        means.append(mean)
        ahead_ref[c] = anomaly
        grams.append(square_by_rows(split(anomaly * jnp.sqrt(total), 3)))
    for c in every:
        gram = grams[c] + jnp.where(rows == cols, spread, 0.0)
        norm = jnp.sum(jnp.sum(gram * gram, axis=0, keepdims=True), axis=1, keepdims=True)
        scales.append(jnp.sqrt(norm))
        root_ref[c] = gram * (1.0 / scales[c])

    def factors():
        p = [dot(root_ref[c], root_ref[c]) for c in every]
        cubic = [dot(0.0625 * p[c] - 0.5625 * root_ref[c], p[c]) for c in every]
        return [1.6875 * p[c] - 2.4375 * root_ref[c] + cubic[c] for c in every]

    def pair(step, carry):
        r = factors()
        t = [2.25 * root_ref[c] + dot(r[c], root_ref[c]) for c in every]
        for c in every:
            ahead_ref[c] = 2.25 * ahead_ref[c] + dot(r[c], ahead_ref[c])
        for c in every:
            root_ref[c] = 2.25 * t[c] + dot(t[c], r[c])
        return carry

    lax.fori_loop(0, PAIRS - 1, pair, 0)
    r = factors()
    ahead = [2.25 * ahead_ref[c] + dot(r[c], ahead_ref[c]) for c in every]
    for c in every:
        w = ahead[c]
        inner = jnp.sum(w * forces[c], axis=1, keepdims=True)
        shift = jnp.sum(w * inner, axis=0, keepdims=True) / scales[c]
        result = means[c] + shift + w * jnp.sqrt(spread / scales[c])
        for k in range(groups):
            outs[k][c] = result[k * local : (k + 1) * local]


def analyse(states, obs, first, me, after, apart):
    groups, columns, local, entries = states.shape
    members = groups * local
    whole = jax.ShapeDtypeStruct(states.shape, jnp.float32)
    token = jax.ShapeDtypeStruct(after.shape, jnp.float32)

    def kernel(*refs):
        analyse_kernel(first, *refs)

    return call(
        kernel,
        ([jax.ShapeDtypeStruct(states.shape[1:], jnp.float32)] * groups if apart else [whole]) + [token],
        columns * 90 * 2 * members * members * entries,
        8 * columns * members * entries,
        in_specs=[SMEM, VMEM, VMEM, VMEM],
        scratch_shapes=[
            pltpu.VMEM((columns, members, members), jnp.float32),
            pltpu.VMEM((columns, members, entries), jnp.float32),
        ],
    )(me, after, obs, states)


def body(background, diffusion, advection, obs_where, obs_count, obs_value, obs_rinv):
    local, columns, entries = background.shape
    groups = lax.axis_size("mem")
    tiles = lax.axis_size("tile")
    half = columns // groups // 2
    size = background.size
    block = (half, local, entries)
    edge = jax.ShapeDtypeStruct((2, local, entries), jnp.float32)
    me = lax.axis_index("mem")[None].astype(jnp.int32)
    pieces = len(pieces_of(local))

    inner, low, high = call(
        inner_kernel,
        [jax.ShapeDtypeStruct((groups, *block), jnp.float32), edge, edge],
        20 * size,
        8 * size,
        vmem=60 * MIB,
        in_specs=[HBM, HBM, HBM],
        out_specs=[HBM, HBM, HBM],
        scratch_shapes=[
            pltpu.VMEM(background.shape, jnp.float32),
            pltpu.VMEM((8, entries), jnp.float32),
            pltpu.VMEM((2, 2, local, entries), jnp.float32),
            pltpu.VMEM((groups, *block), jnp.float32),
            pltpu.SemaphoreType.DMA((2 * pieces + 4,)),
        ],
    )(background, diffusion, advection)
    inner = lax.all_to_all(inner, "mem", split_axis=0, concat_axis=0, tiled=True)
    before = lax.ppermute(high, "tile", [(i, (i + 1) % tiles) for i in range(tiles)])
    after = lax.ppermute(low, "tile", [((i + 1) % tiles, i) for i in range(tiles)])
    obs = call(
        observe_kernel,
        jax.ShapeDtypeStruct((2 * half, 8, entries), jnp.float32),
        2 * half * 2 * 16 * obs_where.shape[2] * entries,
        12 * obs_where.size,
        in_specs=[SMEM, SMEM] + [VMEM] * 3,
    )(me, obs_count, obs_where[0], obs_value[0], obs_rinv[0])
    outer = call(
        outer_kernel,
        jax.ShapeDtypeStruct((groups, *block), jnp.float32),
        20 * size,
        8 * size,
        in_specs=[VMEM] * 6,
        scratch_shapes=[pltpu.VMEM((columns + 4, local, entries), jnp.float32)],
    )(obs, background, before, after, diffusion[None], advection[None])
    outer = lax.all_to_all(outer, "mem", split_axis=0, concat_axis=0, tiled=True)

    inner, done = analyse(inner, obs, 0, me, obs[0], False)
    inner = lax.all_to_all(inner, "mem", split_axis=0, concat_axis=0, tiled=True)
    *outer, _ = analyse(outer, obs, half, me, done, True)
    outer = exchange(outer)
    return call(
        join_kernel,
        jax.ShapeDtypeStruct(background.shape, jnp.float32),
        size,
        8 * size,
        in_specs=[SMEM] + [VMEM] * (groups + 1),
        out_specs=HBM,
        scratch_shapes=[
            pltpu.VMEM((columns, local, entries), jnp.float32),
            pltpu.VMEM(background.shape, jnp.float32),
            pltpu.SemaphoreType.DMA((pieces,)),
        ],
    )(me, inner, *outer)


def solution(mesh):
    return jax.shard_map(
        body,
        mesh=mesh,
        in_specs=(
            P("mem", "tile", None),
            P(),
            P(),
            P("tile", None, None),
            P("tile", None),
            P("tile", None, None),
            P("tile", None, None),
        ),
        out_specs=P("mem", "tile", None),
        check_vma=False,
    )
```

```python
import jax
import jax.numpy as jnp
from jax import lax
from jax.experimental import pallas as pl
from jax.experimental.pallas import tpu as pltpu
from jax.sharding import PartitionSpec as P

PAIRS = 6
MIB = 1024 * 1024
SMEM = pl.BlockSpec(memory_space=pltpu.SMEM)
VMEM = pl.BlockSpec(memory_space=pltpu.VMEM)
HBM = pl.BlockSpec(memory_space=pltpu.HBM)


def call(kernel, out_shape, flops, moved, vmem=48 * MIB, **options):
    return pl.pallas_call(
        kernel,
        out_shape=out_shape,
        compiler_params=pltpu.CompilerParams(vmem_limit_bytes=vmem),
        cost_estimate=pl.CostEstimate(flops=flops, bytes_accessed=moved, transcendentals=0),
        **options,
    )


def target(me, k, groups):
    if groups & (groups - 1) == 0:
        return me ^ k
    return lax.rem(me + k, groups)


def source(me, k, groups):
    if groups & (groups - 1) == 0:
        return me ^ k
    return lax.rem(me + groups - k, groups)


def exchange(blocks):
    groups = len(blocks)
    out = list(blocks)
    for k in sorted(range(1, groups), key=lambda k: (-(k // 2).bit_count(), k == 1, k)):
        pairs = [(i, i ^ k if groups & (groups - 1) == 0 else (i + k) % groups) for i in range(groups)]
        out[k] = lax.ppermute(blocks[k], "mem", pairs)
    return out


def split(x, parts):
    out = []
    for _ in range(parts):
        part = x.astype(jnp.bfloat16)
        out.append(part)
        x = x - part.astype(jnp.float32)
    return out


def dot3(a, b):
    lhs = jnp.concatenate([a[0], a[1], a[0]], axis=1)
    rhs = jnp.concatenate([b[0], b[0], b[1]], axis=0)
    middle = lhs.shape[0] // 2
    upper = jnp.dot(lhs[:middle], rhs, preferred_element_type=jnp.float32)
    lower = jnp.dot(lhs[middle:], rhs, preferred_element_type=jnp.float32)
    return jnp.concatenate([upper, lower], axis=0)


def square_by_rows(parts):
    p0, p1, p2 = parts
    lhs = jnp.concatenate([p2, p0, p1, p1, p0, p0], axis=1)
    rhs = jnp.concatenate([p0, p2, p1, p0, p1, p0], axis=1)
    return lax.dot_general(lhs, rhs, (((1,), (1,)), ((), ())), preferred_element_type=jnp.float32)


def stencil(padded, diffusion, advection):
    middle = padded[1:-1]
    left = padded[:-2]
    right = padded[2:]
    return middle + diffusion * (left - 2.0 * middle + right) + advection * (0.5 * (left - right))


def inner_start(place, quarter):
    return place + quarter


def outer_start(place, quarter):
    return jnp.where(place < quarter, place, place + 2 * quarter)


def pieces_of(members):
    rows = 8 if members % 8 == 0 else members
    return [pl.ds(first, rows) for first in range(0, members, rows)]


def inner_kernel(me_ref, state_ref, diff_ref, adv_ref, *refs):
    *outs, low_ref, high_ref, held_ref, num_ref, edge_ref, made_ref, sems = refs
    members, columns, _ = state_ref.shape
    groups = len(outs)
    half = outs[0].shape[0]
    quarter = columns // 4
    pieces = pieces_of(members)
    count = len(pieces)
    reads = [pltpu.make_async_copy(state_ref.at[part], held_ref.at[part], sems.at[i]) for i, part in enumerate(pieces)]
    reads.append(pltpu.make_async_copy(diff_ref, num_ref.at[0], sems.at[count]))
    reads.append(pltpu.make_async_copy(adv_ref, num_ref.at[1], sems.at[count + 1]))
    for copy in reads[count:] + reads[:count]:
        copy.start()
    reads[count].wait()
    reads[count + 1].wait()
    diffusion = num_ref[0:1][None]
    advection = num_ref[1:2][None]
    for i, part in enumerate(pieces):
        reads[i].wait()
        x = jnp.swapaxes(held_ref[part], 0, 1)
        edge_ref[0, :, part] = x[:2]
        edge_ref[1, :, part] = x[columns - 2 :]
        x = x[quarter - 2 : columns - quarter + 2]
        made_ref[:, part] = stencil(stencil(x, diffusion, advection), diffusion, advection)
    writes = []
    for k in range(groups):
        block = made_ref.at[pl.ds(target(me_ref[0], k, groups) * half, half)]
        writes.append(pltpu.make_async_copy(block, outs[k], sems.at[count + 2 + k]))
    for i, ref in enumerate((low_ref, high_ref)):
        writes.append(pltpu.make_async_copy(edge_ref.at[i], ref, sems.at[count + 2 + groups + i]))
    for copy in writes:
        copy.start()
    for copy in writes:
        copy.wait()


def outer_kernel(obs_ref, state_ref, before_ref, after_ref, diff_ref, adv_ref, out_ref, turned_ref):
    del obs_ref
    columns = state_ref.shape[1]
    quarter = columns // 4
    turned_ref[2 : columns + 2] = jnp.swapaxes(state_ref[...], 0, 1)
    turned_ref[:2] = before_ref[...]
    turned_ref[columns + 2 :] = after_ref[...]
    diffusion = diff_ref[...][None]
    advection = adv_ref[...][None]
    low = turned_ref[: quarter + 4]
    high = turned_ref[columns - quarter :]
    low = stencil(stencil(low, diffusion, advection), diffusion, advection)
    high = stencil(stencil(high, diffusion, advection), diffusion, advection)
    out_ref[...] = jnp.concatenate([low, high], axis=0).reshape(out_ref.shape)


def join_kernel(me_ref, inner_ref, *refs):
    *outer, out_ref, turned_ref, made_ref, sems = refs
    members, columns, entries = out_ref.shape
    groups, half, _, _ = inner_ref.shape
    quarter = columns // 4
    writes = []
    for i, part in enumerate(pieces_of(members)):
        for k in range(groups):
            place = source(me_ref[0], k, groups) * half
            turned_ref[pl.ds(outer_start(place, quarter), half), part] = outer[k][:, part]
        turned_ref[quarter : columns - quarter, part] = inner_ref[:, :, part].reshape(groups * half, part.size, entries)
        made_ref[part] = jnp.swapaxes(turned_ref[:, part], 0, 1)
        copy = pltpu.make_async_copy(made_ref.at[part], out_ref.at[part], sems.at[i])
        copy.start()
        writes.append(copy)
    for copy in writes:
        copy.wait()


def observe_kernel(me_ref, count_ref, where_ref, value_ref, rinv_ref, out_ref):
    columns, _, entries = out_ref.shape
    half = columns // 2
    quarter = where_ref.shape[0] // 4
    slots = where_ref.shape[1]
    place = me_ref[0] * half
    slot = lax.broadcasted_iota(jnp.int32, (1, slots), 1)
    row = lax.broadcasted_iota(jnp.int32, (16, slots), 0)
    entry = lax.broadcasted_iota(jnp.int32, (entries, slots), 0)
    for c in range(columns):
        at = inner_start(place, quarter) + c if c < half else outer_start(place, quarter) + c - half
        weight = jnp.where(slot < count_ref[0, at], rinv_ref[pl.ds(at, 1), :], 0.0)
        lhs = jnp.zeros((16, slots), jnp.float32)
        for first, source in ((0, weight), (3, weight * value_ref[pl.ds(at, 1), :])):
            for k, part in enumerate(split(source, 3)):
                lhs = jnp.where(row == first + k, part.astype(jnp.float32), lhs)
        onehot = (entry == where_ref[pl.ds(at, 1), :]).astype(jnp.float32).astype(jnp.bfloat16)
        sums = lax.dot_general(
            lhs.astype(jnp.bfloat16), onehot, (((1,), (1,)), ((), ())), preferred_element_type=jnp.float32
        )
        out_ref[c, 0:1] = sums[0:1] + (sums[1:2] + sums[2:3])
        out_ref[c, 1:2] = sums[3:4] + (sums[4:5] + sums[5:6])


def analyse_kernel(first, me_ref, after_ref, obs_ref, states, outs, done_ref):
    del after_ref
    done_ref[...] = jnp.zeros_like(done_ref)
    groups = len(outs)
    columns, local, entries = outs[0].shape
    members = groups * local
    spread = members - 1.0
    every = range(columns)
    rows = lax.broadcasted_iota(jnp.int32, (members, members), 0)
    cols = lax.broadcasted_iota(jnp.int32, (members, members), 1)
    means, forces, scales, grams, ahead, root = [], [], [], [], [], []
    for c in every:
        x = jnp.concatenate([ref[c] for ref in states], axis=0)
        mean = jnp.sum(x, axis=0, keepdims=True) * (1.0 / members)
        anomaly = x - mean
        total = obs_ref[first + c, 0:1]
        forces.append(obs_ref[first + c, 1:2] - total * mean)
        means.append(mean)
        ahead.append(anomaly)
        grams.append(square_by_rows(split(anomaly * jnp.sqrt(total), 3)))
    for c in every:
        gram = grams[c] + jnp.where(rows == cols, spread, 0.0)
        norm = jnp.sum(jnp.sum(gram * gram, axis=0, keepdims=True), axis=1, keepdims=True)
        scales.append(jnp.sqrt(norm))
        root.append(gram * (1.0 / scales[c]))

    r = None
    for step in range(PAIRS):
        s = [split(root[c], 2) for c in every]
        p = [dot3(s[c], s[c]) for c in every]
        if r is not None:
            ahead = [2.25 * ahead[c] + dot3(r[c], split(ahead[c], 2)) for c in every]
        cubic = [dot3(split(0.0625 * p[c] - 0.5625 * root[c], 2), split(p[c], 2)) for c in every]
        r = [split(1.6875 * p[c] - 2.4375 * root[c] + cubic[c], 2) for c in every]
        if step < PAIRS - 1:
            t = [2.25 * root[c] + dot3(r[c], s[c]) for c in every]
            root = [2.25 * t[c] + dot3(split(t[c], 2), r[c]) for c in every]
    ahead = [2.25 * ahead[c] + dot3(r[c], split(ahead[c], 2)) for c in every]
    for c in every:
        w = ahead[c]
        inner = jnp.sum(w * forces[c], axis=1, keepdims=True)
        shift = jnp.sum(w * inner, axis=0, keepdims=True) / scales[c]
        result = means[c] + shift + w * jnp.sqrt(spread / scales[c])
        for k in range(groups):
            outs[k][c] = result[k * local : (k + 1) * local]


def analyse(states, obs, first, me, after, apart):
    groups = len(states)
    columns, local, entries = states[0].shape
    members = groups * local
    block = jax.ShapeDtypeStruct((columns, local, entries), jnp.float32)
    whole = jax.ShapeDtypeStruct((groups, columns, local, entries), jnp.float32)
    token = jax.ShapeDtypeStruct(after.shape, jnp.float32)

    def kernel(me_ref, after_ref, obs_ref, *refs):
        if apart:
            states_ref, *outs, done_ref = refs
            ins = [states_ref.at[target(me_ref[0], k, groups)] for k in range(groups)]
        else:
            *ins, out_ref, done_ref = refs
            outs = [out_ref.at[source(me_ref[0], k, groups)] for k in range(groups)]
        analyse_kernel(first, me_ref, after_ref, obs_ref, ins, outs, done_ref)

    operands = [states] if apart else states
    return call(
        kernel,
        [block] * groups + [token] if apart else [whole, token],
        columns * 90 * 2 * members * members * entries,
        8 * columns * members * entries,
        in_specs=[SMEM] + [VMEM] * (len(operands) + 2),
    )(me, after, obs, *operands)


def body(background, diffusion, advection, obs_where, obs_count, obs_value, obs_rinv):
    local, columns, entries = background.shape
    groups = lax.axis_size("mem")
    tiles = lax.axis_size("tile")
    half = columns // groups // 2
    size = background.size
    block = (half, local, entries)
    edge = jax.ShapeDtypeStruct((2, local, entries), jnp.float32)
    me = lax.axis_index("mem")[None].astype(jnp.int32)
    pieces = len(pieces_of(local))

    *inner, low, high = call(
        inner_kernel,
        [jax.ShapeDtypeStruct(block, jnp.float32)] * groups + [edge, edge],
        20 * size,
        8 * size,
        vmem=60 * MIB,
        in_specs=[SMEM, HBM, HBM, HBM],
        out_specs=[HBM] * (groups + 2),
        scratch_shapes=[
            pltpu.VMEM(background.shape, jnp.float32),
            pltpu.VMEM((8, entries), jnp.float32),
            pltpu.VMEM((2, 2, local, entries), jnp.float32),
            pltpu.VMEM((groups * half, local, entries), jnp.float32),
            pltpu.SemaphoreType.DMA((pieces + groups + 4,)),
        ],
    )(me, background, diffusion, advection)
    inner = exchange(inner)
    before = lax.ppermute(high, "tile", [(i, (i + 1) % tiles) for i in range(tiles)])
    after = lax.ppermute(low, "tile", [((i + 1) % tiles, i) for i in range(tiles)])
    obs = call(
        observe_kernel,
        jax.ShapeDtypeStruct((2 * half, 8, entries), jnp.float32),
        2 * half * 2 * 16 * obs_where.shape[2] * entries,
        12 * obs_where.size,
        in_specs=[SMEM, SMEM] + [VMEM] * 3,
    )(me, obs_count, obs_where[0], obs_value[0], obs_rinv[0])
    outer = call(
        outer_kernel,
        jax.ShapeDtypeStruct((groups, *block), jnp.float32),
        20 * size,
        8 * size,
        in_specs=[VMEM] * 6,
        scratch_shapes=[pltpu.VMEM((columns + 4, local, entries), jnp.float32)],
    )(obs, background, before, after, diffusion[None], advection[None])
    outer = lax.all_to_all(outer, "mem", split_axis=0, concat_axis=0, tiled=True)

    inner, done = analyse(inner, obs, 0, me, obs[0], False)
    inner = lax.all_to_all(inner, "mem", split_axis=0, concat_axis=0, tiled=True)
    *outer, _ = analyse(outer, obs, half, me, done, True)
    outer = exchange(outer)
    return call(
        join_kernel,
        jax.ShapeDtypeStruct(background.shape, jnp.float32),
        size,
        8 * size,
        in_specs=[SMEM] + [VMEM] * (groups + 1),
        out_specs=HBM,
        scratch_shapes=[
            pltpu.VMEM((columns, local, entries), jnp.float32),
            pltpu.VMEM(background.shape, jnp.float32),
            pltpu.SemaphoreType.DMA((pieces,)),
        ],
    )(me, inner, *outer)


def solution(mesh):
    return jax.shard_map(
        body,
        mesh=mesh,
        in_specs=(
            P("mem", "tile", None),
            P(),
            P(),
            P("tile", None, None),
            P("tile", None),
            P("tile", None, None),
            P("tile", None, None),
        ),
        out_specs=P("mem", "tile", None),
        check_vma=False,
    )
```

```python
import jax
import jax.numpy as jnp
from jax import lax
from jax.experimental import pallas as pl
from jax.experimental.pallas import tpu as pltpu
from jax.sharding import PartitionSpec as P

PAIRS = 6
MIB = 1024 * 1024
SMEM = pl.BlockSpec(memory_space=pltpu.SMEM)
VMEM = pl.BlockSpec(memory_space=pltpu.VMEM)
HBM = pl.BlockSpec(memory_space=pltpu.HBM)


def call(kernel, out_shape, flops, moved, vmem=48 * MIB, **options):
    return pl.pallas_call(
        kernel,
        out_shape=out_shape,
        compiler_params=pltpu.CompilerParams(vmem_limit_bytes=vmem),
        cost_estimate=pl.CostEstimate(flops=flops, bytes_accessed=moved, transcendentals=0),
        **options,
    )


def target(me, k, groups):
    if groups & (groups - 1) == 0:
        return me ^ k
    return lax.rem(me + k, groups)


def source(me, k, groups):
    if groups & (groups - 1) == 0:
        return me ^ k
    return lax.rem(me + groups - k, groups)


def issue_order(groups):
    return sorted(range(1, groups), key=lambda k: (-(k // 2).bit_count(), k == 1, k)) + [0]


def exchange(blocks):
    groups = len(blocks)
    out = []
    for k in issue_order(groups):
        pairs = [(i, i ^ k if groups & (groups - 1) == 0 else (i + k) % groups) for i in range(groups)]
        out.append(lax.ppermute(blocks[k], "mem", pairs) if k else blocks[0])
    return out


def split(x, parts):
    out = []
    for _ in range(parts):
        part = x.astype(jnp.bfloat16)
        out.append(part)
        x = x - part.astype(jnp.float32)
    return out


def dot3(a, b):
    lhs = jnp.concatenate([a[0], a[1], a[0]], axis=1)
    rhs = jnp.concatenate([b[0], b[0], b[1]], axis=0)
    return jnp.dot(lhs, rhs, preferred_element_type=jnp.float32)


def square_by_rows(parts):
    p0, p1, p2 = parts
    lhs = jnp.concatenate([p2, p0, p1, p1, p0, p0], axis=1)
    rhs = jnp.concatenate([p0, p2, p1, p0, p1, p0], axis=1)
    return lax.dot_general(lhs, rhs, (((1,), (1,)), ((), ())), preferred_element_type=jnp.float32)


def stencil(padded, diffusion, advection):
    middle = padded[1:-1]
    left = padded[:-2]
    right = padded[2:]
    return middle + diffusion * (left - 2.0 * middle + right) + advection * (0.5 * (left - right))


def inner_start(place, quarter):
    return place + quarter


def outer_start(place, quarter):
    return jnp.where(place < quarter, place, place + 2 * quarter)


def pieces_of(members):
    rows = 8 if members % 8 == 0 else members
    return [pl.ds(first, rows) for first in range(0, members, rows)]


def inner_kernel(state_ref, diff_ref, adv_ref, out_ref, low_ref, high_ref, held_ref, num_ref, edge_ref, made_ref, sems):
    members, columns, entries = state_ref.shape
    groups, half, _, _ = out_ref.shape
    quarter = columns // 4
    pieces = pieces_of(members)
    count = len(pieces)
    reads = [pltpu.make_async_copy(state_ref.at[part], held_ref.at[part], sems.at[i]) for i, part in enumerate(pieces)]
    reads.append(pltpu.make_async_copy(diff_ref, num_ref.at[0], sems.at[count]))
    reads.append(pltpu.make_async_copy(adv_ref, num_ref.at[1], sems.at[count + 1]))
    for copy in reads[count:] + reads[:count]:
        copy.start()
    reads[count].wait()
    reads[count + 1].wait()
    diffusion = num_ref[0:1][None]
    advection = num_ref[1:2][None]
    writes = []
    for i, part in enumerate(pieces):
        reads[i].wait()
        x = jnp.swapaxes(held_ref[part], 0, 1)
        edge_ref[0, :, part] = x[:2]
        edge_ref[1, :, part] = x[columns - 2 :]
        x = x[quarter - 2 : columns - quarter + 2]
        x = stencil(stencil(x, diffusion, advection), diffusion, advection)
        made_ref[:, :, part] = x.reshape(groups, half, part.size, entries)
        copy = pltpu.make_async_copy(made_ref.at[:, :, part], out_ref.at[:, :, part], sems.at[count + 2 + i])
        copy.start()
        writes.append(copy)
    for i, ref in enumerate((low_ref, high_ref)):
        copy = pltpu.make_async_copy(edge_ref.at[i], ref, sems.at[2 * count + 2 + i])
        copy.start()
        writes.append(copy)
    for copy in writes:
        copy.wait()


def outer_kernel(obs_ref, state_ref, before_ref, after_ref, diff_ref, adv_ref, out_ref, turned_ref):
    del obs_ref
    columns = state_ref.shape[1]
    quarter = columns // 4
    turned_ref[2 : columns + 2] = jnp.swapaxes(state_ref[...], 0, 1)
    turned_ref[:2] = before_ref[...]
    turned_ref[columns + 2 :] = after_ref[...]
    diffusion = diff_ref[...][None]
    advection = adv_ref[...][None]
    low = turned_ref[: quarter + 4]
    high = turned_ref[columns - quarter :]
    low = stencil(stencil(low, diffusion, advection), diffusion, advection)
    high = stencil(stencil(high, diffusion, advection), diffusion, advection)
    out_ref[...] = jnp.concatenate([low, high], axis=0).reshape(out_ref.shape)


def join_kernel(me_ref, *refs):
    *outer, inner_ref, out_ref, turned_ref, made_ref, sems = refs
    members, columns, entries = out_ref.shape
    groups, half, _, _ = inner_ref.shape
    quarter = columns // 4
    writes = []
    for i, part in enumerate(pieces_of(members)):
        for k, block in zip(issue_order(groups), outer):
            place = source(me_ref[0], k, groups) * half
            turned_ref[pl.ds(outer_start(place, quarter), half), part] = block[:, part]
        turned_ref[quarter : columns - quarter, part] = inner_ref[:, :, part].reshape(groups * half, part.size, entries)
        made_ref[part] = jnp.swapaxes(turned_ref[:, part], 0, 1)
        copy = pltpu.make_async_copy(made_ref.at[part], out_ref.at[part], sems.at[i])
        copy.start()
        writes.append(copy)
    for copy in writes:
        copy.wait()


def observe_kernel(me_ref, count_ref, where_ref, value_ref, rinv_ref, out_ref):
    columns, _, entries = out_ref.shape
    half = columns // 2
    quarter = where_ref.shape[0] // 4
    slots = where_ref.shape[1]
    place = me_ref[0] * half
    slot = lax.broadcasted_iota(jnp.int32, (1, slots), 1)
    row = lax.broadcasted_iota(jnp.int32, (16, slots), 0)
    entry = lax.broadcasted_iota(jnp.int32, (entries, slots), 0)
    for c in range(columns):
        at = inner_start(place, quarter) + c if c < half else outer_start(place, quarter) + c - half
        weight = jnp.where(slot < count_ref[0, at], rinv_ref[pl.ds(at, 1), :], 0.0)
        lhs = jnp.zeros((16, slots), jnp.float32)
        for first, source in ((0, weight), (3, weight * value_ref[pl.ds(at, 1), :])):
            for k, part in enumerate(split(source, 3)):
                lhs = jnp.where(row == first + k, part.astype(jnp.float32), lhs)
        onehot = (entry == where_ref[pl.ds(at, 1), :]).astype(jnp.float32).astype(jnp.bfloat16)
        sums = lax.dot_general(
            lhs.astype(jnp.bfloat16), onehot, (((1,), (1,)), ((), ())), preferred_element_type=jnp.float32
        )
        out_ref[c, 0:1] = sums[0:1] + (sums[1:2] + sums[2:3])
        out_ref[c, 1:2] = sums[3:4] + (sums[4:5] + sums[5:6])


def analyse_kernel(first, after_ref, obs_ref, states, outs, done_ref):
    del after_ref
    done_ref[...] = jnp.zeros_like(done_ref)
    groups = len(outs)
    columns, local, entries = outs[0].shape
    members = groups * local
    spread = members - 1.0
    every = range(columns)
    rows = lax.broadcasted_iota(jnp.int32, (members, members), 0)
    cols = lax.broadcasted_iota(jnp.int32, (members, members), 1)
    means, forces, scales, grams, ahead, root = [], [], [], [], [], []
    for c in every:
        x = jnp.concatenate([ref[c] for ref in states], axis=0)
        mean = jnp.sum(x, axis=0, keepdims=True) * (1.0 / members)
        anomaly = x - mean
        total = obs_ref[first + c, 0:1]
        forces.append(obs_ref[first + c, 1:2] - total * mean)
        means.append(mean)
        ahead.append(anomaly)
        grams.append(square_by_rows(split(anomaly * jnp.sqrt(total), 3)))
    for c in every:
        gram = grams[c] + jnp.where(rows == cols, spread, 0.0)
        norm = jnp.sum(jnp.sum(gram * gram, axis=0, keepdims=True), axis=1, keepdims=True)
        scales.append(jnp.sqrt(norm))
        root.append(gram * (1.0 / scales[c]))

    r = None
    for step in range(PAIRS):
        s = [split(root[c], 2) for c in every]
        p = [dot3(s[c], s[c]) for c in every]
        if r is not None:
            ahead = [2.25 * ahead[c] + dot3(r[c], split(ahead[c], 2)) for c in every]
        cubic = [dot3(split(0.0625 * p[c] - 0.5625 * root[c], 2), split(p[c], 2)) for c in every]
        r = [split(1.6875 * p[c] - 2.4375 * root[c] + cubic[c], 2) for c in every]
        if step < PAIRS - 1:
            t = [2.25 * root[c] + dot3(r[c], s[c]) for c in every]
            root = [2.25 * t[c] + dot3(split(t[c], 2), r[c]) for c in every]
    ahead = [2.25 * ahead[c] + dot3(r[c], split(ahead[c], 2)) for c in every]
    for c in every:
        w = ahead[c]
        inner = jnp.sum(w * forces[c], axis=1, keepdims=True)
        shift = jnp.sum(w * inner, axis=0, keepdims=True) / scales[c]
        result = means[c] + shift + w * jnp.sqrt(spread / scales[c])
        for k in range(groups):
            outs[k][c] = result[k * local : (k + 1) * local]


def analyse(states, obs, first, me, after, apart):
    groups, columns, local, entries = states.shape
    members = groups * local
    block = jax.ShapeDtypeStruct((columns, local, entries), jnp.float32)
    whole = jax.ShapeDtypeStruct(states.shape, jnp.float32)
    token = jax.ShapeDtypeStruct(after.shape, jnp.float32)

    def kernel(me_ref, after_ref, obs_ref, states_ref, *refs):
        *outs, done_ref = refs
        if apart:
            ins = [states_ref.at[target(me_ref[0], k, groups)] for k in range(groups)]
        else:
            ins = [states_ref.at[k] for k in range(groups)]
            outs = [outs[0].at[k] for k in range(groups)]
        analyse_kernel(first, after_ref, obs_ref, ins, outs, done_ref)

    return call(
        kernel,
        [block] * groups + [token] if apart else [whole, token],
        columns * 90 * 2 * members * members * entries,
        8 * columns * members * entries,
        in_specs=[SMEM] + [VMEM] * 3,
    )(me, after, obs, states)


def body(background, diffusion, advection, obs_where, obs_count, obs_value, obs_rinv):
    local, columns, entries = background.shape
    groups = lax.axis_size("mem")
    tiles = lax.axis_size("tile")
    half = columns // groups // 2
    size = background.size
    block = (half, local, entries)
    edge = jax.ShapeDtypeStruct((2, local, entries), jnp.float32)
    me = lax.axis_index("mem")[None].astype(jnp.int32)
    pieces = len(pieces_of(local))

    inner, low, high = call(
        inner_kernel,
        [jax.ShapeDtypeStruct((groups, *block), jnp.float32), edge, edge],
        20 * size,
        8 * size,
        vmem=60 * MIB,
        in_specs=[HBM, HBM, HBM],
        out_specs=[HBM, HBM, HBM],
        scratch_shapes=[
            pltpu.VMEM(background.shape, jnp.float32),
            pltpu.VMEM((8, entries), jnp.float32),
            pltpu.VMEM((2, 2, local, entries), jnp.float32),
            pltpu.VMEM((groups, *block), jnp.float32),
            pltpu.SemaphoreType.DMA((2 * pieces + 4,)),
        ],
    )(background, diffusion, advection)
    inner = lax.all_to_all(inner, "mem", split_axis=0, concat_axis=0, tiled=True)
    before = lax.ppermute(high, "tile", [(i, (i + 1) % tiles) for i in range(tiles)])
    after = lax.ppermute(low, "tile", [((i + 1) % tiles, i) for i in range(tiles)])
    obs = call(
        observe_kernel,
        jax.ShapeDtypeStruct((2 * half, 8, entries), jnp.float32),
        2 * half * 2 * 16 * obs_where.shape[2] * entries,
        12 * obs_where.size,
        in_specs=[SMEM, SMEM] + [VMEM] * 3,
    )(me, obs_count, obs_where[0], obs_value[0], obs_rinv[0])
    outer = call(
        outer_kernel,
        jax.ShapeDtypeStruct((groups, *block), jnp.float32),
        20 * size,
        8 * size,
        in_specs=[VMEM] * 6,
        scratch_shapes=[pltpu.VMEM((columns + 4, local, entries), jnp.float32)],
    )(obs, background, before, after, diffusion[None], advection[None])
    outer = lax.all_to_all(outer, "mem", split_axis=0, concat_axis=0, tiled=True)

    inner, done = analyse(inner, obs, 0, me, obs[0], False)
    inner = lax.all_to_all(inner, "mem", split_axis=0, concat_axis=0, tiled=True)
    *outer, _ = analyse(outer, obs, half, me, done, True)
    outer = exchange(outer)
    return call(
        join_kernel,
        jax.ShapeDtypeStruct(background.shape, jnp.float32),
        size,
        8 * size,
        in_specs=[SMEM] + [VMEM] * (groups + 1),
        out_specs=HBM,
        scratch_shapes=[
            pltpu.VMEM((columns, local, entries), jnp.float32),
            pltpu.VMEM(background.shape, jnp.float32),
            pltpu.SemaphoreType.DMA((pieces,)),
        ],
    )(me, *outer, inner)


def solution(mesh):
    return jax.shard_map(
        body,
        mesh=mesh,
        in_specs=(
            P("mem", "tile", None),
            P(),
            P(),
            P("tile", None, None),
            P("tile", None),
            P("tile", None, None),
            P("tile", None, None),
        ),
        out_specs=P("mem", "tile", None),
        check_vma=False,
    )
```

```python
import jax
import jax.numpy as jnp
from jax import lax
from jax.experimental import pallas as pl
from jax.experimental.pallas import tpu as pltpu
from jax.sharding import PartitionSpec as P

PAIRS = 6
SCRATCH = 9
MIB = 1024 * 1024
SMEM = pl.BlockSpec(memory_space=pltpu.SMEM)
VMEM = pl.BlockSpec(memory_space=pltpu.VMEM)
HBM = pl.BlockSpec(memory_space=pltpu.HBM)


def call(kernel, out_shape, flops, moved, vmem=48 * MIB, **options):
    return pl.pallas_call(
        kernel,
        out_shape=out_shape,
        compiler_params=pltpu.CompilerParams(vmem_limit_bytes=vmem),
        cost_estimate=pl.CostEstimate(flops=flops, bytes_accessed=moved, transcendentals=0),
        **options,
    )


def target(me, k, groups):
    if groups & (groups - 1) == 0:
        return me ^ k
    return lax.rem(me + k, groups)


def source(me, k, groups):
    if groups & (groups - 1) == 0:
        return me ^ k
    return lax.rem(me + groups - k, groups)


def issue_order(groups):
    return sorted(range(1, groups), key=lambda k: (k != 1, -(k // 2).bit_count(), k)) + [0]


def exchange(blocks):
    groups = len(blocks)
    out = []
    for k in issue_order(groups):
        pairs = [(i, i ^ k if groups & (groups - 1) == 0 else (i + k) % groups) for i in range(groups)]
        out.append(lax.ppermute(blocks[k], "mem", pairs) if k else blocks[0])
    return out


def split(x, parts):
    out = []
    for _ in range(parts):
        part = x.astype(jnp.bfloat16)
        out.append(part)
        x = x - part.astype(jnp.float32)
    return out


def store(ref, c, rows, x):
    for i, part in enumerate(split(x, 2)):
        ref[i, c, rows] = part


def multiply(a_ref, b_ref, c, rows):
    lhs = jnp.concatenate([a_ref[0, c, rows], a_ref[1, c, rows], a_ref[0, c, rows]], axis=1)
    rhs = jnp.concatenate([b_ref[0, c], b_ref[0, c], b_ref[1, c]], axis=0)
    return jnp.dot(lhs, rhs, preferred_element_type=jnp.float32)


def square_by_rows(parts):
    p0, p1, p2 = parts
    lhs = jnp.concatenate([p2, p0, p1, p1, p0, p0], axis=1)
    rhs = jnp.concatenate([p0, p2, p1, p0, p1, p0], axis=1)
    return lax.dot_general(lhs, rhs, (((1,), (1,)), ((), ())), preferred_element_type=jnp.float32)


def stencil(padded, diffusion, advection):
    middle = padded[1:-1]
    left = padded[:-2]
    right = padded[2:]
    return middle + diffusion * (left - 2.0 * middle + right) + advection * (0.5 * (left - right))


def inner_start(place, quarter):
    return place + quarter


def outer_start(place, quarter):
    return jnp.where(place < quarter, place, place + 2 * quarter)


def pieces_of(members):
    rows = 8 if members % 8 == 0 else members
    return [pl.ds(first, rows) for first in range(0, members, rows)]


def inner_kernel(state_ref, diff_ref, adv_ref, out_ref, low_ref, high_ref, held_ref, num_ref, edge_ref, made_ref, sems):
    members, columns, entries = state_ref.shape
    groups, half, _, _ = out_ref.shape
    quarter = columns // 4
    pieces = pieces_of(members)
    count = len(pieces)
    reads = [pltpu.make_async_copy(state_ref.at[part], held_ref.at[part], sems.at[i]) for i, part in enumerate(pieces)]
    reads.append(pltpu.make_async_copy(diff_ref, num_ref.at[0], sems.at[count]))
    reads.append(pltpu.make_async_copy(adv_ref, num_ref.at[1], sems.at[count + 1]))
    for copy in reads[count:] + reads[:count]:
        copy.start()
    reads[count].wait()
    reads[count + 1].wait()
    diffusion = num_ref[0:1][None]
    advection = num_ref[1:2][None]
    writes = []
    for i, part in enumerate(pieces):
        reads[i].wait()
        x = jnp.swapaxes(held_ref[part], 0, 1)
        edge_ref[0, :, part] = x[:2]
        edge_ref[1, :, part] = x[columns - 2 :]
        x = x[quarter - 2 : columns - quarter + 2]
        x = stencil(stencil(x, diffusion, advection), diffusion, advection)
        made_ref[:, :, part] = x.reshape(groups, half, part.size, entries)
        copy = pltpu.make_async_copy(made_ref.at[:, :, part], out_ref.at[:, :, part], sems.at[count + 2 + i])
        copy.start()
        writes.append(copy)
    for i, ref in enumerate((low_ref, high_ref)):
        copy = pltpu.make_async_copy(edge_ref.at[i], ref, sems.at[2 * count + 2 + i])
        copy.start()
        writes.append(copy)
    for copy in writes:
        copy.wait()


def outer_kernel(obs_ref, state_ref, before_ref, after_ref, diff_ref, adv_ref, out_ref, turned_ref):
    del obs_ref
    columns = state_ref.shape[1]
    quarter = columns // 4
    turned_ref[2 : columns + 2] = jnp.swapaxes(state_ref[...], 0, 1)
    turned_ref[:2] = before_ref[...]
    turned_ref[columns + 2 :] = after_ref[...]
    diffusion = diff_ref[...][None]
    advection = adv_ref[...][None]
    low = turned_ref[: quarter + 4]
    high = turned_ref[columns - quarter :]
    low = stencil(stencil(low, diffusion, advection), diffusion, advection)
    high = stencil(stencil(high, diffusion, advection), diffusion, advection)
    out_ref[...] = jnp.concatenate([low, high], axis=0).reshape(out_ref.shape)


def join_kernel(me_ref, *refs):
    *outer, inner_ref, out_ref, turned_ref, made_ref, sems = refs
    members, columns, entries = out_ref.shape
    groups, half, _, _ = inner_ref.shape
    quarter = columns // 4
    writes = []
    for i, part in enumerate(pieces_of(members)):
        for k, block in zip(issue_order(groups), outer):
            place = source(me_ref[0], k, groups) * half
            turned_ref[pl.ds(outer_start(place, quarter), half), part] = block[:, part]
        turned_ref[quarter : columns - quarter, part] = inner_ref[:, :, part].reshape(groups * half, part.size, entries)
        made_ref[part] = jnp.swapaxes(turned_ref[:, part], 0, 1)
        copy = pltpu.make_async_copy(made_ref.at[part], out_ref.at[part], sems.at[i])
        copy.start()
        writes.append(copy)
    for copy in writes:
        copy.wait()


def observe_kernel(me_ref, count_ref, where_ref, value_ref, rinv_ref, out_ref):
    columns, _, entries = out_ref.shape
    half = columns // 2
    quarter = where_ref.shape[0] // 4
    slots = where_ref.shape[1]
    place = me_ref[0] * half
    slot = lax.broadcasted_iota(jnp.int32, (1, slots), 1)
    row = lax.broadcasted_iota(jnp.int32, (16, slots), 0)
    entry = lax.broadcasted_iota(jnp.int32, (entries, slots), 0)
    for c in range(columns):
        at = inner_start(place, quarter) + c if c < half else outer_start(place, quarter) + c - half
        weight = jnp.where(slot < count_ref[0, at], rinv_ref[pl.ds(at, 1), :], 0.0)
        lhs = jnp.zeros((16, slots), jnp.float32)
        for first, source in ((0, weight), (3, weight * value_ref[pl.ds(at, 1), :])):
            for k, part in enumerate(split(source, 3)):
                lhs = jnp.where(row == first + k, part.astype(jnp.float32), lhs)
        onehot = (entry == where_ref[pl.ds(at, 1), :]).astype(jnp.float32).astype(jnp.bfloat16)
        sums = lax.dot_general(
            lhs.astype(jnp.bfloat16), onehot, (((1,), (1,)), ((), ())), preferred_element_type=jnp.float32
        )
        out_ref[c, 0:1] = sums[0:1] + (sums[1:2] + sums[2:3])
        out_ref[c, 1:2] = sums[3:4] + (sums[4:5] + sums[5:6])


def analyse_kernel(first, after_ref, obs_ref, states, outs, done_ref, root, mixed, ahead, s, p, u, t, r, w):
    del after_ref
    done_ref[...] = jnp.zeros_like(done_ref)
    groups = len(outs)
    columns, local, entries = outs[0].shape
    members = groups * local
    spread = members - 1.0
    every = range(columns)
    parts = [(c, pl.ds(half, members // 2)) for c in every for half in (0, members // 2)]
    rows = lax.broadcasted_iota(jnp.int32, (members, members), 0)
    cols = lax.broadcasted_iota(jnp.int32, (members, members), 1)
    means, forces, scales, grams = [], [], [], []
    for c in every:
        x = jnp.concatenate([ref[c] for ref in states], axis=0)
        mean = jnp.sum(x, axis=0, keepdims=True) * (1.0 / members)
        anomaly = x - mean
        total = obs_ref[first + c, 0:1]
        forces.append(obs_ref[first + c, 1:2] - total * mean)
        means.append(mean)
        grams.append(square_by_rows(split(anomaly * jnp.sqrt(total), 3)))
        ahead[c] = anomaly
        store(w.at[0], c, slice(None), anomaly)
    for c in every:
        gram = grams[c] + jnp.where(rows == cols, spread, 0.0)
        norm = jnp.sum(jnp.sum(gram * gram, axis=0, keepdims=True), axis=1, keepdims=True)
        scales.append(jnp.sqrt(norm))
        gram = gram * (1.0 / scales[c])
        root[c] = gram
        store(s, c, slice(None), gram)

    def advance(step):
        for c, rows in parts:
            x = 2.25 * ahead[c, rows] + multiply(r.at[step % 2], w.at[step % 2], c, rows)
            ahead[c, rows] = x
            if step < PAIRS - 1:
                store(w.at[(step + 1) % 2], c, rows, x)

    for step in range(PAIRS):
        for c, rows in parts:
            x = multiply(s, s, c, rows)
            y = root[c, rows]
            store(p, c, rows, x)
            store(u, c, rows, 0.0625 * x - 0.5625 * y)
            mixed[c, rows] = 1.6875 * x - 2.4375 * y
        if step > 0:
            advance(step - 1)
        for c, rows in parts:
            store(r.at[step % 2], c, rows, mixed[c, rows] + multiply(u, p, c, rows))
        if step < PAIRS - 1:
            for c, rows in parts:
                x = 2.25 * root[c, rows] + multiply(r.at[step % 2], s, c, rows)
                store(t, c, rows, x)
                mixed[c, rows] = 2.25 * x
            for c, rows in parts:
                x = mixed[c, rows] + multiply(t, r.at[step % 2], c, rows)
                root[c, rows] = x
                store(s, c, rows, x)
    advance(PAIRS - 1)
    for c in every:
        x = ahead[c]
        inner = jnp.sum(x * forces[c], axis=1, keepdims=True)
        shift = jnp.sum(x * inner, axis=0, keepdims=True) / scales[c]
        result = means[c] + shift + x * jnp.sqrt(spread / scales[c])
        for k in range(groups):
            outs[k][c] = result[k * local : (k + 1) * local]


def analyse(states, obs, first, me, after, apart):
    groups, columns, local, entries = states.shape
    members = groups * local
    block = jax.ShapeDtypeStruct((columns, local, entries), jnp.float32)
    whole = jax.ShapeDtypeStruct(states.shape, jnp.float32)
    token = jax.ShapeDtypeStruct(after.shape, jnp.float32)
    full = pltpu.VMEM((columns, members, members), jnp.float32)
    pair = pltpu.VMEM((2, columns, members, members), jnp.bfloat16)
    two = pltpu.VMEM((2, 2, columns, members, members), jnp.bfloat16)
    ahead = pltpu.VMEM((columns, members, entries), jnp.float32)
    factor = pltpu.VMEM((2, 2, columns, members, entries), jnp.bfloat16)

    def kernel(me_ref, after_ref, obs_ref, states_ref, *refs):
        *outs, done_ref = refs[:-SCRATCH]
        scratch = refs[-SCRATCH:]
        if apart:
            ins = [states_ref.at[target(me_ref[0], k, groups)] for k in range(groups)]
        else:
            ins = [states_ref.at[k] for k in range(groups)]
            outs = [outs[0].at[k] for k in range(groups)]
        analyse_kernel(first, after_ref, obs_ref, ins, outs, done_ref, *scratch)

    return call(
        kernel,
        [block] * groups + [token] if apart else [whole, token],
        columns * 90 * 2 * members * members * entries,
        8 * columns * members * entries,
        in_specs=[SMEM] + [VMEM] * 3,
        scratch_shapes=[full, full, ahead, pair, pair, pair, pair, two, factor],
    )(me, after, obs, states)


def body(background, diffusion, advection, obs_where, obs_count, obs_value, obs_rinv):
    local, columns, entries = background.shape
    groups = lax.axis_size("mem")
    tiles = lax.axis_size("tile")
    half = columns // groups // 2
    size = background.size
    block = (half, local, entries)
    edge = jax.ShapeDtypeStruct((2, local, entries), jnp.float32)
    me = lax.axis_index("mem")[None].astype(jnp.int32)
    pieces = len(pieces_of(local))

    inner, low, high = call(
        inner_kernel,
        [jax.ShapeDtypeStruct((groups, *block), jnp.float32), edge, edge],
        20 * size,
        8 * size,
        vmem=60 * MIB,
        in_specs=[HBM, HBM, HBM],
        out_specs=[HBM, HBM, HBM],
        scratch_shapes=[
            pltpu.VMEM(background.shape, jnp.float32),
            pltpu.VMEM((8, entries), jnp.float32),
            pltpu.VMEM((2, 2, local, entries), jnp.float32),
            pltpu.VMEM((groups, *block), jnp.float32),
            pltpu.SemaphoreType.DMA((2 * pieces + 4,)),
        ],
    )(background, diffusion, advection)
    inner = lax.all_to_all(inner, "mem", split_axis=0, concat_axis=0, tiled=True)
    before = lax.ppermute(high, "tile", [(i, (i + 1) % tiles) for i in range(tiles)])
    after = lax.ppermute(low, "tile", [((i + 1) % tiles, i) for i in range(tiles)])
    obs = call(
        observe_kernel,
        jax.ShapeDtypeStruct((2 * half, 8, entries), jnp.float32),
        2 * half * 2 * 16 * obs_where.shape[2] * entries,
        12 * obs_where.size,
        in_specs=[SMEM, SMEM] + [VMEM] * 3,
    )(me, obs_count, obs_where[0], obs_value[0], obs_rinv[0])
    outer = call(
        outer_kernel,
        jax.ShapeDtypeStruct((groups, *block), jnp.float32),
        20 * size,
        8 * size,
        in_specs=[VMEM] * 6,
        scratch_shapes=[pltpu.VMEM((columns + 4, local, entries), jnp.float32)],
    )(obs, background, before, after, diffusion[None], advection[None])
    outer = lax.all_to_all(outer, "mem", split_axis=0, concat_axis=0, tiled=True)

    inner, done = analyse(inner, obs, 0, me, obs[0], False)
    inner = lax.all_to_all(inner, "mem", split_axis=0, concat_axis=0, tiled=True)
    *outer, _ = analyse(outer, obs, half, me, done, True)
    outer = exchange(outer)
    return call(
        join_kernel,
        jax.ShapeDtypeStruct(background.shape, jnp.float32),
        size,
        8 * size,
        in_specs=[SMEM] + [VMEM] * (groups + 1),
        out_specs=HBM,
        scratch_shapes=[
            pltpu.VMEM((columns, local, entries), jnp.float32),
            pltpu.VMEM(background.shape, jnp.float32),
            pltpu.SemaphoreType.DMA((pieces,)),
        ],
    )(me, *outer, inner)


def solution(mesh):
    return jax.shard_map(
        body,
        mesh=mesh,
        in_specs=(
            P("mem", "tile", None),
            P(),
            P(),
            P("tile", None, None),
            P("tile", None),
            P("tile", None, None),
            P("tile", None, None),
        ),
        out_specs=P("mem", "tile", None),
        check_vma=False,
    )
```

```python
import jax
import jax.numpy as jnp
from jax import lax
from jax.experimental import pallas as pl
from jax.experimental.pallas import tpu as pltpu
from jax.sharding import PartitionSpec as P

PAIRS = 6
SCRATCH = 9
MIB = 1024 * 1024
SMEM = pl.BlockSpec(memory_space=pltpu.SMEM)
VMEM = pl.BlockSpec(memory_space=pltpu.VMEM)
HBM = pl.BlockSpec(memory_space=pltpu.HBM)


def call(kernel, out_shape, flops, moved, vmem=48 * MIB, **options):
    return pl.pallas_call(
        kernel,
        out_shape=out_shape,
        compiler_params=pltpu.CompilerParams(vmem_limit_bytes=vmem),
        cost_estimate=pl.CostEstimate(flops=flops, bytes_accessed=moved, transcendentals=0),
        **options,
    )


def target(me, k, groups):
    if groups & (groups - 1) == 0:
        return me ^ k
    return lax.rem(me + k, groups)


def issue_order(groups):
    return sorted(range(1, groups), key=lambda k: (k != 1, -(k // 2).bit_count(), k)) + [0]


def exchange(blocks, back):
    groups = len(blocks)
    out = list(blocks)
    for k in issue_order(groups)[:-1]:
        pairs = [(i, i ^ k if groups & (groups - 1) == 0 else (i + k) % groups) for i in range(groups)]
        if back:
            pairs = [(j, i) for i, j in pairs]
        out[k] = lax.ppermute(blocks[k], "mem", pairs)
    return out


def split(x, parts):
    out = []
    for _ in range(parts):
        part = x.astype(jnp.bfloat16)
        out.append(part)
        x = x - part.astype(jnp.float32)
    return out


def store(ref, c, rows, x):
    for i, part in enumerate(split(x, 2)):
        ref[i, c, rows] = part


def multiply(a_ref, b_ref, c, rows):
    lhs = jnp.concatenate([a_ref[0, c, rows], a_ref[1, c, rows], a_ref[0, c, rows]], axis=1)
    rhs = jnp.concatenate([b_ref[0, c], b_ref[0, c], b_ref[1, c]], axis=0)
    return jnp.dot(lhs, rhs, preferred_element_type=jnp.float32)


def square_by_rows(parts):
    p0, p1, p2 = parts
    lhs = jnp.concatenate([p2, p0, p1, p1, p0, p0], axis=1)
    rhs = jnp.concatenate([p0, p2, p1, p0, p1, p0], axis=1)
    return lax.dot_general(lhs, rhs, (((1,), (1,)), ((), ())), preferred_element_type=jnp.float32)


def stencil(padded, diffusion, advection):
    middle = padded[1:-1]
    left = padded[:-2]
    right = padded[2:]
    return middle + diffusion * (left - 2.0 * middle + right) + advection * (0.5 * (left - right))


def inner_start(place, quarter):
    return place + quarter


def outer_start(place, quarter):
    return jnp.where(place < quarter, place, place + 2 * quarter)


def pieces_of(members):
    rows = 8 if members % 8 == 0 else members
    return [pl.ds(first, rows) for first in range(0, members, rows)]


def inner_kernel(tile_ref, state_ref, diff_ref, adv_ref, out_ref, first_ref, second_ref, held_ref, num_ref, edge_ref, made_ref, sems):
    members, columns, entries = state_ref.shape
    groups, half, _, _ = out_ref.shape
    quarter = columns // 4
    pieces = pieces_of(members)
    count = len(pieces)
    reads = [pltpu.make_async_copy(state_ref.at[part], held_ref.at[part], sems.at[i]) for i, part in enumerate(pieces)]
    reads.append(pltpu.make_async_copy(diff_ref, num_ref.at[0], sems.at[count]))
    reads.append(pltpu.make_async_copy(adv_ref, num_ref.at[1], sems.at[count + 1]))
    for copy in reads[count:] + reads[:count]:
        copy.start()
    reads[count].wait()
    reads[count + 1].wait()
    diffusion = num_ref[0:1][None]
    advection = num_ref[1:2][None]
    writes = []
    for i, part in enumerate(pieces):
        reads[i].wait()
        x = jnp.swapaxes(held_ref[part], 0, 1)
        edge_ref[0, :, part] = x[:2]
        edge_ref[1, :, part] = x[columns - 2 :]
        x = x[quarter - 2 : columns - quarter + 2]
        x = stencil(stencil(x, diffusion, advection), diffusion, advection)
        made_ref[:, :, part] = x.reshape(groups, half, part.size, entries)
        copy = pltpu.make_async_copy(made_ref.at[:, :, part], out_ref.at[:, :, part], sems.at[count + 2 + i])
        copy.start()
        writes.append(copy)
    odd = tile_ref[0] & 1
    for i, ref in enumerate((first_ref, second_ref)):
        copy = pltpu.make_async_copy(edge_ref.at[1 - odd if i == 0 else odd], ref, sems.at[2 * count + 2 + i])
        copy.start()
        writes.append(copy)
    for copy in writes:
        copy.wait()


def outer_kernel(me_ref, tile_ref, obs_ref, state_ref, first_ref, second_ref, diff_ref, adv_ref, *refs):
    del obs_ref
    *outs, turned_ref = refs
    groups = len(outs)
    half = outs[0].shape[0]
    columns = state_ref.shape[1]
    turned_ref[2 : columns + 2] = jnp.swapaxes(state_ref[...], 0, 1)
    odd = tile_ref[0] & 1
    first_side = pl.ds((columns + 2) * (1 - odd), 2)
    second_side = pl.ds((columns + 2) * odd, 2)
    turned_ref[first_side] = first_ref[1 - odd]
    turned_ref[second_side] = second_ref[odd]
    diffusion = diff_ref[...][None]
    advection = adv_ref[...][None]
    for k in range(groups):
        start = outer_start(target(me_ref[0], k, groups) * half, columns // 4)
        x = turned_ref[pl.ds(start, half + 4)]
        outs[k][...] = stencil(stencil(x, diffusion, advection), diffusion, advection)


def join_kernel(me_ref, *refs):
    *outer, inner_ref, out_ref, turned_ref, made_ref, sems = refs
    members, columns, entries = out_ref.shape
    groups, half, _, _ = inner_ref.shape
    quarter = columns // 4
    writes = []
    for i, part in enumerate(pieces_of(members)):
        for k, block in zip(issue_order(groups), outer):
            place = target(me_ref[0], k, groups) * half
            turned_ref[pl.ds(outer_start(place, quarter), half), part] = block[:, part]
        turned_ref[quarter : columns - quarter, part] = inner_ref[:, :, part].reshape(groups * half, part.size, entries)
        made_ref[part] = jnp.swapaxes(turned_ref[:, part], 0, 1)
        copy = pltpu.make_async_copy(made_ref.at[part], out_ref.at[part], sems.at[i])
        copy.start()
        writes.append(copy)
    for copy in writes:
        copy.wait()


def observe_kernel(me_ref, count_ref, where_ref, value_ref, rinv_ref, out_ref):
    columns, _, entries = out_ref.shape
    half = columns // 2
    quarter = where_ref.shape[0] // 4
    slots = where_ref.shape[1]
    place = me_ref[0] * half
    slot = lax.broadcasted_iota(jnp.int32, (1, slots), 1)
    row = lax.broadcasted_iota(jnp.int32, (16, slots), 0)
    entry = lax.broadcasted_iota(jnp.int32, (entries, slots), 0)
    for c in range(columns):
        at = inner_start(place, quarter) + c if c < half else outer_start(place, quarter) + c - half
        weight = jnp.where(slot < count_ref[0, at], rinv_ref[pl.ds(at, 1), :], 0.0)
        lhs = jnp.zeros((16, slots), jnp.float32)
        for first, source in ((0, weight), (3, weight * value_ref[pl.ds(at, 1), :])):
            for k, part in enumerate(split(source, 3)):
                lhs = jnp.where(row == first + k, part.astype(jnp.float32), lhs)
        onehot = (entry == where_ref[pl.ds(at, 1), :]).astype(jnp.float32).astype(jnp.bfloat16)
        sums = lax.dot_general(
            lhs.astype(jnp.bfloat16), onehot, (((1,), (1,)), ((), ())), preferred_element_type=jnp.float32
        )
        out_ref[c, 0:1] = sums[0:1] + (sums[1:2] + sums[2:3])
        out_ref[c, 1:2] = sums[3:4] + (sums[4:5] + sums[5:6])


def analyse_kernel(first, after_ref, obs_ref, states, outs, done_ref, root, mixed, ahead, s, p, u, t, r, w):
    del after_ref
    done_ref[...] = jnp.zeros_like(done_ref)
    groups = len(outs)
    columns, local, entries = outs[0].shape
    members = groups * local
    spread = members - 1.0
    every = range(columns)
    parts = [(c, pl.ds(half, members // 2)) for c in every for half in (0, members // 2)]
    rows = lax.broadcasted_iota(jnp.int32, (members, members), 0)
    cols = lax.broadcasted_iota(jnp.int32, (members, members), 1)
    means, forces, scales, grams = [], [], [], []
    for c in every:
        x = jnp.concatenate([ref[c] for ref in states], axis=0)
        mean = jnp.sum(x, axis=0, keepdims=True) * (1.0 / members)
        anomaly = x - mean
        total = obs_ref[first + c, 0:1]
        forces.append(obs_ref[first + c, 1:2] - total * mean)
        means.append(mean)
        grams.append(square_by_rows(split(anomaly * jnp.sqrt(total), 3)))
        ahead[c] = anomaly
        store(w.at[0], c, slice(None), anomaly)
    for c in every:
        gram = grams[c] + jnp.where(rows == cols, spread, 0.0)
        norm = jnp.sum(jnp.sum(gram * gram, axis=0, keepdims=True), axis=1, keepdims=True)
        scales.append(jnp.sqrt(norm))
        gram = gram * (1.0 / scales[c])
        root[c] = gram
        store(s, c, slice(None), gram)

    def advance(step):
        for c, rows in parts:
            x = 2.25 * ahead[c, rows] + multiply(r.at[step % 2], w.at[step % 2], c, rows)
            ahead[c, rows] = x
            if step < PAIRS - 1:
                store(w.at[(step + 1) % 2], c, rows, x)

    for step in range(PAIRS):
        for c, rows in parts:
            x = multiply(s, s, c, rows)
            y = root[c, rows]
            store(p, c, rows, x)
            store(u, c, rows, 0.0625 * x - 0.5625 * y)
            mixed[c, rows] = 1.6875 * x - 2.4375 * y
        if step > 0:
            advance(step - 1)
        for c, rows in parts:
            store(r.at[step % 2], c, rows, mixed[c, rows] + multiply(u, p, c, rows))
        if step < PAIRS - 1:
            for c, rows in parts:
                x = 2.25 * root[c, rows] + multiply(r.at[step % 2], s, c, rows)
                store(t, c, rows, x)
                mixed[c, rows] = 2.25 * x
            for c, rows in parts:
                x = mixed[c, rows] + multiply(t, r.at[step % 2], c, rows)
                root[c, rows] = x
                store(s, c, rows, x)
    advance(PAIRS - 1)
    for c in every:
        x = ahead[c]
        inner = jnp.sum(x * forces[c], axis=1, keepdims=True)
        shift = jnp.sum(x * inner, axis=0, keepdims=True) / scales[c]
        result = means[c] + shift + x * jnp.sqrt(spread / scales[c])
        for k in range(groups):
            outs[k][c] = result[k * local : (k + 1) * local]


def analyse(states, obs, first, after, apart):
    groups = len(states)
    columns, local, entries = states[0].shape
    members = groups * local
    block = jax.ShapeDtypeStruct((columns, local, entries), jnp.float32)
    whole = jax.ShapeDtypeStruct((groups, columns, local, entries), jnp.float32)
    token = jax.ShapeDtypeStruct(after.shape, jnp.float32)
    full = pltpu.VMEM((columns, members, members), jnp.float32)
    pair = pltpu.VMEM((2, columns, members, members), jnp.bfloat16)
    two = pltpu.VMEM((2, 2, columns, members, members), jnp.bfloat16)
    ahead = pltpu.VMEM((columns, members, entries), jnp.float32)
    factor = pltpu.VMEM((2, 2, columns, members, entries), jnp.bfloat16)

    def kernel(after_ref, obs_ref, *refs):
        *blocks, done_ref = refs[:-SCRATCH]
        if not apart:
            blocks = [ref.at[k] for ref in blocks for k in range(groups)]
        analyse_kernel(first, after_ref, obs_ref, blocks[:groups], blocks[groups:], done_ref, *refs[-SCRATCH:])

    operands = states if apart else [states]

    return call(
        kernel,
        [block] * groups + [token] if apart else [whole, token],
        columns * 90 * 2 * members * members * entries,
        8 * columns * members * entries,
        in_specs=[VMEM] * (2 + len(operands)),
        scratch_shapes=[full, full, ahead, pair, pair, pair, pair, two, factor],
    )(after, obs, *operands)


def body(background, diffusion, advection, obs_where, obs_count, obs_value, obs_rinv):
    local, columns, entries = background.shape
    groups = lax.axis_size("mem")
    tiles = lax.axis_size("tile")
    half = columns // groups // 2
    size = background.size
    block = (half, local, entries)
    edge = jax.ShapeDtypeStruct((2, local, entries), jnp.float32)
    me = lax.axis_index("mem")[None].astype(jnp.int32)
    tile = lax.axis_index("tile")[None].astype(jnp.int32)
    pieces = len(pieces_of(local))

    inner, first, second = call(
        inner_kernel,
        [jax.ShapeDtypeStruct((groups, *block), jnp.float32), edge, edge],
        20 * size,
        8 * size,
        vmem=60 * MIB,
        in_specs=[SMEM, HBM, HBM, HBM],
        out_specs=[HBM, HBM, HBM],
        scratch_shapes=[
            pltpu.VMEM(background.shape, jnp.float32),
            pltpu.VMEM((8, entries), jnp.float32),
            pltpu.VMEM((2, 2, local, entries), jnp.float32),
            pltpu.VMEM((groups, *block), jnp.float32),
            pltpu.SemaphoreType.DMA((2 * pieces + 4,)),
        ],
    )(tile, background, diffusion, advection)
    inner = lax.all_to_all(inner, "mem", split_axis=0, concat_axis=0, tiled=True)
    pairs = [[[(i + shift) % tiles, (i + 1 + shift) % tiles] for i in range(0, tiles, 2)] for shift in range(2)]
    first = lax.all_gather(first, "tile", axis_index_groups=pairs[0])
    second = lax.all_gather(second, "tile", axis_index_groups=pairs[1])
    obs = call(
        observe_kernel,
        jax.ShapeDtypeStruct((2 * half, 8, entries), jnp.float32),
        2 * half * 2 * 16 * obs_where.shape[2] * entries,
        12 * obs_where.size,
        in_specs=[SMEM, SMEM] + [VMEM] * 3,
    )(me, obs_count, obs_where[0], obs_value[0], obs_rinv[0])
    outer = call(
        outer_kernel,
        [jax.ShapeDtypeStruct(block, jnp.float32)] * groups,
        20 * size,
        8 * size,
        in_specs=[SMEM, SMEM] + [VMEM] * 6,
        scratch_shapes=[pltpu.VMEM((columns + 4, local, entries), jnp.float32)],
    )(me, tile, obs, background, first, second, diffusion[None], advection[None])
    outer = exchange(outer, False)
    outer = [outer[k] for k in issue_order(groups)]

    inner, done = analyse(inner, obs, 0, obs[0], False)
    inner = lax.all_to_all(inner, "mem", split_axis=0, concat_axis=0, tiled=True)
    *outer, _ = analyse(outer, obs, half, done, True)
    outer = exchange([outer[issue_order(groups).index(k)] for k in range(groups)], True)
    outer = [outer[k] for k in issue_order(groups)]
    return call(
        join_kernel,
        jax.ShapeDtypeStruct(background.shape, jnp.float32),
        size,
        8 * size,
        in_specs=[SMEM] + [VMEM] * (groups + 1),
        out_specs=HBM,
        scratch_shapes=[
            pltpu.VMEM((columns, local, entries), jnp.float32),
            pltpu.VMEM(background.shape, jnp.float32),
            pltpu.SemaphoreType.DMA((pieces,)),
        ],
    )(me, *outer, inner)


def solution(mesh):
    return jax.shard_map(
        body,
        mesh=mesh,
        in_specs=(
            P("mem", "tile", None),
            P(),
            P(),
            P("tile", None, None),
            P("tile", None),
            P("tile", None, None),
            P("tile", None, None),
        ),
        out_specs=P("mem", "tile", None),
        check_vma=False,
    )
```

```python
import jax
import jax.numpy as jnp
from jax import lax
from jax.experimental import pallas as pl
from jax.experimental.pallas import tpu as pltpu
from jax.sharding import PartitionSpec as P

PAIRS = 6
SCRATCH = 9
MIB = 1024 * 1024
SMEM = pl.BlockSpec(memory_space=pltpu.SMEM)
VMEM = pl.BlockSpec(memory_space=pltpu.VMEM)
HBM = pl.BlockSpec(memory_space=pltpu.HBM)


def call(kernel, out_shape, flops, moved, vmem=48 * MIB, **options):
    return pl.pallas_call(
        kernel,
        out_shape=out_shape,
        compiler_params=pltpu.CompilerParams(vmem_limit_bytes=vmem),
        cost_estimate=pl.CostEstimate(flops=flops, bytes_accessed=moved, transcendentals=0),
        **options,
    )


def target(me, step, other, chips):
    chip = me // 2 ^ step if chips & (chips - 1) == 0 else lax.rem(me // 2 + step, chips)
    return 2 * chip + (me & 1 ^ other)


def source(me, step, other, chips):
    chip = me // 2 ^ step if chips & (chips - 1) == 0 else lax.rem(me // 2 + chips - step, chips)
    return 2 * chip + (me & 1 ^ other)


def issue_order(chips):
    steps = sorted(range(1, chips), key=lambda step: (-step.bit_count(), step))
    return [(0, 1)] + [(step, other) for step in steps for other in range(2)] + [(0, 0)]


def exchange(blocks):
    chips = len(blocks) // 2
    out = []
    for (step, other), block in zip(issue_order(chips), blocks):
        pairs = []
        for i in range(2 * chips):
            chip = i // 2 ^ step if chips & (chips - 1) == 0 else (i // 2 + step) % chips
            pairs.append((i, 2 * chip + (i & 1 ^ other)))
        out.append(lax.ppermute(block, "mem", pairs) if step or other else block)
    return out


def gather(blocks):
    chips = blocks.shape[0]
    same = [[2 * chip + core for chip in range(chips)] for core in range(2)]
    blocks = lax.all_to_all(blocks, "mem", split_axis=0, concat_axis=0, axis_index_groups=same, tiled=True)
    return blocks, lax.ppermute(blocks[:, 1], "mem", [(i, i ^ 1) for i in range(2 * chips)])


def split(x, parts):
    out = []
    for _ in range(parts):
        part = x.astype(jnp.bfloat16)
        out.append(part)
        x = x - part.astype(jnp.float32)
    return out


def store(ref, c, rows, x):
    for i, part in enumerate(split(x, 2)):
        ref[i, c, rows] = part


def multiply(a_ref, b_ref, c, rows):
    lhs = jnp.concatenate([a_ref[0, c, rows], a_ref[1, c, rows], a_ref[0, c, rows]], axis=1)
    rhs = jnp.concatenate([b_ref[0, c], b_ref[0, c], b_ref[1, c]], axis=0)
    return jnp.dot(lhs, rhs, preferred_element_type=jnp.float32)


def square_by_rows(parts):
    p0, p1, p2 = parts
    lhs = jnp.concatenate([p2, p0, p1, p1, p0, p0], axis=1)
    rhs = jnp.concatenate([p0, p2, p1, p0, p1, p0], axis=1)
    return lax.dot_general(lhs, rhs, (((1,), (1,)), ((), ())), preferred_element_type=jnp.float32)


def stencil(padded, diffusion, advection):
    middle = padded[1:-1]
    left = padded[:-2]
    right = padded[2:]
    return middle + diffusion * (left - 2.0 * middle + right) + advection * (0.5 * (left - right))


def inner_start(place, quarter):
    return place + quarter


def outer_start(place, quarter):
    return jnp.where(place < quarter, place, place + 2 * quarter)


def pieces_of(members):
    rows = 8 if members % 8 == 0 else members
    return [pl.ds(first, rows) for first in range(0, members, rows)]


def place_blocks(out_ref, me, x, part):
    chips, _, half, _, _ = out_ref.shape
    for chip in range(chips):
        for core in range(2):
            first = (2 * chip + core) * half
            out_ref[chip, me & 1 ^ core, :, part] = x[first : first + half]


def inner_kernel(place_ref, state_ref, diff_ref, adv_ref, out_ref, first_ref, second_ref, held_ref, num_ref, edge_ref, made_ref, sems):
    members, columns, _ = state_ref.shape
    quarter = columns // 4
    pieces = pieces_of(members)
    count = len(pieces)
    reads = [pltpu.make_async_copy(state_ref.at[part], held_ref.at[part], sems.at[i]) for i, part in enumerate(pieces)]
    reads.append(pltpu.make_async_copy(diff_ref, num_ref.at[0], sems.at[count]))
    reads.append(pltpu.make_async_copy(adv_ref, num_ref.at[1], sems.at[count + 1]))
    for copy in reads[count:] + reads[:count]:
        copy.start()
    reads[count].wait()
    reads[count + 1].wait()
    diffusion = num_ref[0:1][None]
    advection = num_ref[1:2][None]
    writes = []
    for i, part in enumerate(pieces):
        reads[i].wait()
        x = jnp.swapaxes(held_ref[part], 0, 1)
        edge_ref[0, :, part] = x[:2]
        edge_ref[1, :, part] = x[columns - 2 :]
        x = x[quarter - 2 : columns - quarter + 2]
        x = stencil(stencil(x, diffusion, advection), diffusion, advection)
        place_blocks(made_ref, place_ref[0], x, part)
        copy = pltpu.make_async_copy(made_ref.at[:, :, :, part], out_ref.at[:, :, :, part], sems.at[count + 2 + i])
        copy.start()
        writes.append(copy)
    odd = place_ref[1] & 1
    for i, ref in enumerate((first_ref, second_ref)):
        copy = pltpu.make_async_copy(edge_ref.at[odd if i else 1 - odd], ref, sems.at[2 * count + 2 + i])
        copy.start()
        writes.append(copy)
    for copy in writes:
        copy.wait()


def outer_kernel(place_ref, obs_ref, state_ref, first_ref, second_ref, out_ref, turned_ref):
    members, columns, _ = state_ref.shape
    quarter = columns // 4
    odd = place_ref[1] & 1
    turned_ref[2 : columns + 2] = jnp.swapaxes(state_ref[...], 0, 1)
    turned_ref[pl.ds((columns + 2) * (1 - odd), 2)] = first_ref[...]
    turned_ref[pl.ds((columns + 2) * odd, 2)] = second_ref[...]
    diffusion = obs_ref[0, 2:3][None]
    advection = obs_ref[0, 3:4][None]
    low = turned_ref[: quarter + 4]
    high = turned_ref[columns - quarter :]
    low = stencil(stencil(low, diffusion, advection), diffusion, advection)
    high = stencil(stencil(high, diffusion, advection), diffusion, advection)
    place_blocks(out_ref, place_ref[0], jnp.concatenate([low, high], axis=0), pl.ds(0, members))


def join_kernel(me_ref, *refs):
    *outer, inner_ref, out_ref, turned_ref, made_ref, sems = refs
    members, columns, entries = out_ref.shape
    groups, half, _, _ = inner_ref.shape
    quarter = columns // 4
    writes = []
    for i, part in enumerate(pieces_of(members)):
        for (step, other), block in zip(issue_order(groups // 2), outer):
            place = source(me_ref[0], step, other, groups // 2) * half
            turned_ref[pl.ds(outer_start(place, quarter), half), part] = block[:, part]
        turned_ref[quarter : columns - quarter, part] = inner_ref[:, :, part].reshape(groups * half, part.size, entries)
        made_ref[part] = jnp.swapaxes(turned_ref[:, part], 0, 1)
        copy = pltpu.make_async_copy(made_ref.at[part], out_ref.at[part], sems.at[i])
        copy.start()
        writes.append(copy)
    for copy in writes:
        copy.wait()


def observe_kernel(me_ref, count_ref, where_ref, value_ref, rinv_ref, diff_ref, adv_ref, out_ref):
    columns, _, entries = out_ref.shape
    half = columns // 2
    quarter = where_ref.shape[0] // 4
    slots = where_ref.shape[1]
    place = me_ref[0] * half
    slot = lax.broadcasted_iota(jnp.int32, (1, slots), 1)
    row = lax.broadcasted_iota(jnp.int32, (16, slots), 0)
    entry = lax.broadcasted_iota(jnp.int32, (entries, slots), 0)
    for c in range(columns):
        at = inner_start(place, quarter) + c if c < half else outer_start(place, quarter) + c - half
        weight = jnp.where(slot < count_ref[0, at], rinv_ref[pl.ds(at, 1), :], 0.0)
        lhs = jnp.zeros((16, slots), jnp.float32)
        for first, source in ((0, weight), (3, weight * value_ref[pl.ds(at, 1), :])):
            for k, part in enumerate(split(source, 3)):
                lhs = jnp.where(row == first + k, part.astype(jnp.float32), lhs)
        onehot = (entry == where_ref[pl.ds(at, 1), :]).astype(jnp.float32).astype(jnp.bfloat16)
        sums = lax.dot_general(
            lhs.astype(jnp.bfloat16), onehot, (((1,), (1,)), ((), ())), preferred_element_type=jnp.float32
        )
        out_ref[c, 0:1] = sums[0:1] + (sums[1:2] + sums[2:3])
        out_ref[c, 1:2] = sums[3:4] + (sums[4:5] + sums[5:6])
    out_ref[0, 2:3] = diff_ref[...]
    out_ref[0, 3:4] = adv_ref[...]


def analyse_kernel(first, after_ref, obs_ref, states, outs, done_ref, root, mixed, ahead, s, p, u, t, r, w):
    del after_ref
    done_ref[...] = jnp.zeros_like(done_ref)
    groups = len(outs)
    columns, local, entries = outs[0].shape
    members = groups * local
    spread = members - 1.0
    every = range(columns)
    parts = [(c, pl.ds(half, members // 2)) for c in every for half in (0, members // 2)]
    rows = lax.broadcasted_iota(jnp.int32, (members, members), 0)
    cols = lax.broadcasted_iota(jnp.int32, (members, members), 1)
    means, forces, scales, grams = [], [], [], []
    for c in every:
        x = jnp.concatenate([ref[c] for ref in states], axis=0)
        mean = jnp.sum(x, axis=0, keepdims=True) * (1.0 / members)
        anomaly = x - mean
        total = obs_ref[first + c, 0:1]
        forces.append(obs_ref[first + c, 1:2] - total * mean)
        means.append(mean)
        grams.append(square_by_rows(split(anomaly * jnp.sqrt(total), 3)))
        ahead[c] = anomaly
        store(w.at[0], c, slice(None), anomaly)
    for c in every:
        gram = grams[c] + jnp.where(rows == cols, spread, 0.0)
        norm = jnp.sum(jnp.sum(gram * gram, axis=0, keepdims=True), axis=1, keepdims=True)
        scales.append(jnp.sqrt(norm))
        gram = gram * (1.0 / scales[c])
        root[c] = gram
        store(s, c, slice(None), gram)

    def advance(step):
        for c, rows in parts:
            x = 2.25 * ahead[c, rows] + multiply(r.at[step % 2], w.at[step % 2], c, rows)
            ahead[c, rows] = x
            if step < PAIRS - 1:
                store(w.at[(step + 1) % 2], c, rows, x)

    for step in range(PAIRS):
        for c, rows in parts:
            x = multiply(s, s, c, rows)
            y = root[c, rows]
            store(p, c, rows, x)
            store(u, c, rows, 0.0625 * x - 0.5625 * y)
            mixed[c, rows] = 1.6875 * x - 2.4375 * y
        if step > 0:
            advance(step - 1)
        for c, rows in parts:
            store(r.at[step % 2], c, rows, mixed[c, rows] + multiply(u, p, c, rows))
        if step < PAIRS - 1:
            for c, rows in parts:
                x = 2.25 * root[c, rows] + multiply(r.at[step % 2], s, c, rows)
                store(t, c, rows, x)
                mixed[c, rows] = 2.25 * x
            for c, rows in parts:
                x = mixed[c, rows] + multiply(t, r.at[step % 2], c, rows)
                root[c, rows] = x
                store(s, c, rows, x)
    advance(PAIRS - 1)
    for c in every:
        x = ahead[c]
        inner = jnp.sum(x * forces[c], axis=1, keepdims=True)
        shift = jnp.sum(x * inner, axis=0, keepdims=True) / scales[c]
        result = means[c] + shift + x * jnp.sqrt(spread / scales[c])
        for k in range(groups):
            outs[k][c] = result[k * local : (k + 1) * local]


def analyse(states, obs, first, place, after, apart):
    same, swapped = states
    chips, _, columns, local, entries = same.shape
    members = 2 * chips * local
    block = jax.ShapeDtypeStruct((columns, local, entries), jnp.float32)
    whole = jax.ShapeDtypeStruct((2 * chips, columns, local, entries), jnp.float32)
    token = jax.ShapeDtypeStruct(after.shape, jnp.float32)
    full = pltpu.VMEM((columns, members, members), jnp.float32)
    pair = pltpu.VMEM((2, columns, members, members), jnp.bfloat16)
    two = pltpu.VMEM((2, 2, columns, members, members), jnp.bfloat16)
    ahead = pltpu.VMEM((columns, members, entries), jnp.float32)
    factor = pltpu.VMEM((2, 2, columns, members, entries), jnp.bfloat16)

    def kernel(place_ref, after_ref, obs_ref, same_ref, swapped_ref, *refs):
        *outs, done_ref = refs[:-SCRATCH]
        targets = [target(place_ref[0], step, other, chips) for step, other in issue_order(chips)]
        ins = [
            swapped_ref.at[device // 2] if other else same_ref.at[device // 2, 0]
            for device, (_, other) in zip(targets, issue_order(chips))
        ]
        if not apart:
            outs = [outs[0].at[device] for device in targets]
        analyse_kernel(first, after_ref, obs_ref, ins, outs, done_ref, *refs[-SCRATCH:])

    return call(
        kernel,
        [block] * (2 * chips) + [token] if apart else [whole, token],
        columns * 90 * 2 * members * members * entries,
        8 * columns * members * entries,
        in_specs=[SMEM] + [VMEM] * 4,
        scratch_shapes=[full, full, ahead, pair, pair, pair, pair, two, factor],
    )(place, after, obs, same, swapped)


def body(background, diffusion, advection, obs_where, obs_count, obs_value, obs_rinv):
    local, columns, entries = background.shape
    groups = lax.axis_size("mem")
    tiles = lax.axis_size("tile")
    half = columns // groups // 2
    size = background.size
    edge = jax.ShapeDtypeStruct((2, local, entries), jnp.float32)
    blocks = (groups // 2, 2, half, local, entries)
    place = jnp.stack([lax.axis_index("mem"), lax.axis_index("tile")]).astype(jnp.int32)
    pieces = len(pieces_of(local))

    inner, first, second = call(
        inner_kernel,
        [jax.ShapeDtypeStruct(blocks, jnp.float32), edge, edge],
        20 * size,
        8 * size,
        vmem=60 * MIB,
        in_specs=[SMEM, HBM, HBM, HBM],
        out_specs=[HBM, HBM, HBM],
        scratch_shapes=[
            pltpu.VMEM(background.shape, jnp.float32),
            pltpu.VMEM((8, entries), jnp.float32),
            pltpu.VMEM((2, 2, local, entries), jnp.float32),
            pltpu.VMEM(blocks, jnp.float32),
            pltpu.SemaphoreType.DMA((2 * pieces + 4,)),
        ],
    )(place, background, diffusion, advection)
    inner = gather(inner)
    ring = [(i, (i + 1) % tiles) for i in range(tiles)]
    first = lax.ppermute(first, "tile", [pair for i, j in ring[::2] for pair in ((i, j), (j, i))])
    second = lax.ppermute(second, "tile", [pair for i, j in ring[1::2] for pair in ((i, j), (j, i))])
    obs = call(
        observe_kernel,
        jax.ShapeDtypeStruct((2 * half, 8, entries), jnp.float32),
        2 * half * 2 * 16 * obs_where.shape[2] * entries,
        12 * obs_where.size,
        in_specs=[SMEM, SMEM] + [VMEM] * 5,
    )(place, obs_count, obs_where[0], obs_value[0], obs_rinv[0], diffusion[None], advection[None])
    outer = call(
        outer_kernel,
        jax.ShapeDtypeStruct(blocks, jnp.float32),
        20 * size,
        8 * size,
        in_specs=[SMEM] + [VMEM] * 4,
        scratch_shapes=[pltpu.VMEM((columns + 4, local, entries), jnp.float32)],
    )(place, obs, background, first, second)
    outer = gather(outer)

    inner, done = analyse(inner, obs, 0, place, obs[0], False)
    inner = lax.all_to_all(inner, "mem", split_axis=0, concat_axis=0, tiled=True)
    *outer, _ = analyse(outer, obs, half, place, done, True)
    outer = exchange(outer)
    return call(
        join_kernel,
        jax.ShapeDtypeStruct(background.shape, jnp.float32),
        size,
        8 * size,
        in_specs=[SMEM] + [VMEM] * (groups + 1),
        out_specs=HBM,
        scratch_shapes=[
            pltpu.VMEM((columns, local, entries), jnp.float32),
            pltpu.VMEM(background.shape, jnp.float32),
            pltpu.SemaphoreType.DMA((pieces,)),
        ],
    )(place, *outer, inner)


def solution(mesh):
    return jax.shard_map(
        body,
        mesh=mesh,
        in_specs=(
            P("mem", "tile", None),
            P(),
            P(),
            P("tile", None, None),
            P("tile", None),
            P("tile", None, None),
            P("tile", None, None),
        ),
        out_specs=P("mem", "tile", None),
        check_vma=False,
    )
```

```python
import jax
import jax.numpy as jnp
from jax import lax
from jax.experimental import pallas as pl
from jax.experimental.pallas import tpu as pltpu
from jax.sharding import PartitionSpec as P

PAIRS = 6
SCRATCH = 9
MIB = 1024 * 1024
SMEM = pl.BlockSpec(memory_space=pltpu.SMEM)
VMEM = pl.BlockSpec(memory_space=pltpu.VMEM)
HBM = pl.BlockSpec(memory_space=pltpu.HBM)


def call(kernel, out_shape, flops, moved, vmem=48 * MIB, **options):
    return pl.pallas_call(
        kernel,
        out_shape=out_shape,
        compiler_params=pltpu.CompilerParams(vmem_limit_bytes=vmem),
        cost_estimate=pl.CostEstimate(flops=flops, bytes_accessed=moved, transcendentals=0),
        **options,
    )


def target(me, k, groups):
    if groups & (groups - 1) == 0:
        return me ^ k
    return lax.rem(me + k, groups)


def source(me, k, groups):
    if groups & (groups - 1) == 0:
        return me ^ k
    return lax.rem(me + groups - k, groups)


def issue_order(groups):
    return sorted(range(1, groups), key=lambda k: (k != 1, -(k // 2).bit_count(), k)) + [0]


def exchange(blocks):
    groups = len(blocks)
    out = []
    for k in issue_order(groups):
        pairs = [(i, i ^ k if groups & (groups - 1) == 0 else (i + k) % groups) for i in range(groups)]
        out.append(lax.ppermute(blocks[k], "mem", pairs) if k else blocks[0])
    return out


def split(x, parts):
    out = []
    for _ in range(parts):
        part = x.astype(jnp.bfloat16)
        out.append(part)
        x = x - part.astype(jnp.float32)
    return out


def store(ref, c, rows, x):
    for i, part in enumerate(split(x, 2)):
        ref[i, c, rows] = part


def multiply(a_ref, b_ref, c, rows):
    lhs = jnp.concatenate([a_ref[0, c, rows], a_ref[1, c, rows], a_ref[0, c, rows]], axis=1)
    rhs = jnp.concatenate([b_ref[0, c], b_ref[0, c], b_ref[1, c]], axis=0)
    return jnp.dot(lhs, rhs, preferred_element_type=jnp.float32)


def square_by_rows(x):
    a, b = split(x, 3), split(x.T, 3)
    lhs = jnp.concatenate([a[2], a[0], a[1], a[1], a[0], a[0]], axis=1)
    rhs = jnp.concatenate([b[0], b[2], b[1], b[0], b[1], b[0]], axis=0)
    middle = lhs.shape[0] // 2
    upper = jnp.dot(lhs[:middle], rhs, preferred_element_type=jnp.float32)
    lower = jnp.dot(lhs[middle:], rhs, preferred_element_type=jnp.float32)
    return jnp.concatenate([upper, lower], axis=0)


def stencil(padded, diffusion, advection):
    middle = padded[1:-1]
    left = padded[:-2]
    right = padded[2:]
    return middle + diffusion * (left - 2.0 * middle + right) + advection * (0.5 * (left - right))


def inner_start(place, quarter):
    return place + quarter


def outer_start(place, quarter):
    return jnp.where(place < quarter, place, place + 2 * quarter)


def pieces_of(members):
    rows = 8 if members % 8 == 0 else members
    return [pl.ds(first, rows) for first in range(0, members, rows)]


def inner_kernel(state_ref, diff_ref, adv_ref, out_ref, low_ref, high_ref, held_ref, num_ref, sems):
    members, columns, entries = state_ref.shape
    groups, half, _, _ = out_ref.shape
    quarter = columns // 4
    pieces = pieces_of(members)
    count = len(pieces)
    reads = [pltpu.make_async_copy(state_ref.at[part], held_ref.at[part], sems.at[i]) for i, part in enumerate(pieces)]
    reads.append(pltpu.make_async_copy(diff_ref, num_ref.at[0], sems.at[count]))
    reads.append(pltpu.make_async_copy(adv_ref, num_ref.at[1], sems.at[count + 1]))
    for copy in reads[count:] + reads[:count]:
        copy.start()
    reads[count].wait()
    reads[count + 1].wait()
    diffusion = num_ref[0:1][None]
    advection = num_ref[1:2][None]
    for i, part in enumerate(pieces):
        reads[i].wait()
        x = jnp.swapaxes(held_ref[part], 0, 1)
        low_ref[:, part] = x[:2]
        high_ref[:, part] = x[columns - 2 :]
        x = x[quarter - 2 : columns - quarter + 2]
        x = stencil(stencil(x, diffusion, advection), diffusion, advection)
        out_ref[:, :, part] = x.reshape(groups, half, part.size, entries)


def outer_kernel(obs_ref, state_ref, before_ref, after_ref, diff_ref, adv_ref, out_ref, turned_ref):
    del obs_ref
    columns = state_ref.shape[1]
    quarter = columns // 4
    turned_ref[2 : columns + 2] = jnp.swapaxes(state_ref[...], 0, 1)
    turned_ref[:2] = before_ref[...]
    turned_ref[columns + 2 :] = after_ref[...]
    diffusion = diff_ref[...][None]
    advection = adv_ref[...][None]
    low = turned_ref[: quarter + 4]
    high = turned_ref[columns - quarter :]
    low = stencil(stencil(low, diffusion, advection), diffusion, advection)
    high = stencil(stencil(high, diffusion, advection), diffusion, advection)
    out_ref[...] = jnp.concatenate([low, high], axis=0).reshape(out_ref.shape)


def inner_join_kernel(after_ref, inner_ref, out_ref, made_ref, sems):
    del after_ref
    members, columns, entries = out_ref.shape
    groups, half, _, _ = inner_ref.shape
    quarter = columns // 4
    writes = []
    for i, part in enumerate(pieces_of(members)):
        x = inner_ref[:, :, part].reshape(groups * half, part.size, entries)
        made_ref[part] = jnp.swapaxes(x, 0, 1)
        copy = pltpu.make_async_copy(
            made_ref.at[part], out_ref.at[part, pl.ds(quarter, columns - 2 * quarter)], sems.at[i]
        )
        copy.start()
        writes.append(copy)
    for copy in writes:
        copy.wait()


def outer_join_kernel(me_ref, held_ref, *refs):
    del held_ref
    *outer, out_ref, turned_ref, made_ref, sems = refs
    members, columns, _ = out_ref.shape
    groups = len(outer)
    half = outer[0].shape[0]
    quarter = columns // 4
    writes = []
    for i, part in enumerate(pieces_of(members)):
        for k, block in zip(issue_order(groups), outer):
            turned_ref[pl.ds(source(me_ref[0], k, groups) * half, half), part] = block[:, part]
        made_ref[part] = jnp.swapaxes(turned_ref[:, part], 0, 1)
        for side in range(2):
            copy = pltpu.make_async_copy(
                made_ref.at[part, pl.ds(side * quarter, quarter)],
                out_ref.at[part, pl.ds(side * (columns - quarter), quarter)],
                sems.at[2 * i + side],
            )
            copy.start()
            writes.append(copy)
    for copy in writes:
        copy.wait()


def observe_kernel(me_ref, count_ref, where_ref, value_ref, rinv_ref, out_ref):
    columns, _, entries = out_ref.shape
    half = columns // 2
    quarter = where_ref.shape[0] // 4
    slots = where_ref.shape[1]
    place = me_ref[0] * half
    slot = lax.broadcasted_iota(jnp.int32, (1, slots), 1)
    row = lax.broadcasted_iota(jnp.int32, (16, slots), 0)
    entry = lax.broadcasted_iota(jnp.int32, (entries, slots), 0)
    for c in range(columns):
        at = inner_start(place, quarter) + c if c < half else outer_start(place, quarter) + c - half
        weight = jnp.where(slot < count_ref[0, at], rinv_ref[pl.ds(at, 1), :], 0.0)
        lhs = jnp.zeros((16, slots), jnp.float32)
        for first, source in ((0, weight), (3, weight * value_ref[pl.ds(at, 1), :])):
            for k, part in enumerate(split(source, 3)):
                lhs = jnp.where(row == first + k, part.astype(jnp.float32), lhs)
        onehot = (entry == where_ref[pl.ds(at, 1), :]).astype(jnp.float32).astype(jnp.bfloat16)
        sums = lax.dot_general(
            lhs.astype(jnp.bfloat16), onehot, (((1,), (1,)), ((), ())), preferred_element_type=jnp.float32
        )
        out_ref[c, 0:1] = sums[0:1] + (sums[1:2] + sums[2:3])
        out_ref[c, 1:2] = sums[3:4] + (sums[4:5] + sums[5:6])


def analyse_kernel(first, after_ref, obs_ref, states, outs, done_ref, root, mixed, ahead, s, p, u, t, r, w):
    del after_ref
    done_ref[...] = jnp.zeros_like(done_ref)
    groups = len(outs)
    columns, local, entries = outs[0].shape
    members = groups * local
    spread = members - 1.0
    every = range(columns)
    parts = [(c, pl.ds(half, members // 2)) for c in every for half in (0, members // 2)]
    rows = lax.broadcasted_iota(jnp.int32, (members, members), 0)
    cols = lax.broadcasted_iota(jnp.int32, (members, members), 1)
    means, forces, scales, grams = [], [], [], []
    for c in every:
        x = jnp.concatenate([ref[c] for ref in states], axis=0)
        mean = jnp.sum(x, axis=0, keepdims=True) * (1.0 / members)
        anomaly = x - mean
        total = obs_ref[first + c, 0:1]
        forces.append(obs_ref[first + c, 1:2] - total * mean)
        means.append(mean)
        grams.append(square_by_rows(anomaly * jnp.sqrt(total)))
        ahead[c] = anomaly
        store(w.at[0], c, slice(None), anomaly)
    for c in every:
        gram = grams[c] + jnp.where(rows == cols, spread, 0.0)
        norm = jnp.sum(jnp.sum(gram * gram, axis=0, keepdims=True), axis=1, keepdims=True)
        scales.append(jnp.sqrt(norm))
        gram = gram * (1.0 / scales[c])
        root[c] = gram
        store(s, c, slice(None), gram)

    def advance(step):
        for c, rows in parts:
            x = 2.25 * ahead[c, rows] + multiply(r.at[step % 2], w.at[step % 2], c, rows)
            ahead[c, rows] = x
            if step < PAIRS - 1:
                store(w.at[(step + 1) % 2], c, rows, x)

    for step in range(PAIRS):
        for c, rows in parts:
            x = multiply(s, s, c, rows)
            y = root[c, rows]
            store(p, c, rows, x)
            store(u, c, rows, 0.0625 * x - 0.5625 * y)
            mixed[c, rows] = 1.6875 * x - 2.4375 * y
        if step > 0:
            advance(step - 1)
        for c, rows in parts:
            store(r.at[step % 2], c, rows, mixed[c, rows] + multiply(u, p, c, rows))
        if step < PAIRS - 1:
            for c, rows in parts:
                x = 2.25 * root[c, rows] + multiply(r.at[step % 2], s, c, rows)
                store(t, c, rows, x)
                mixed[c, rows] = 2.25 * x
            for c, rows in parts:
                x = mixed[c, rows] + multiply(t, r.at[step % 2], c, rows)
                root[c, rows] = x
                store(s, c, rows, x)
    advance(PAIRS - 1)
    for c in every:
        x = ahead[c]
        inner = jnp.sum(x * forces[c], axis=1, keepdims=True)
        shift = jnp.sum(x * inner, axis=0, keepdims=True) / scales[c]
        result = means[c] + shift + x * jnp.sqrt(spread / scales[c])
        for k in range(groups):
            outs[k][c] = result[k * local : (k + 1) * local]


def analyse(states, obs, first, me, after, apart):
    groups, columns, local, entries = states.shape
    members = groups * local
    block = jax.ShapeDtypeStruct((columns, local, entries), jnp.float32)
    whole = jax.ShapeDtypeStruct(states.shape, jnp.float32)
    token = jax.ShapeDtypeStruct(after.shape, jnp.float32)
    full = pltpu.VMEM((columns, members, members), jnp.float32)
    pair = pltpu.VMEM((2, columns, members, members), jnp.bfloat16)
    two = pltpu.VMEM((2, 2, columns, members, members), jnp.bfloat16)
    ahead = pltpu.VMEM((columns, members, entries), jnp.float32)
    factor = pltpu.VMEM((2, 2, columns, members, entries), jnp.bfloat16)

    def kernel(me_ref, after_ref, obs_ref, states_ref, *refs):
        *outs, done_ref = refs[:-SCRATCH]
        scratch = refs[-SCRATCH:]
        if apart:
            ins = [states_ref.at[target(me_ref[0], k, groups)] for k in range(groups)]
        else:
            ins = [states_ref.at[k] for k in range(groups)]
            outs = [outs[0].at[k] for k in range(groups)]
        analyse_kernel(first, after_ref, obs_ref, ins, outs, done_ref, *scratch)

    return call(
        kernel,
        [block] * groups + [token] if apart else [whole, token],
        columns * 90 * 2 * members * members * entries,
        8 * columns * members * entries,
        in_specs=[SMEM] + [VMEM] * 3,
        scratch_shapes=[full, full, ahead, pair, pair, pair, pair, two, factor],
    )(me, after, obs, states)


def body(background, diffusion, advection, obs_where, obs_count, obs_value, obs_rinv):
    local, columns, entries = background.shape
    groups = lax.axis_size("mem")
    tiles = lax.axis_size("tile")
    half = columns // groups // 2
    size = background.size
    block = (half, local, entries)
    edge = jax.ShapeDtypeStruct((2, local, entries), jnp.float32)
    me = lax.axis_index("mem")[None].astype(jnp.int32)
    pieces = len(pieces_of(local))

    inner, low, high = call(
        inner_kernel,
        [jax.ShapeDtypeStruct((groups, *block), jnp.float32), edge, edge],
        20 * size,
        8 * size,
        in_specs=[HBM] * 3,
        scratch_shapes=[
            pltpu.VMEM(background.shape, jnp.float32),
            pltpu.VMEM((8, entries), jnp.float32),
            pltpu.SemaphoreType.DMA((pieces + 2,)),
        ],
    )(*(pltpu.with_memory_space_constraint(x, pltpu.HBM) for x in (background, diffusion, advection)))
    inner = lax.all_to_all(inner, "mem", split_axis=0, concat_axis=0, tiled=True)
    before = lax.ppermute(high, "tile", [(i, (i + 1) % tiles) for i in range(tiles)])
    after = lax.ppermute(low, "tile", [((i + 1) % tiles, i) for i in range(tiles)])
    obs = call(
        observe_kernel,
        jax.ShapeDtypeStruct((2 * half, 8, entries), jnp.float32),
        2 * half * 2 * 16 * obs_where.shape[2] * entries,
        12 * obs_where.size,
        in_specs=[SMEM, SMEM] + [VMEM] * 3,
    )(me, obs_count, obs_where[0], obs_value[0], obs_rinv[0])
    outer = call(
        outer_kernel,
        jax.ShapeDtypeStruct((groups, *block), jnp.float32),
        20 * size,
        8 * size,
        in_specs=[VMEM] * 6,
        scratch_shapes=[pltpu.VMEM((columns + 4, local, entries), jnp.float32)],
    )(obs, background, before, after, diffusion[None], advection[None])
    outer = lax.all_to_all(outer, "mem", split_axis=0, concat_axis=0, tiled=True)

    inner, done = analyse(inner, obs, 0, me, obs[0], False)
    inner = lax.all_to_all(inner, "mem", split_axis=0, concat_axis=0, tiled=True)
    *outer, _ = analyse(outer, obs, half, me, done, True)
    outer = exchange(outer)
    result = jax.ShapeDtypeStruct(background.shape, jnp.float32)
    made = call(
        inner_join_kernel,
        result,
        size,
        4 * size,
        in_specs=[VMEM, VMEM],
        out_specs=HBM,
        scratch_shapes=[
            pltpu.VMEM((local, groups * half, entries), jnp.float32),
            pltpu.SemaphoreType.DMA((pieces,)),
        ],
    )(outer[2], inner)
    return call(
        outer_join_kernel,
        result,
        size,
        4 * size,
        in_specs=[SMEM, HBM] + [VMEM] * groups,
        out_specs=HBM,
        scratch_shapes=[
            pltpu.VMEM((groups * half, local, entries), jnp.float32),
            pltpu.VMEM((local, groups * half, entries), jnp.float32),
            pltpu.SemaphoreType.DMA((2 * pieces,)),
        ],
        input_output_aliases={1: 0},
    )(me, made, *outer)


def solution(mesh):
    return jax.shard_map(
        body,
        mesh=mesh,
        in_specs=(
            P("mem", "tile", None),
            P(),
            P(),
            P("tile", None, None),
            P("tile", None),
            P("tile", None, None),
            P("tile", None, None),
        ),
        out_specs=P("mem", "tile", None),
        check_vma=False,
    )
```

```python
import jax
import jax.numpy as jnp
from jax import lax
from jax.experimental import pallas as pl
from jax.experimental.pallas import tpu as pltpu
from jax.sharding import PartitionSpec as P

PAIRS = 6
SCRATCH = 9
MIB = 1024 * 1024
SMEM = pl.BlockSpec(memory_space=pltpu.SMEM)
VMEM = pl.BlockSpec(memory_space=pltpu.VMEM)
HBM = pl.BlockSpec(memory_space=pltpu.HBM)


def call(kernel, out_shape, flops, moved, vmem=48 * MIB, **options):
    return pl.pallas_call(
        kernel,
        out_shape=out_shape,
        compiler_params=pltpu.CompilerParams(vmem_limit_bytes=vmem),
        cost_estimate=pl.CostEstimate(flops=flops, bytes_accessed=moved, transcendentals=0),
        **options,
    )


def target(me, k, groups):
    if groups & (groups - 1) == 0:
        return me ^ k
    return lax.rem(me + k, groups)


def source(me, k, groups):
    if groups & (groups - 1) == 0:
        return me ^ k
    return lax.rem(me + groups - k, groups)


def issue_order(groups):
    return sorted(range(1, groups), key=lambda k: (k != 1, -(k // 2).bit_count(), k)) + [0]


def exchange(blocks):
    groups = len(blocks)
    out = []
    for k in issue_order(groups):
        pairs = [(i, i ^ k if groups & (groups - 1) == 0 else (i + k) % groups) for i in range(groups)]
        out.append(lax.ppermute(blocks[k], "mem", pairs) if k else blocks[0])
    return out


def split(x, parts):
    out = []
    for _ in range(parts):
        part = x.astype(jnp.bfloat16)
        out.append(part)
        x = x - part.astype(jnp.float32)
    return out


def store(ref, c, rows, x):
    for i, part in enumerate(split(x, 2)):
        ref[i, c, rows] = part


def multiply(a_ref, b_ref, c, rows):
    lhs = jnp.concatenate([a_ref[0, c, rows], a_ref[1, c, rows], a_ref[0, c, rows]], axis=1)
    rhs = jnp.concatenate([b_ref[0, c], b_ref[0, c], b_ref[1, c]], axis=0)
    return jnp.dot(lhs, rhs, preferred_element_type=jnp.float32)


def square_by_rows(x):
    p0, p1, p2 = split(x, 3)
    lhs = jnp.concatenate([p2, p0, p1, p1, p0, p0], axis=1)
    rhs = jnp.concatenate([p0, p2, p1, p0, p1, p0], axis=1)
    middle = lhs.shape[0] // 2
    dims = (((1,), (1,)), ((), ()))
    upper = lax.dot_general(lhs[:middle], rhs, dims, preferred_element_type=jnp.float32)
    lower = lax.dot_general(lhs[middle:], rhs, dims, preferred_element_type=jnp.float32)
    return jnp.concatenate([upper, lower], axis=0)


def stencil(padded, diffusion, advection):
    middle = padded[1:-1]
    left = padded[:-2]
    right = padded[2:]
    return middle + diffusion * (left - 2.0 * middle + right) + advection * (0.5 * (left - right))


def inner_start(place, quarter):
    return place + quarter


def outer_start(place, quarter):
    return jnp.where(place < quarter, place, place + 2 * quarter)


def pieces_of(members):
    rows = 8 if members % 8 == 0 else members
    return [pl.ds(first, rows) for first in range(0, members, rows)]


def inner_kernel(state_ref, diff_ref, adv_ref, out_ref, rest_ref, low_ref, high_ref, held_ref, num_ref, sems):
    members, columns, entries = state_ref.shape
    groups, half, _, _ = out_ref.shape
    quarter = columns // 4
    pieces = pieces_of(members)
    count = len(pieces)
    reads = [pltpu.make_async_copy(state_ref.at[part], held_ref.at[part], sems.at[i]) for i, part in enumerate(pieces)]
    reads.append(pltpu.make_async_copy(diff_ref, num_ref.at[0], sems.at[count]))
    reads.append(pltpu.make_async_copy(adv_ref, num_ref.at[1], sems.at[count + 1]))
    for copy in reads[count:] + reads[:count]:
        copy.start()
    reads[count].wait()
    reads[count + 1].wait()
    diffusion = num_ref[0:1][None]
    advection = num_ref[1:2][None]
    for i, part in enumerate(pieces):
        reads[i].wait()
        x = jnp.swapaxes(held_ref[part], 0, 1)
        low_ref[:, part] = x[:2]
        high_ref[:, part] = x[columns - 2 :]
        rest_ref[0, :, part] = x[: quarter + 2]
        rest_ref[1, :, part] = x[columns - quarter - 2 :]
        x = x[quarter - 2 : columns - quarter + 2]
        x = stencil(stencil(x, diffusion, advection), diffusion, advection)
        out_ref[:, :, part] = x.reshape(groups, half, part.size, entries)


def outer_kernel(obs_ref, rest_ref, before_ref, after_ref, diff_ref, adv_ref, out_ref):
    del obs_ref
    diffusion = diff_ref[...][None]
    advection = adv_ref[...][None]
    low = jnp.concatenate([before_ref[...], rest_ref[0]], axis=0)
    high = jnp.concatenate([rest_ref[1], after_ref[...]], axis=0)
    low = stencil(stencil(low, diffusion, advection), diffusion, advection)
    high = stencil(stencil(high, diffusion, advection), diffusion, advection)
    out_ref[...] = jnp.concatenate([low, high], axis=0).reshape(out_ref.shape)


def inner_join_kernel(after_ref, inner_ref, out_ref, made_ref, sems):
    del after_ref
    members, columns, entries = out_ref.shape
    groups, half, _, _ = inner_ref.shape
    quarter = columns // 4
    writes = []
    for i, part in enumerate(pieces_of(members)):
        x = inner_ref[:, :, part].reshape(groups * half, part.size, entries)
        made_ref[part] = jnp.swapaxes(x, 0, 1)
        copy = pltpu.make_async_copy(
            made_ref.at[part], out_ref.at[part, pl.ds(quarter, columns - 2 * quarter)], sems.at[i]
        )
        copy.start()
        writes.append(copy)
    for copy in writes:
        copy.wait()


def outer_join_kernel(me_ref, held_ref, *refs):
    del held_ref
    *outer, out_ref, turned_ref, made_ref, sems = refs
    members, columns, _ = out_ref.shape
    groups = len(outer)
    half = outer[0].shape[0]
    quarter = columns // 4
    writes = []
    for i, part in enumerate(pieces_of(members)):
        for k, block in zip(issue_order(groups), outer):
            turned_ref[pl.ds(source(me_ref[0], k, groups) * half, half), part] = block[:, part]
        made_ref[part] = jnp.swapaxes(turned_ref[:, part], 0, 1)
        for side in range(2):
            copy = pltpu.make_async_copy(
                made_ref.at[part, pl.ds(side * quarter, quarter)],
                out_ref.at[part, pl.ds(side * (columns - quarter), quarter)],
                sems.at[2 * i + side],
            )
            copy.start()
            writes.append(copy)
    for copy in writes:
        copy.wait()


def observe_kernel(me_ref, count_ref, where_ref, value_ref, rinv_ref, out_ref):
    columns, _, entries = out_ref.shape
    half = columns // 2
    quarter = where_ref.shape[0] // 4
    slots = where_ref.shape[1]
    place = me_ref[0] * half
    slot = lax.broadcasted_iota(jnp.int32, (1, slots), 1)
    row = lax.broadcasted_iota(jnp.int32, (16, slots), 0)
    entry = lax.broadcasted_iota(jnp.int32, (entries, slots), 0)
    for c in range(columns):
        at = inner_start(place, quarter) + c if c < half else outer_start(place, quarter) + c - half
        weight = jnp.where(slot < count_ref[0, at], rinv_ref[pl.ds(at, 1), :], 0.0)
        lhs = jnp.zeros((16, slots), jnp.float32)
        for first, source in ((0, weight), (3, weight * value_ref[pl.ds(at, 1), :])):
            for k, part in enumerate(split(source, 3)):
                lhs = jnp.where(row == first + k, part.astype(jnp.float32), lhs)
        onehot = (entry == where_ref[pl.ds(at, 1), :]).astype(jnp.float32).astype(jnp.bfloat16)
        sums = lax.dot_general(
            lhs.astype(jnp.bfloat16), onehot, (((1,), (1,)), ((), ())), preferred_element_type=jnp.float32
        )
        out_ref[c, 0:1] = sums[0:1] + (sums[1:2] + sums[2:3])
        out_ref[c, 1:2] = sums[3:4] + (sums[4:5] + sums[5:6])


def analyse_kernel(first, after_ref, obs_ref, states, outs, done_ref, root, mixed, ahead, s, p, u, t, r, w):
    del after_ref
    done_ref[...] = jnp.zeros_like(done_ref)
    groups = len(outs)
    columns, local, entries = outs[0].shape
    members = groups * local
    spread = members - 1.0
    every = range(columns)
    parts = [(c, pl.ds(half, members // 2)) for c in every for half in (0, members // 2)]
    rows = lax.broadcasted_iota(jnp.int32, (members, members), 0)
    cols = lax.broadcasted_iota(jnp.int32, (members, members), 1)
    means, forces, scales, grams = [], [], [], []
    for c in every:
        x = jnp.concatenate([ref[c] for ref in states], axis=0)
        mean = jnp.sum(x, axis=0, keepdims=True) * (1.0 / members)
        anomaly = x - mean
        total = obs_ref[first + c, 0:1]
        forces.append(obs_ref[first + c, 1:2] - total * mean)
        means.append(mean)
        grams.append(square_by_rows(anomaly * jnp.sqrt(total)))
        ahead[c] = anomaly
        store(w.at[0], c, slice(None), anomaly)
    for c in every:
        gram = grams[c] + jnp.where(rows == cols, spread, 0.0)
        norm = jnp.sum(jnp.sum(gram * gram, axis=0, keepdims=True), axis=1, keepdims=True)
        scales.append(jnp.sqrt(norm))
        gram = gram * (1.0 / scales[c])
        root[c] = gram
        store(s, c, slice(None), gram)

    def advance(step):
        for c, rows in parts:
            x = 2.25 * ahead[c, rows] + multiply(r.at[step % 2], w.at[step % 2], c, rows)
            ahead[c, rows] = x
            if step < PAIRS - 1:
                store(w.at[(step + 1) % 2], c, rows, x)

    for step in range(PAIRS):
        for c, rows in parts:
            x = multiply(s, s, c, rows)
            y = root[c, rows]
            store(p, c, rows, x)
            store(u, c, rows, 0.0625 * x - 0.5625 * y)
            mixed[c, rows] = 1.6875 * x - 2.4375 * y
        if step > 0:
            advance(step - 1)
        for c, rows in parts:
            store(r.at[step % 2], c, rows, mixed[c, rows] + multiply(u, p, c, rows))
        if step < PAIRS - 1:
            for c, rows in parts:
                x = 2.25 * root[c, rows] + multiply(r.at[step % 2], s, c, rows)
                store(t, c, rows, x)
                mixed[c, rows] = 2.25 * x
            for c, rows in parts:
                x = mixed[c, rows] + multiply(t, r.at[step % 2], c, rows)
                root[c, rows] = x
                store(s, c, rows, x)
    advance(PAIRS - 1)
    for c in every:
        x = ahead[c]
        inner = jnp.sum(x * forces[c], axis=1, keepdims=True)
        shift = jnp.sum(x * inner, axis=0, keepdims=True) / scales[c]
        result = means[c] + shift + x * jnp.sqrt(spread / scales[c])
        for k in range(groups):
            outs[k][c] = result[k * local : (k + 1) * local]


def analyse(states, obs, first, me, after, apart):
    groups, columns, local, entries = states.shape
    members = groups * local
    block = jax.ShapeDtypeStruct((columns, local, entries), jnp.float32)
    whole = jax.ShapeDtypeStruct(states.shape, jnp.float32)
    token = jax.ShapeDtypeStruct(after.shape, jnp.float32)
    full = pltpu.VMEM((columns, members, members), jnp.float32)
    pair = pltpu.VMEM((2, columns, members, members), jnp.bfloat16)
    two = pltpu.VMEM((2, 2, columns, members, members), jnp.bfloat16)
    ahead = pltpu.VMEM((columns, members, entries), jnp.float32)
    factor = pltpu.VMEM((2, 2, columns, members, entries), jnp.bfloat16)

    def kernel(me_ref, after_ref, obs_ref, states_ref, *refs):
        *outs, done_ref = refs[:-SCRATCH]
        scratch = refs[-SCRATCH:]
        if apart:
            ins = [states_ref.at[target(me_ref[0], k, groups)] for k in range(groups)]
        else:
            ins = [states_ref.at[k] for k in range(groups)]
            outs = [outs[0].at[k] for k in range(groups)]
        analyse_kernel(first, after_ref, obs_ref, ins, outs, done_ref, *scratch)

    return call(
        kernel,
        [block] * groups + [token] if apart else [whole, token],
        columns * 90 * 2 * members * members * entries,
        8 * columns * members * entries,
        in_specs=[SMEM] + [VMEM] * 3,
        scratch_shapes=[full, full, ahead, pair, pair, pair, pair, two, factor],
    )(me, after, obs, states)


def body(background, diffusion, advection, obs_where, obs_count, obs_value, obs_rinv):
    local, columns, entries = background.shape
    groups = lax.axis_size("mem")
    tiles = lax.axis_size("tile")
    half = columns // groups // 2
    size = background.size
    block = (half, local, entries)
    rest = jax.ShapeDtypeStruct((2, columns // 4 + 2, local, entries), jnp.float32)
    edge = jax.ShapeDtypeStruct((2, local, entries), jnp.float32)
    me = lax.axis_index("mem")[None].astype(jnp.int32)
    pieces = len(pieces_of(local))

    inner, rest, low, high = call(
        inner_kernel,
        [jax.ShapeDtypeStruct((groups, *block), jnp.float32), rest, edge, edge],
        20 * size,
        8 * size,
        in_specs=[HBM] * 3,
        scratch_shapes=[
            pltpu.VMEM(background.shape, jnp.float32),
            pltpu.VMEM((8, entries), jnp.float32),
            pltpu.SemaphoreType.DMA((pieces + 2,)),
        ],
    )(*(pltpu.with_memory_space_constraint(x, pltpu.HBM) for x in (background, diffusion, advection)))
    inner = lax.all_to_all(inner, "mem", split_axis=0, concat_axis=0, tiled=True)
    before = lax.ppermute(high, "tile", [(i, (i + 1) % tiles) for i in range(tiles)])
    after = lax.ppermute(low, "tile", [((i + 1) % tiles, i) for i in range(tiles)])
    obs = call(
        observe_kernel,
        jax.ShapeDtypeStruct((2 * half, 8, entries), jnp.float32),
        2 * half * 2 * 16 * obs_where.shape[2] * entries,
        12 * obs_where.size,
        in_specs=[SMEM, SMEM] + [VMEM] * 3,
    )(me, obs_count, obs_where[0], obs_value[0], obs_rinv[0])
    outer = call(
        outer_kernel,
        jax.ShapeDtypeStruct((groups, *block), jnp.float32),
        20 * size,
        8 * size,
        in_specs=[VMEM] * 6,
    )(obs, rest, before, after, diffusion[None], advection[None])
    outer = lax.all_to_all(outer, "mem", split_axis=0, concat_axis=0, tiled=True)

    inner, done = analyse(inner, obs, 0, me, obs[0], False)
    inner = lax.all_to_all(inner, "mem", split_axis=0, concat_axis=0, tiled=True)
    *outer, _ = analyse(outer, obs, half, me, done, True)
    outer = exchange(outer)
    result = jax.ShapeDtypeStruct(background.shape, jnp.float32)
    made = call(
        inner_join_kernel,
        result,
        size,
        4 * size,
        in_specs=[VMEM, VMEM],
        out_specs=HBM,
        scratch_shapes=[
            pltpu.VMEM((local, groups * half, entries), jnp.float32),
            pltpu.SemaphoreType.DMA((pieces,)),
        ],
    )(outer[2], inner)
    return call(
        outer_join_kernel,
        result,
        size,
        4 * size,
        in_specs=[SMEM, HBM] + [VMEM] * groups,
        out_specs=HBM,
        scratch_shapes=[
            pltpu.VMEM((groups * half, local, entries), jnp.float32),
            pltpu.VMEM((local, groups * half, entries), jnp.float32),
            pltpu.SemaphoreType.DMA((2 * pieces,)),
        ],
        input_output_aliases={1: 0},
    )(me, made, *outer)


def solution(mesh):
    return jax.shard_map(
        body,
        mesh=mesh,
        in_specs=(
            P("mem", "tile", None),
            P(),
            P(),
            P("tile", None, None),
            P("tile", None),
            P("tile", None, None),
            P("tile", None, None),
        ),
        out_specs=P("mem", "tile", None),
        check_vma=False,
    )
```

```python
import jax
import jax.numpy as jnp
from jax import lax
from jax.experimental import pallas as pl
from jax.experimental.pallas import tpu as pltpu
from jax.sharding import PartitionSpec as P

PAIRS = 6
MIB = 1024 * 1024
SMEM = pl.BlockSpec(memory_space=pltpu.SMEM)
VMEM = pl.BlockSpec(memory_space=pltpu.VMEM)
HBM = pl.BlockSpec(memory_space=pltpu.HBM)


def call(kernel, out_shape, flops, moved, vmem=48 * MIB, **options):
    return pl.pallas_call(
        kernel,
        out_shape=out_shape,
        compiler_params=pltpu.CompilerParams(vmem_limit_bytes=vmem),
        cost_estimate=pl.CostEstimate(flops=flops, bytes_accessed=moved, transcendentals=0),
        **options,
    )


def in_hbm(x):
    return pltpu.with_memory_space_constraint(x, pltpu.HBM)


def target(me, k, groups):
    if groups & (groups - 1) == 0:
        return me ^ k
    return lax.rem(me + k, groups)


def issue_order(groups):
    return sorted(range(1, groups), key=lambda k: (k != 1, -(k // 2).bit_count(), k)) + [0]


def exchange(blocks, back):
    groups = len(blocks)
    out = []
    for k, block in zip(issue_order(groups), blocks):
        pairs = [(i, i ^ k if groups & (groups - 1) == 0 else (i + k) % groups) for i in range(groups)]
        if back:
            pairs = [(j, i) for i, j in pairs]
        out.append(lax.ppermute(block, "mem", pairs) if k else block)
    return out


def split(x, parts):
    out = []
    for _ in range(parts):
        part = x.astype(jnp.bfloat16)
        out.append(part)
        x = x - part.astype(jnp.float32)
    return out


def store(ref, c, rows, x):
    for i, part in enumerate(split(x, 2)):
        ref[i, c, rows] = part


def multiply(a_ref, b_ref, c, rows):
    lhs = jnp.concatenate([a_ref[0, c, rows], a_ref[1, c, rows], a_ref[0, c, rows]], axis=1)
    rhs = jnp.concatenate([b_ref[0, c], b_ref[0, c], b_ref[1, c]], axis=0)
    return jnp.dot(lhs, rhs, preferred_element_type=jnp.float32)


def square_by_rows(parts):
    p0, p1, p2 = parts
    lhs = jnp.concatenate([p2, p0, p1, p1, p0, p0], axis=1)
    rhs = jnp.concatenate([p0, p2, p1, p0, p1, p0], axis=1)
    return lax.dot_general(lhs, rhs, (((1,), (1,)), ((), ())), preferred_element_type=jnp.float32)


def stencil(padded, diffusion, advection):
    middle = padded[1:-1]
    left = padded[:-2]
    right = padded[2:]
    return middle + diffusion * (left - 2.0 * middle + right) + advection * (0.5 * (left - right))


def pieces_of(members):
    rows = 8 if members % 8 == 0 else members
    return [pl.ds(first, rows) for first in range(0, members, rows)]


def edge_kernel(state_ref, low_ref, high_ref, held_ref, sems):
    columns = state_ref.shape[1]
    width = held_ref.shape[2]
    reads = [
        pltpu.make_async_copy(state_ref.at[:, pl.ds(first, width)], held_ref.at[i], sems.at[i])
        for i, first in enumerate((0, columns - width))
    ]
    for copy in reads:
        copy.start()
    reads[0].wait()
    for i in range(2):
        low_ref[i] = held_ref[0, :, i]
    reads[1].wait()
    for i in range(2):
        high_ref[i] = held_ref[1, :, width - 2 + i]


def forecast_kernel(me_ref, state_ref, before_ref, after_ref, diff_ref, adv_ref, *refs):
    *outs, turned_ref = refs
    groups = len(outs)
    owned = outs[0].shape[0]
    columns = state_ref.shape[1]
    turned_ref[2 : columns + 2] = jnp.swapaxes(state_ref[...], 0, 1)
    turned_ref[:2] = before_ref[...]
    turned_ref[columns + 2 :] = after_ref[...]
    diffusion = diff_ref[...][None]
    advection = adv_ref[...][None]
    for k, out_ref in zip(issue_order(groups), outs):
        x = turned_ref[pl.ds(target(me_ref[0], k, groups) * owned, owned + 4)]
        out_ref[...] = stencil(stencil(x, diffusion, advection), diffusion, advection)


def join_kernel(me_ref, *refs):
    *blocks, out_ref, turned_ref, made_ref, sems = refs
    groups = len(blocks)
    owned = blocks[0].shape[0]
    writes = []
    for i, part in enumerate(pieces_of(out_ref.shape[0])):
        for k, block in zip(issue_order(groups), blocks):
            turned_ref[pl.ds(target(me_ref[0], k, groups) * owned, owned), part] = block[:, part]
        made_ref[part] = jnp.swapaxes(turned_ref[:, part], 0, 1)
        copy = pltpu.make_async_copy(made_ref.at[part], out_ref.at[part], sems.at[i])
        copy.start()
        writes.append(copy)
    for copy in writes:
        copy.wait()


def observe_kernel(me_ref, count_ref, after_ref, where_hbm, value_hbm, rinv_hbm, out_ref, where_ref, value_ref, rinv_ref, sems):
    del after_ref
    reads = [
        pltpu.make_async_copy(source, ref, sems.at[i])
        for i, (source, ref) in enumerate(((where_hbm, where_ref), (value_hbm, value_ref), (rinv_hbm, rinv_ref)))
    ]
    for copy in reads:
        copy.start()
    for copy in reads:
        copy.wait()
    columns, _, entries = out_ref.shape
    slots = where_ref.shape[1]
    slot = lax.broadcasted_iota(jnp.int32, (1, slots), 1)
    row = lax.broadcasted_iota(jnp.int32, (16, slots), 0)
    entry = lax.broadcasted_iota(jnp.int32, (entries, slots), 0)
    for c in range(columns):
        at = me_ref[0] * columns + c
        weight = jnp.where(slot < count_ref[0, at], rinv_ref[pl.ds(at, 1), :], 0.0)
        lhs = jnp.zeros((16, slots), jnp.float32)
        for first, source in ((0, weight), (3, weight * value_ref[pl.ds(at, 1), :])):
            for k, part in enumerate(split(source, 3)):
                lhs = jnp.where(row == first + k, part.astype(jnp.float32), lhs)
        onehot = (entry == where_ref[pl.ds(at, 1), :]).astype(jnp.float32).astype(jnp.bfloat16)
        sums = lax.dot_general(
            lhs.astype(jnp.bfloat16), onehot, (((1,), (1,)), ((), ())), preferred_element_type=jnp.float32
        )
        out_ref[c, 0:1] = sums[0:1] + (sums[1:2] + sums[2:3])
        out_ref[c, 1:2] = sums[3:4] + (sums[4:5] + sums[5:6])


def analyse_kernel(obs_ref, *refs):
    *blocks, root, mixed, ahead, s, p, u, t, r, w = refs
    groups = len(blocks) // 2
    states, outs = blocks[:groups], blocks[groups:]
    columns, local, entries = outs[0].shape
    members = groups * local
    spread = members - 1.0
    every = range(columns)
    parts = [(c, pl.ds(0, members)) for c in every]
    rows = lax.broadcasted_iota(jnp.int32, (members, members), 0)
    cols = lax.broadcasted_iota(jnp.int32, (members, members), 1)
    means, forces, scales, grams = [], [], [], []
    for c in every:
        x = jnp.concatenate([ref[c] for ref in states], axis=0)
        mean = jnp.sum(x, axis=0, keepdims=True) * (1.0 / members)
        anomaly = x - mean
        total = obs_ref[c, 0:1]
        forces.append(obs_ref[c, 1:2] - total * mean)
        means.append(mean)
        grams.append(square_by_rows(split(anomaly * jnp.sqrt(total), 3)))
        ahead[c] = anomaly
        store(w.at[0], c, slice(None), anomaly)
    for c in every:
        gram = grams[c] + jnp.where(rows == cols, spread, 0.0)
        norm = jnp.sum(jnp.sum(gram * gram, axis=0, keepdims=True), axis=1, keepdims=True)
        scales.append(jnp.sqrt(norm))
        gram = gram * (1.0 / scales[c])
        root[c] = gram
        store(s, c, slice(None), gram)

    def advance(step):
        for c, rows in parts:
            x = 2.25 * ahead[c, rows] + multiply(r.at[step % 2], w.at[step % 2], c, rows)
            ahead[c, rows] = x
            if step < PAIRS - 1:
                store(w.at[(step + 1) % 2], c, rows, x)

    for step in range(PAIRS):
        for c, rows in parts:
            x = multiply(s, s, c, rows)
            y = root[c, rows]
            store(p, c, rows, x)
            store(u, c, rows, 0.0625 * x - 0.5625 * y)
            mixed[c, rows] = 1.6875 * x - 2.4375 * y
        if step > 0:
            advance(step - 1)
        for c, rows in parts:
            store(r.at[step % 2], c, rows, mixed[c, rows] + multiply(u, p, c, rows))
        if step < PAIRS - 1:
            for c, rows in parts:
                x = 2.25 * root[c, rows] + multiply(r.at[step % 2], s, c, rows)
                store(t, c, rows, x)
                mixed[c, rows] = 2.25 * x
            for c, rows in parts:
                x = mixed[c, rows] + multiply(t, r.at[step % 2], c, rows)
                root[c, rows] = x
                store(s, c, rows, x)
    advance(PAIRS - 1)
    for c in every:
        x = ahead[c]
        inner = jnp.sum(x * forces[c], axis=1, keepdims=True)
        shift = jnp.sum(x * inner, axis=0, keepdims=True) / scales[c]
        result = means[c] + shift + x * jnp.sqrt(spread / scales[c])
        for k in range(groups):
            outs[k][c] = result[k * local : (k + 1) * local]


def analyse(states, obs):
    groups = len(states)
    columns, local, entries = states[0].shape
    members = groups * local
    full = pltpu.VMEM((columns, members, members), jnp.float32)
    pair = pltpu.VMEM((2, columns, members, members), jnp.bfloat16)
    two = pltpu.VMEM((2, 2, columns, members, members), jnp.bfloat16)
    ahead = pltpu.VMEM((columns, members, entries), jnp.float32)
    factor = pltpu.VMEM((2, 2, columns, members, entries), jnp.bfloat16)
    return call(
        analyse_kernel,
        [jax.ShapeDtypeStruct(states[0].shape, jnp.float32)] * groups,
        columns * 90 * 2 * members * members * entries,
        8 * columns * members * entries,
        scratch_shapes=[full, full, ahead, pair, pair, pair, pair, two, factor],
    )(obs, *states)


def body(background, diffusion, advection, obs_where, obs_count, obs_value, obs_rinv):
    local, columns, entries = background.shape
    groups = lax.axis_size("mem")
    tiles = lax.axis_size("tile")
    owned = columns // groups
    size = background.size
    block = jax.ShapeDtypeStruct((owned, local, entries), jnp.float32)
    edge = jax.ShapeDtypeStruct((2, local, entries), jnp.float32)
    me = lax.axis_index("mem")[None].astype(jnp.int32)
    width = min(columns, 8)

    low, high = call(
        edge_kernel,
        [edge, edge],
        0,
        16 * local * width * entries,
        in_specs=[HBM],
        scratch_shapes=[
            pltpu.VMEM((2, local, width, entries), jnp.float32),
            pltpu.SemaphoreType.DMA((2,)),
        ],
    )(in_hbm(background))
    before = lax.ppermute(high, "tile", [(i, (i + 1) % tiles) for i in range(tiles)])
    after = lax.ppermute(low, "tile", [((i + 1) % tiles, i) for i in range(tiles)])
    states = call(
        forecast_kernel,
        [block] * groups,
        20 * size,
        8 * size,
        in_specs=[SMEM] + [VMEM] * 5,
        scratch_shapes=[pltpu.VMEM((columns + 4, local, entries), jnp.float32)],
    )(me, background, before, after, diffusion[None], advection[None])
    obs = call(
        observe_kernel,
        jax.ShapeDtypeStruct((owned, 8, entries), jnp.float32),
        owned * 2 * 16 * obs_where.shape[2] * entries,
        12 * obs_where.size,
        in_specs=[SMEM, SMEM, VMEM] + [HBM] * 3,
        scratch_shapes=[
            pltpu.VMEM(obs_where.shape[1:], jnp.int32),
            pltpu.VMEM(obs_where.shape[1:], jnp.float32),
            pltpu.VMEM(obs_where.shape[1:], jnp.float32),
            pltpu.SemaphoreType.DMA((3,)),
        ],
    )(me, obs_count, states[-1], *(in_hbm(x[0]) for x in (obs_where, obs_value, obs_rinv)))
    results = exchange(analyse(exchange(states, False), obs), True)
    return call(
        join_kernel,
        jax.ShapeDtypeStruct(background.shape, jnp.float32),
        size,
        8 * size,
        in_specs=[SMEM] + [VMEM] * groups,
        out_specs=HBM,
        scratch_shapes=[
            pltpu.VMEM((columns, local, entries), jnp.float32),
            pltpu.VMEM(background.shape, jnp.float32),
            pltpu.SemaphoreType.DMA((len(pieces_of(local)),)),
        ],
    )(me, *results)


def solution(mesh):
    return jax.shard_map(
        body,
        mesh=mesh,
        in_specs=(
            P("mem", "tile", None),
            P(),
            P(),
            P("tile", None, None),
            P("tile", None),
            P("tile", None, None),
            P("tile", None, None),
        ),
        out_specs=P("mem", "tile", None),
        check_vma=False,
    )
```

```python
import jax
import jax.numpy as jnp
from jax import lax
from jax.experimental import pallas as pl
from jax.experimental.pallas import tpu as pltpu
from jax.sharding import PartitionSpec as P

PAIRS = 6
SCRATCH = 9
MIB = 1024 * 1024
SMEM = pl.BlockSpec(memory_space=pltpu.SMEM)
VMEM = pl.BlockSpec(memory_space=pltpu.VMEM)
HBM = pl.BlockSpec(memory_space=pltpu.HBM)


def call(kernel, out_shape, flops, moved, vmem=48 * MIB, **options):
    return pl.pallas_call(
        kernel,
        out_shape=out_shape,
        compiler_params=pltpu.CompilerParams(vmem_limit_bytes=vmem),
        cost_estimate=pl.CostEstimate(flops=flops, bytes_accessed=moved, transcendentals=0),
        **options,
    )


def in_hbm(x):
    return pltpu.with_memory_space_constraint(x, pltpu.HBM)


def target(me, k, groups):
    if groups & (groups - 1) == 0:
        return me ^ k
    return lax.rem(me + k, groups)


def source(me, k, groups):
    if groups & (groups - 1) == 0:
        return me ^ k
    return lax.rem(me + groups - k, groups)


def issue_order(groups):
    return sorted(range(1, groups), key=lambda k: (k != 1, -(k // 2).bit_count(), k)) + [0]


def exchange(blocks):
    groups = len(blocks)
    out = []
    for k, block in zip(issue_order(groups), blocks):
        pairs = [(i, i ^ k if groups & (groups - 1) == 0 else (i + k) % groups) for i in range(groups)]
        out.append(lax.ppermute(block, "mem", pairs) if k else block)
    return out


def split(x, parts):
    out = []
    for _ in range(parts):
        part = x.astype(jnp.bfloat16)
        out.append(part)
        x = x - part.astype(jnp.float32)
    return out


def store(ref, c, rows, x):
    for i, part in enumerate(split(x, 2)):
        ref[i, c, rows] = part


def multiply(a_ref, b_ref, c, rows):
    lhs = jnp.concatenate([a_ref[0, c, rows], a_ref[1, c, rows], a_ref[0, c, rows]], axis=1)
    rhs = jnp.concatenate([b_ref[0, c], b_ref[0, c], b_ref[1, c]], axis=0)
    return jnp.dot(lhs, rhs, preferred_element_type=jnp.float32)


def square_by_rows(parts):
    p0, p1, p2 = parts
    lhs = jnp.concatenate([p2, p0, p1, p1, p0, p0], axis=1)
    rhs = jnp.concatenate([p0, p2, p1, p0, p1, p0], axis=1)
    return lax.dot_general(lhs, rhs, (((1,), (1,)), ((), ())), preferred_element_type=jnp.float32)


def stencil(padded, diffusion, advection):
    middle = padded[1:-1]
    left = padded[:-2]
    right = padded[2:]
    return middle + diffusion * (left - 2.0 * middle + right) + advection * (0.5 * (left - right))


def inner_start(place, quarter):
    return place + quarter


def outer_start(place, quarter):
    return jnp.where(place < quarter, place, place + 2 * quarter)


def pieces_of(members):
    rows = 8 if members % 8 == 0 else members
    return [pl.ds(first, rows) for first in range(0, members, rows)]


def edge_kernel(state_ref, low_ref, high_ref, held_ref, sems):
    columns = state_ref.shape[1]
    width = held_ref.shape[2]
    reads = [
        pltpu.make_async_copy(state_ref.at[:, pl.ds(first, width)], held_ref.at[i], sems.at[i])
        for i, first in enumerate((0, columns - width))
    ]
    for copy in reads:
        copy.start()
    reads[0].wait()
    for i in range(2):
        low_ref[i] = held_ref[0, :, i]
    reads[1].wait()
    for i in range(2):
        high_ref[i] = held_ref[1, :, width - 2 + i]


def inner_kernel(me_ref, after_ref, state_ref, diff_ref, adv_ref, *refs):
    del after_ref
    *outs, rest_ref, turned_ref = refs
    groups = len(outs)
    half = outs[0].shape[0]
    columns = state_ref.shape[1]
    quarter = columns // 4
    turned_ref[...] = jnp.swapaxes(state_ref[...], 0, 1)
    diffusion = diff_ref[...][None]
    advection = adv_ref[...][None]
    for k, out_ref in zip(issue_order(groups), outs):
        x = turned_ref[pl.ds(target(me_ref[0], k, groups) * half + (quarter - 2), half + 4)]
        out_ref[...] = stencil(stencil(x, diffusion, advection), diffusion, advection)
    rest_ref[0] = turned_ref[: quarter + 2]
    rest_ref[1] = turned_ref[columns - quarter - 2 :]


def outer_kernel(
    me_ref, rest_ref, before_ref, after_ref, diff_ref, adv_ref, count_ref, where_ref, value_ref, rinv_ref, out_ref, obs_ref
):
    diffusion = diff_ref[...][None]
    advection = adv_ref[...][None]
    low = jnp.concatenate([before_ref[...], rest_ref[0]], axis=0)
    high = jnp.concatenate([rest_ref[1], after_ref[...]], axis=0)
    low = stencil(stencil(low, diffusion, advection), diffusion, advection)
    high = stencil(stencil(high, diffusion, advection), diffusion, advection)
    out_ref[...] = jnp.concatenate([low, high], axis=0).reshape(out_ref.shape)
    observe(me_ref[0], count_ref, where_ref, value_ref, rinv_ref, obs_ref)


def inner_join_kernel(after_ref, inner_ref, out_ref, made_ref, sems):
    del after_ref
    members, columns, entries = out_ref.shape
    groups, half, _, _ = inner_ref.shape
    quarter = columns // 4
    writes = []
    for i, part in enumerate(pieces_of(members)):
        x = inner_ref[:, :, part].reshape(groups * half, part.size, entries)
        made_ref[part] = jnp.swapaxes(x, 0, 1)
        copy = pltpu.make_async_copy(
            made_ref.at[part], out_ref.at[part, pl.ds(quarter, columns - 2 * quarter)], sems.at[i]
        )
        copy.start()
        writes.append(copy)
    for copy in writes:
        copy.wait()


def outer_join_kernel(me_ref, held_ref, *refs):
    del held_ref
    *outer, out_ref, turned_ref, made_ref, sems = refs
    members, columns, _ = out_ref.shape
    groups = len(outer)
    half = outer[0].shape[0]
    quarter = columns // 4
    writes = []
    for i, part in enumerate(pieces_of(members)):
        for k, block in zip(issue_order(groups), outer):
            turned_ref[pl.ds(source(me_ref[0], k, groups) * half, half), part] = block[:, part]
        made_ref[part] = jnp.swapaxes(turned_ref[:, part], 0, 1)
        for side in range(2):
            copy = pltpu.make_async_copy(
                made_ref.at[part, pl.ds(side * quarter, quarter)],
                out_ref.at[part, pl.ds(side * (columns - quarter), quarter)],
                sems.at[2 * i + side],
            )
            copy.start()
            writes.append(copy)
    for copy in writes:
        copy.wait()


def observe(me, count_ref, where_ref, value_ref, rinv_ref, out_ref):
    columns, _, entries = out_ref.shape
    half = columns // 2
    quarter = where_ref.shape[0] // 4
    slots = where_ref.shape[1]
    place = me * half
    column = lax.broadcasted_iota(jnp.int32, count_ref.shape, 1)
    slot = lax.broadcasted_iota(jnp.int32, (1, slots), 1)
    row = lax.broadcasted_iota(jnp.int32, (16, slots), 0)
    entry = lax.broadcasted_iota(jnp.int32, (entries, slots), 0)
    for c in range(columns):
        at = inner_start(place, quarter) + c if c < half else outer_start(place, quarter) + c - half
        count = jnp.sum(jnp.where(column == at, count_ref[...], 0), axis=1, keepdims=True)
        weight = jnp.where(slot < count, rinv_ref[pl.ds(at, 1), :], 0.0)
        lhs = jnp.zeros((16, slots), jnp.float32)
        for first, source in ((0, weight), (3, weight * value_ref[pl.ds(at, 1), :])):
            for k, part in enumerate(split(source, 3)):
                lhs = jnp.where(row == first + k, part.astype(jnp.float32), lhs)
        onehot = (entry == where_ref[pl.ds(at, 1), :]).astype(jnp.float32).astype(jnp.bfloat16)
        sums = lax.dot_general(
            lhs.astype(jnp.bfloat16), onehot, (((1,), (1,)), ((), ())), preferred_element_type=jnp.float32
        )
        out_ref[c, 0:1] = sums[0:1] + (sums[1:2] + sums[2:3])
        out_ref[c, 1:2] = sums[3:4] + (sums[4:5] + sums[5:6])


def analyse_kernel(first, after_ref, obs_ref, states, outs, done_ref, root, mixed, ahead, s, p, u, t, r, w):
    del after_ref
    done_ref[...] = jnp.zeros_like(done_ref)
    groups = len(outs)
    columns, local, entries = outs[0].shape
    members = groups * local
    spread = members - 1.0
    every = range(columns)
    parts = [(c, pl.ds(half, members // 2)) for c in every for half in (0, members // 2)]
    rows = lax.broadcasted_iota(jnp.int32, (members, members), 0)
    cols = lax.broadcasted_iota(jnp.int32, (members, members), 1)
    means, forces, scales, grams = [], [], [], []
    for c in every:
        x = jnp.concatenate([ref[c] for ref in states], axis=0)
        mean = jnp.sum(x, axis=0, keepdims=True) * (1.0 / members)
        anomaly = x - mean
        total = obs_ref[first + c, 0:1]
        forces.append(obs_ref[first + c, 1:2] - total * mean)
        means.append(mean)
        grams.append(square_by_rows(split(anomaly * jnp.sqrt(total), 3)))
        ahead[c] = anomaly
        store(w.at[0], c, slice(None), anomaly)
    for c in every:
        gram = grams[c] + jnp.where(rows == cols, spread, 0.0)
        norm = jnp.sum(jnp.sum(gram * gram, axis=0, keepdims=True), axis=1, keepdims=True)
        scales.append(jnp.sqrt(norm))
        gram = gram * (1.0 / scales[c])
        root[c] = gram
        store(s, c, slice(None), gram)

    def advance(step):
        for c, rows in parts:
            x = 2.25 * ahead[c, rows] + multiply(r.at[step % 2], w.at[step % 2], c, rows)
            ahead[c, rows] = x
            if step < PAIRS - 1:
                store(w.at[(step + 1) % 2], c, rows, x)

    for step in range(PAIRS):
        for c, rows in parts:
            x = multiply(s, s, c, rows)
            y = root[c, rows]
            store(p, c, rows, x)
            store(u, c, rows, 0.0625 * x - 0.5625 * y)
            mixed[c, rows] = 1.6875 * x - 2.4375 * y
        if step > 0:
            advance(step - 1)
        for c, rows in parts:
            store(r.at[step % 2], c, rows, mixed[c, rows] + multiply(u, p, c, rows))
        if step < PAIRS - 1:
            for c, rows in parts:
                x = 2.25 * root[c, rows] + multiply(r.at[step % 2], s, c, rows)
                store(t, c, rows, x)
                mixed[c, rows] = 2.25 * x
            for c, rows in parts:
                x = mixed[c, rows] + multiply(t, r.at[step % 2], c, rows)
                root[c, rows] = x
                store(s, c, rows, x)
    advance(PAIRS - 1)
    for c in every:
        x = ahead[c]
        inner = jnp.sum(x * forces[c], axis=1, keepdims=True)
        shift = jnp.sum(x * inner, axis=0, keepdims=True) / scales[c]
        result = means[c] + shift + x * jnp.sqrt(spread / scales[c])
        for k in range(groups):
            outs[k][c] = result[k * local : (k + 1) * local]


def analyse(states, obs, first, me, after, back):
    groups = len(states)
    columns, local, entries = states[0].shape
    members = groups * local
    block = jax.ShapeDtypeStruct((columns, local, entries), jnp.float32)
    whole = jax.ShapeDtypeStruct((groups, columns, local, entries), jnp.float32)
    token = jax.ShapeDtypeStruct(after.shape, jnp.float32)
    full = pltpu.VMEM((columns, members, members), jnp.float32)
    pair = pltpu.VMEM((2, columns, members, members), jnp.bfloat16)
    two = pltpu.VMEM((2, 2, columns, members, members), jnp.bfloat16)
    ahead = pltpu.VMEM((columns, members, entries), jnp.float32)
    factor = pltpu.VMEM((2, 2, columns, members, entries), jnp.bfloat16)

    def kernel(me_ref, after_ref, obs_ref, *refs):
        *blocks, done_ref = refs[:-SCRATCH]
        if back:
            whole_ref, *outs = blocks
            ins = [whole_ref.at[target(me_ref[0], k, groups)] for k in issue_order(groups)]
        else:
            *ins, whole_ref = blocks
            outs = [whole_ref.at[source(me_ref[0], k, groups)] for k in issue_order(groups)]
        analyse_kernel(first, after_ref, obs_ref, ins, outs, done_ref, *refs[-SCRATCH:])

    operands = [states] if back else states
    return call(
        kernel,
        [block] * groups + [token] if back else [whole, token],
        columns * 90 * 2 * members * members * entries,
        8 * columns * members * entries,
        in_specs=[SMEM] + [VMEM] * (len(operands) + 2),
        scratch_shapes=[full, full, ahead, pair, pair, pair, pair, two, factor],
    )(me, after, obs, *operands)


def body(background, diffusion, advection, obs_where, obs_count, obs_value, obs_rinv):
    local, columns, entries = background.shape
    groups = lax.axis_size("mem")
    tiles = lax.axis_size("tile")
    half = columns // groups // 2
    size = background.size
    block = jax.ShapeDtypeStruct((half, local, entries), jnp.float32)
    whole = jax.ShapeDtypeStruct((groups, half, local, entries), jnp.float32)
    rest = jax.ShapeDtypeStruct((2, columns // 4 + 2, local, entries), jnp.float32)
    edge = jax.ShapeDtypeStruct((2, local, entries), jnp.float32)
    me = lax.axis_index("mem")[None].astype(jnp.int32)
    pieces = len(pieces_of(local))
    width = min(columns, 8)
    diffusion, advection = diffusion[None], advection[None]

    low, high = call(
        edge_kernel,
        [edge, edge],
        0,
        16 * local * width * entries,
        in_specs=[HBM],
        scratch_shapes=[
            pltpu.VMEM((2, local, width, entries), jnp.float32),
            pltpu.SemaphoreType.DMA((2,)),
        ],
    )(in_hbm(background))
    before = lax.ppermute(high, "tile", [(i, (i + 1) % tiles) for i in range(tiles)])
    after = lax.ppermute(low, "tile", [((i + 1) % tiles, i) for i in range(tiles)])
    *inner, rest = call(
        inner_kernel,
        [block] * groups + [rest],
        20 * size,
        8 * size,
        in_specs=[SMEM] + [VMEM] * 4,
        scratch_shapes=[pltpu.VMEM((columns, local, entries), jnp.float32)],
    )(me, low, background, diffusion, advection)
    inner = exchange(inner)
    outer, obs = call(
        outer_kernel,
        [whole, jax.ShapeDtypeStruct((2 * half, 8, entries), jnp.float32)],
        20 * size,
        8 * size,
        in_specs=[SMEM] + [VMEM] * 9,
    )(me, rest, before, after, diffusion, advection, obs_count, obs_where[0], obs_value[0], obs_rinv[0])
    outer = lax.all_to_all(outer, "mem", split_axis=0, concat_axis=0, tiled=True)

    inner, done = analyse(inner, obs, 0, me, obs[0], False)
    inner = lax.all_to_all(inner, "mem", split_axis=0, concat_axis=0, tiled=True)
    *outer, _ = analyse(outer, obs, half, me, done, True)
    outer = exchange(outer)
    result = jax.ShapeDtypeStruct(background.shape, jnp.float32)
    made = call(
        inner_join_kernel,
        result,
        size,
        4 * size,
        in_specs=[VMEM, VMEM],
        out_specs=HBM,
        scratch_shapes=[
            pltpu.VMEM((local, groups * half, entries), jnp.float32),
            pltpu.SemaphoreType.DMA((pieces,)),
        ],
    )(outer[2], inner)
    return call(
        outer_join_kernel,
        result,
        size,
        4 * size,
        in_specs=[SMEM, HBM] + [VMEM] * groups,
        out_specs=HBM,
        scratch_shapes=[
            pltpu.VMEM((groups * half, local, entries), jnp.float32),
            pltpu.VMEM((local, groups * half, entries), jnp.float32),
            pltpu.SemaphoreType.DMA((2 * pieces,)),
        ],
        input_output_aliases={1: 0},
    )(me, made, *outer)


def solution(mesh):
    return jax.shard_map(
        body,
        mesh=mesh,
        in_specs=(
            P("mem", "tile", None),
            P(),
            P(),
            P("tile", None, None),
            P("tile", None),
            P("tile", None, None),
            P("tile", None, None),
        ),
        out_specs=P("mem", "tile", None),
        check_vma=False,
    )
```

```python
import jax
import jax.numpy as jnp
from jax import lax
from jax.experimental import pallas as pl
from jax.experimental.pallas import tpu as pltpu
from jax.sharding import PartitionSpec as P

PAIRS = 6
SCRATCH = 9
MIB = 1024 * 1024
SMEM = pl.BlockSpec(memory_space=pltpu.SMEM)
VMEM = pl.BlockSpec(memory_space=pltpu.VMEM)
HBM = pl.BlockSpec(memory_space=pltpu.HBM)


def call(kernel, out_shape, flops, moved, vmem=48 * MIB, **options):
    return pl.pallas_call(
        kernel,
        out_shape=out_shape,
        compiler_params=pltpu.CompilerParams(vmem_limit_bytes=vmem),
        cost_estimate=pl.CostEstimate(flops=flops, bytes_accessed=moved, transcendentals=0),
        **options,
    )


def in_hbm(x):
    return pltpu.with_memory_space_constraint(x, pltpu.HBM)


def target(me, k, groups):
    if groups & (groups - 1) == 0:
        return me ^ k
    return lax.rem(me + k, groups)


def source(me, k, groups):
    if groups & (groups - 1) == 0:
        return me ^ k
    return lax.rem(me + groups - k, groups)


def issue_order(groups):
    return sorted(range(1, groups), key=lambda k: (k != 1, -(k // 2).bit_count(), k)) + [0]


def exchange(blocks):
    groups = len(blocks)
    out = []
    for k, block in zip(issue_order(groups), blocks):
        pairs = [(i, i ^ k if groups & (groups - 1) == 0 else (i + k) % groups) for i in range(groups)]
        out.append(lax.ppermute(block, "mem", pairs) if k else block)
    return out


def split(x, parts):
    out = []
    for _ in range(parts):
        part = x.astype(jnp.bfloat16)
        out.append(part)
        x = x - part.astype(jnp.float32)
    return out


def store(ref, c, rows, x):
    for i, part in enumerate(split(x, 2)):
        ref[i, c, rows] = part


def multiply(a_ref, b_ref, c, rows):
    lhs = jnp.concatenate([a_ref[0, c, rows], a_ref[1, c, rows], a_ref[0, c, rows]], axis=1)
    rhs = jnp.concatenate([b_ref[0, c], b_ref[0, c], b_ref[1, c]], axis=0)
    return jnp.dot(lhs, rhs, preferred_element_type=jnp.float32)


def square_by_rows(parts):
    p0, p1, p2 = parts
    lhs = jnp.concatenate([p2, p0, p1, p1, p0, p0], axis=1)
    rhs = jnp.concatenate([p0, p2, p1, p0, p1, p0], axis=1)
    return lax.dot_general(lhs, rhs, (((1,), (1,)), ((), ())), preferred_element_type=jnp.float32)


def stencil(padded, diffusion, advection):
    middle = padded[1:-1]
    left = padded[:-2]
    right = padded[2:]
    return middle + diffusion * (left - 2.0 * middle + right) + advection * (0.5 * (left - right))


def inner_start(place, quarter):
    return place + quarter


def outer_start(place, quarter):
    return jnp.where(place < quarter, place, place + 2 * quarter)


def pieces_of(members):
    rows = 8 if members % 8 == 0 else members
    return [pl.ds(first, rows) for first in range(0, members, rows)]


def edge_kernel(state_ref, diff_ref, adv_ref, count_ref, low_ref, high_ref, num_ref, counts_ref, held_ref, sems):
    columns = state_ref.shape[1]
    width = held_ref.shape[2]
    reads = [
        pltpu.make_async_copy(state_ref.at[:, pl.ds(first, width)], held_ref.at[i], sems.at[i])
        for i, first in enumerate((0, columns - width))
    ]
    reads.append(pltpu.make_async_copy(diff_ref, num_ref.at[0], sems.at[2]))
    reads.append(pltpu.make_async_copy(adv_ref, num_ref.at[1], sems.at[3]))
    reads.append(pltpu.make_async_copy(count_ref, counts_ref, sems.at[4]))
    for copy in reads:
        copy.start()
    reads[0].wait()
    for i in range(2):
        low_ref[i] = held_ref[0, :, i]
    reads[1].wait()
    for i in range(2):
        high_ref[i] = held_ref[1, :, width - 2 + i]
    for copy in reads[2:]:
        copy.wait()


def inner_kernel(me_ref, state_ref, num_ref, *refs):
    *outs, rest_ref, turned_ref = refs
    groups = len(outs)
    half = outs[0].shape[0]
    columns = state_ref.shape[1]
    quarter = columns // 4
    turned_ref[...] = jnp.swapaxes(state_ref[...], 0, 1)
    diffusion = num_ref[0:1][None]
    advection = num_ref[1:2][None]
    for k, out_ref in zip(issue_order(groups), outs):
        x = turned_ref[pl.ds(target(me_ref[0], k, groups) * half + (quarter - 2), half + 4)]
        out_ref[...] = stencil(stencil(x, diffusion, advection), diffusion, advection)
    rest_ref[0] = turned_ref[: quarter + 2]
    rest_ref[1] = turned_ref[columns - quarter - 2 :]


def outer_kernel(
    me_ref, rest_ref, before_ref, after_ref, num_ref, count_ref, where_ref, value_ref, rinv_ref, out_ref, obs_ref
):
    diffusion = num_ref[0:1][None]
    advection = num_ref[1:2][None]
    low = jnp.concatenate([before_ref[...], rest_ref[0]], axis=0)
    high = jnp.concatenate([rest_ref[1], after_ref[...]], axis=0)
    low = stencil(stencil(low, diffusion, advection), diffusion, advection)
    high = stencil(stencil(high, diffusion, advection), diffusion, advection)
    out_ref[...] = jnp.concatenate([low, high], axis=0).reshape(out_ref.shape)
    half = obs_ref.shape[0]
    first = inner_start(me_ref[0] * half, where_ref.shape[0] // 4)
    observe(first, count_ref, where_ref, value_ref, rinv_ref, obs_ref)


def inner_join_kernel(after_ref, inner_ref, out_ref, made_ref, sems):
    del after_ref
    members, columns, entries = out_ref.shape
    groups, half, _, _ = inner_ref.shape
    quarter = columns // 4
    writes = []
    for i, part in enumerate(pieces_of(members)):
        x = inner_ref[:, :, part].reshape(groups * half, part.size, entries)
        made_ref[part] = jnp.swapaxes(x, 0, 1)
        copy = pltpu.make_async_copy(
            made_ref.at[part], out_ref.at[part, pl.ds(quarter, columns - 2 * quarter)], sems.at[i]
        )
        copy.start()
        writes.append(copy)
    for copy in writes:
        copy.wait()


def outer_join_kernel(me_ref, held_ref, *refs):
    del held_ref
    *outer, out_ref, turned_ref, made_ref, sems = refs
    members, columns, _ = out_ref.shape
    groups = len(outer)
    half = outer[0].shape[0]
    quarter = columns // 4
    writes = []
    for i, part in enumerate(pieces_of(members)):
        for k, block in zip(issue_order(groups), outer):
            turned_ref[pl.ds(source(me_ref[0], k, groups) * half, half), part] = block[:, part]
        made_ref[part] = jnp.swapaxes(turned_ref[:, part], 0, 1)
        for side in range(2):
            copy = pltpu.make_async_copy(
                made_ref.at[part, pl.ds(side * quarter, quarter)],
                out_ref.at[part, pl.ds(side * (columns - quarter), quarter)],
                sems.at[2 * i + side],
            )
            copy.start()
            writes.append(copy)
    for copy in writes:
        copy.wait()


def observe_kernel(me_ref, after_ref, count_ref, where_ref, value_ref, rinv_ref, out_ref):
    del after_ref
    half = out_ref.shape[0]
    first = outer_start(me_ref[0] * half, where_ref.shape[0] // 4)
    observe(first, count_ref, where_ref, value_ref, rinv_ref, out_ref)


def observe(first, count_ref, where_ref, value_ref, rinv_ref, out_ref):
    columns, _, entries = out_ref.shape
    slots = where_ref.shape[1]
    column = lax.broadcasted_iota(jnp.int32, count_ref.shape, 1)
    slot = lax.broadcasted_iota(jnp.int32, (1, slots), 1)
    row = lax.broadcasted_iota(jnp.int32, (16, slots), 0)
    entry = lax.broadcasted_iota(jnp.int32, (entries, slots), 0)
    for c in range(columns):
        at = first + c
        count = jnp.sum(jnp.where(column == at, count_ref[...], 0), axis=1, keepdims=True)
        weight = jnp.where(slot < count, rinv_ref[pl.ds(at, 1), :], 0.0)
        lhs = jnp.zeros((16, slots), jnp.float32)
        for line, values in ((0, weight), (3, weight * value_ref[pl.ds(at, 1), :])):
            for k, part in enumerate(split(values, 3)):
                lhs = jnp.where(row == line + k, part.astype(jnp.float32), lhs)
        onehot = (entry == where_ref[pl.ds(at, 1), :]).astype(jnp.float32).astype(jnp.bfloat16)
        sums = lax.dot_general(
            lhs.astype(jnp.bfloat16), onehot, (((1,), (1,)), ((), ())), preferred_element_type=jnp.float32
        )
        out_ref[c, 0:1] = sums[0:1] + (sums[1:2] + sums[2:3])
        out_ref[c, 1:2] = sums[3:4] + (sums[4:5] + sums[5:6])


def analyse_kernel(after_ref, obs_ref, states, outs, done_ref, root, mixed, ahead, s, p, u, t, r, w):
    del after_ref
    done_ref[...] = jnp.zeros_like(done_ref)
    groups = len(outs)
    columns, local, entries = outs[0].shape
    members = groups * local
    spread = members - 1.0
    every = range(columns)
    parts = [(c, pl.ds(half, members // 2)) for c in every for half in (0, members // 2)]
    rows = lax.broadcasted_iota(jnp.int32, (members, members), 0)
    cols = lax.broadcasted_iota(jnp.int32, (members, members), 1)
    means, forces, scales, grams = [], [], [], []
    for c in every:
        x = jnp.concatenate([ref[c] for ref in states], axis=0)
        mean = jnp.sum(x, axis=0, keepdims=True) * (1.0 / members)
        anomaly = x - mean
        total = obs_ref[c, 0:1]
        forces.append(obs_ref[c, 1:2] - total * mean)
        means.append(mean)
        grams.append(square_by_rows(split(anomaly * jnp.sqrt(total), 3)))
        ahead[c] = anomaly
        store(w.at[0], c, slice(None), anomaly)
    for c in every:
        gram = grams[c] + jnp.where(rows == cols, spread, 0.0)
        norm = jnp.sum(jnp.sum(gram * gram, axis=0, keepdims=True), axis=1, keepdims=True)
        scales.append(jnp.sqrt(norm))
        gram = gram * (1.0 / scales[c])
        root[c] = gram
        store(s, c, slice(None), gram)

    def advance(step):
        for c, rows in parts:
            x = 2.25 * ahead[c, rows] + multiply(r.at[step % 2], w.at[step % 2], c, rows)
            ahead[c, rows] = x
            if step < PAIRS - 1:
                store(w.at[(step + 1) % 2], c, rows, x)

    for step in range(PAIRS):
        for c, rows in parts:
            x = multiply(s, s, c, rows)
            y = root[c, rows]
            store(p, c, rows, x)
            store(u, c, rows, 0.0625 * x - 0.5625 * y)
            mixed[c, rows] = 1.6875 * x - 2.4375 * y
        if step > 0:
            advance(step - 1)
        for c, rows in parts:
            store(r.at[step % 2], c, rows, mixed[c, rows] + multiply(u, p, c, rows))
        if step < PAIRS - 1:
            for c, rows in parts:
                x = 2.25 * root[c, rows] + multiply(r.at[step % 2], s, c, rows)
                store(t, c, rows, x)
                mixed[c, rows] = 2.25 * x
            for c, rows in parts:
                x = mixed[c, rows] + multiply(t, r.at[step % 2], c, rows)
                root[c, rows] = x
                store(s, c, rows, x)
    advance(PAIRS - 1)
    for c in every:
        x = ahead[c]
        inner = jnp.sum(x * forces[c], axis=1, keepdims=True)
        shift = jnp.sum(x * inner, axis=0, keepdims=True) / scales[c]
        result = means[c] + shift + x * jnp.sqrt(spread / scales[c])
        for k in range(groups):
            outs[k][c] = result[k * local : (k + 1) * local]


def analyse(states, obs, me, after, back):
    groups = len(states)
    columns, local, entries = states[0].shape
    members = groups * local
    block = jax.ShapeDtypeStruct((columns, local, entries), jnp.float32)
    whole = jax.ShapeDtypeStruct((groups, columns, local, entries), jnp.float32)
    token = jax.ShapeDtypeStruct(after.shape, jnp.float32)
    full = pltpu.VMEM((columns, members, members), jnp.float32)
    pair = pltpu.VMEM((2, columns, members, members), jnp.bfloat16)
    two = pltpu.VMEM((2, 2, columns, members, members), jnp.bfloat16)
    ahead = pltpu.VMEM((columns, members, entries), jnp.float32)
    factor = pltpu.VMEM((2, 2, columns, members, entries), jnp.bfloat16)

    def kernel(me_ref, after_ref, obs_ref, *refs):
        *blocks, done_ref = refs[:-SCRATCH]
        if back:
            whole_ref, *outs = blocks
            ins = [whole_ref.at[target(me_ref[0], k, groups)] for k in issue_order(groups)]
        else:
            *ins, whole_ref = blocks
            outs = [whole_ref.at[source(me_ref[0], k, groups)] for k in issue_order(groups)]
        analyse_kernel(after_ref, obs_ref, ins, outs, done_ref, *refs[-SCRATCH:])

    operands = [states] if back else states
    return call(
        kernel,
        [block] * groups + [token] if back else [whole, token],
        columns * 90 * 2 * members * members * entries,
        8 * columns * members * entries,
        in_specs=[SMEM] + [VMEM] * (len(operands) + 2),
        scratch_shapes=[full, full, ahead, pair, pair, pair, pair, two, factor],
    )(me, after, obs, *operands)


def body(background, diffusion, advection, obs_where, obs_count, obs_value, obs_rinv):
    local, columns, entries = background.shape
    groups = lax.axis_size("mem")
    tiles = lax.axis_size("tile")
    half = columns // groups // 2
    size = background.size
    block = jax.ShapeDtypeStruct((half, local, entries), jnp.float32)
    whole = jax.ShapeDtypeStruct((groups, half, local, entries), jnp.float32)
    rest = jax.ShapeDtypeStruct((2, columns // 4 + 2, local, entries), jnp.float32)
    edge = jax.ShapeDtypeStruct((2, local, entries), jnp.float32)
    me = lax.axis_index("mem")[None].astype(jnp.int32)
    pieces = len(pieces_of(local))
    width = min(columns, 8)
    seen = jax.ShapeDtypeStruct((half, 8, entries), jnp.float32)
    numbers = jax.ShapeDtypeStruct((8, entries), jnp.float32)

    low, high, numbers, counts = call(
        edge_kernel,
        [edge, edge, numbers, jax.ShapeDtypeStruct(obs_count.shape, jnp.int32)],
        0,
        16 * local * width * entries,
        in_specs=[HBM] * 4,
        scratch_shapes=[
            pltpu.VMEM((2, local, width, entries), jnp.float32),
            pltpu.SemaphoreType.DMA((5,)),
        ],
    )(*(in_hbm(x) for x in (background, diffusion, advection, obs_count)))
    before = lax.ppermute(high, "tile", [(i, (i + 1) % tiles) for i in range(tiles)])
    after = lax.ppermute(low, "tile", [((i + 1) % tiles, i) for i in range(tiles)])
    *inner, rest = call(
        inner_kernel,
        [block] * groups + [rest],
        20 * size,
        8 * size,
        in_specs=[SMEM] + [VMEM] * 2,
        scratch_shapes=[pltpu.VMEM((columns, local, entries), jnp.float32)],
    )(me, background, numbers)
    inner = exchange(inner)
    slots = (counts, obs_where[0], obs_value[0], obs_rinv[0])
    outer, obs = call(
        outer_kernel,
        [whole, seen],
        20 * size,
        8 * size,
        in_specs=[SMEM] + [VMEM] * 8,
    )(me, rest, before, after, numbers, *slots)
    outer = lax.all_to_all(outer, "mem", split_axis=0, concat_axis=0, tiled=True)

    inner, done = analyse(inner, obs, me, obs[0], False)
    inner = lax.all_to_all(inner, "mem", split_axis=0, concat_axis=0, tiled=True)
    obs = call(
        observe_kernel,
        seen,
        half * 2 * 16 * obs_where.shape[2] * entries,
        12 * obs_where.size,
        in_specs=[SMEM] + [VMEM] * 5,
    )(me, done, *slots)
    *outer, _ = analyse(outer, obs, me, done, True)
    outer = exchange(outer)
    result = jax.ShapeDtypeStruct(background.shape, jnp.float32)
    made = call(
        inner_join_kernel,
        result,
        size,
        4 * size,
        in_specs=[VMEM, VMEM],
        out_specs=HBM,
        scratch_shapes=[
            pltpu.VMEM((local, groups * half, entries), jnp.float32),
            pltpu.SemaphoreType.DMA((pieces,)),
        ],
    )(outer[2], inner)
    return call(
        outer_join_kernel,
        result,
        size,
        4 * size,
        in_specs=[SMEM, HBM] + [VMEM] * groups,
        out_specs=HBM,
        scratch_shapes=[
            pltpu.VMEM((groups * half, local, entries), jnp.float32),
            pltpu.VMEM((local, groups * half, entries), jnp.float32),
            pltpu.SemaphoreType.DMA((2 * pieces,)),
        ],
        input_output_aliases={1: 0},
    )(me, made, *outer)


def solution(mesh):
    return jax.shard_map(
        body,
        mesh=mesh,
        in_specs=(
            P("mem", "tile", None),
            P(),
            P(),
            P("tile", None, None),
            P("tile", None),
            P("tile", None, None),
            P("tile", None, None),
        ),
        out_specs=P("mem", "tile", None),
        check_vma=False,
    )
```

```python
import jax
import jax.numpy as jnp
from jax import lax
from jax.experimental import pallas as pl
from jax.experimental.pallas import tpu as pltpu
from jax.sharding import PartitionSpec as P

PAIRS = 6
SCRATCH = 9
MIB = 1024 * 1024
SMEM = pl.BlockSpec(memory_space=pltpu.SMEM)
VMEM = pl.BlockSpec(memory_space=pltpu.VMEM)
HBM = pl.BlockSpec(memory_space=pltpu.HBM)


def call(kernel, out_shape, flops, moved, vmem=48 * MIB, **options):
    return pl.pallas_call(
        kernel,
        out_shape=out_shape,
        compiler_params=pltpu.CompilerParams(vmem_limit_bytes=vmem),
        cost_estimate=pl.CostEstimate(flops=flops, bytes_accessed=moved, transcendentals=0),
        **options,
    )


def in_hbm(x):
    return pltpu.with_memory_space_constraint(x, pltpu.HBM)


def target(me, k, groups):
    if groups & (groups - 1) == 0:
        return me ^ k
    return lax.rem(me + k, groups)


def source(me, k, groups):
    if groups & (groups - 1) == 0:
        return me ^ k
    return lax.rem(me + groups - k, groups)


def issue_order(groups):
    return sorted(range(1, groups), key=lambda k: (k != 1, -(k // 2).bit_count(), k)) + [0]


def exchange(blocks):
    groups = len(blocks)
    out = []
    for k, block in zip(issue_order(groups), blocks):
        pairs = [(i, i ^ k if groups & (groups - 1) == 0 else (i + k) % groups) for i in range(groups)]
        out.append(lax.ppermute(block, "mem", pairs) if k else block)
    return out


def split(x, parts):
    out = []
    for _ in range(parts):
        part = x.astype(jnp.bfloat16)
        out.append(part)
        x = x - part.astype(jnp.float32)
    return out


def store(ref, c, rows, x):
    for i, part in enumerate(split(x, 2)):
        ref[i, c, rows] = part


def multiply(a_ref, b_ref, c, rows):
    lhs = jnp.concatenate([a_ref[0, c, rows], a_ref[1, c, rows], a_ref[0, c, rows]], axis=1)
    rhs = jnp.concatenate([b_ref[0, c], b_ref[0, c], b_ref[1, c]], axis=0)
    return jnp.dot(lhs, rhs, preferred_element_type=jnp.float32)


def square_by_rows(parts):
    p0, p1, p2 = parts
    lhs = jnp.concatenate([p2, p0, p1, p1, p0, p0], axis=1)
    rhs = jnp.concatenate([p0, p2, p1, p0, p1, p0], axis=1)
    return lax.dot_general(lhs, rhs, (((1,), (1,)), ((), ())), preferred_element_type=jnp.float32)


def stencil(padded, diffusion, advection):
    middle = padded[1:-1]
    left = padded[:-2]
    right = padded[2:]
    return middle + diffusion * (left - 2.0 * middle + right) + advection * (0.5 * (left - right))


def outer_start(place, side, columns):
    return jnp.where(place < side, place, place + columns - 2 * side)


def pieces_of(members):
    rows = 8 if members % 8 == 0 else members
    return [pl.ds(first, rows) for first in range(0, members, rows)]


def edge_kernel(state_ref, diff_ref, adv_ref, count_ref, low_ref, high_ref, num_ref, counts_ref, held_ref, sems):
    columns = state_ref.shape[1]
    width = held_ref.shape[2]
    reads = [
        pltpu.make_async_copy(state_ref.at[:, pl.ds(first, width)], held_ref.at[i], sems.at[i])
        for i, first in enumerate((0, columns - width))
    ]
    reads.append(pltpu.make_async_copy(diff_ref, num_ref.at[0], sems.at[2]))
    reads.append(pltpu.make_async_copy(adv_ref, num_ref.at[1], sems.at[3]))
    reads.append(pltpu.make_async_copy(count_ref, counts_ref, sems.at[4]))
    for copy in reads:
        copy.start()
    reads[0].wait()
    for i in range(2):
        low_ref[i] = held_ref[0, :, i]
    reads[1].wait()
    for i in range(2):
        high_ref[i] = held_ref[1, :, width - 2 + i]
    for copy in reads[2:]:
        copy.wait()


def inner_kernel(me_ref, state_ref, num_ref, *refs):
    *outs, rest_ref, turned_ref = refs
    groups = len(outs)
    owned = outs[0].shape[0]
    columns = state_ref.shape[1]
    side = rest_ref.shape[1] - 2
    turned_ref[...] = jnp.swapaxes(state_ref[...], 0, 1)
    diffusion = num_ref[0:1][None]
    advection = num_ref[1:2][None]
    for k, out_ref in zip(issue_order(groups), outs):
        x = turned_ref[pl.ds(target(me_ref[0], k, groups) * owned + (side - 2), owned + 4)]
        out_ref[...] = stencil(stencil(x, diffusion, advection), diffusion, advection)
    rest_ref[0] = turned_ref[: side + 2]
    rest_ref[1] = turned_ref[columns - side - 2 :]


def outer_kernel(
    me_ref, rest_ref, before_ref, after_ref, num_ref, count_ref, where_ref, value_ref, rinv_ref, out_ref, obs_ref
):
    diffusion = num_ref[0:1][None]
    advection = num_ref[1:2][None]
    low = jnp.concatenate([before_ref[...], rest_ref[0]], axis=0)
    high = jnp.concatenate([rest_ref[1], after_ref[...]], axis=0)
    low = stencil(stencil(low, diffusion, advection), diffusion, advection)
    high = stencil(stencil(high, diffusion, advection), diffusion, advection)
    out_ref[...] = jnp.concatenate([low, high], axis=0).reshape(out_ref.shape)
    first = me_ref[0] * obs_ref.shape[0] + (rest_ref.shape[1] - 2)
    observe(first, count_ref, where_ref, value_ref, rinv_ref, obs_ref)


def join_kernel(me_ref, *refs):
    *outer, inner_ref, out_ref, turned_ref, made_ref, sems = refs
    members, columns, entries = out_ref.shape
    groups, owned, _, _ = inner_ref.shape
    side = (columns - groups * owned) // 2
    writes = []
    for i, part in enumerate(pieces_of(members)):
        for k, block in zip(issue_order(groups), outer):
            place = source(me_ref[0], k, groups) * block.shape[0]
            turned_ref[pl.ds(outer_start(place, side, columns), block.shape[0]), part] = block[:, part]
        turned_ref[side : columns - side, part] = inner_ref[:, :, part].reshape(groups * owned, part.size, entries)
        made_ref[part] = jnp.swapaxes(turned_ref[:, part], 0, 1)
        copy = pltpu.make_async_copy(made_ref.at[part], out_ref.at[part], sems.at[i])
        copy.start()
        writes.append(copy)
    for copy in writes:
        copy.wait()


def observe_kernel(side, me_ref, after_ref, count_ref, where_ref, value_ref, rinv_ref, out_ref):
    del after_ref
    first = outer_start(me_ref[0] * out_ref.shape[0], side, where_ref.shape[0])
    observe(first, count_ref, where_ref, value_ref, rinv_ref, out_ref)


def observe(first, count_ref, where_ref, value_ref, rinv_ref, out_ref):
    columns, _, entries = out_ref.shape
    slots = where_ref.shape[1]
    column = lax.broadcasted_iota(jnp.int32, count_ref.shape, 1)
    slot = lax.broadcasted_iota(jnp.int32, (1, slots), 1)
    row = lax.broadcasted_iota(jnp.int32, (16, slots), 0)
    entry = lax.broadcasted_iota(jnp.int32, (entries, slots), 0)
    for c in range(columns):
        at = first + c
        count = jnp.sum(jnp.where(column == at, count_ref[...], 0), axis=1, keepdims=True)
        weight = jnp.where(slot < count, rinv_ref[pl.ds(at, 1), :], 0.0)
        lhs = jnp.zeros((16, slots), jnp.float32)
        for line, values in ((0, weight), (3, weight * value_ref[pl.ds(at, 1), :])):
            for k, part in enumerate(split(values, 3)):
                lhs = jnp.where(row == line + k, part.astype(jnp.float32), lhs)
        onehot = (entry == where_ref[pl.ds(at, 1), :]).astype(jnp.float32).astype(jnp.bfloat16)
        sums = lax.dot_general(
            lhs.astype(jnp.bfloat16), onehot, (((1,), (1,)), ((), ())), preferred_element_type=jnp.float32
        )
        out_ref[c, 0:1] = sums[0:1] + (sums[1:2] + sums[2:3])
        out_ref[c, 1:2] = sums[3:4] + (sums[4:5] + sums[5:6])


def analyse_kernel(after_ref, obs_ref, states, outs, done_ref, root, mixed, ahead, s, p, u, t, r, w):
    del after_ref
    done_ref[...] = jnp.zeros_like(done_ref)
    groups = len(outs)
    columns, local, entries = outs[0].shape
    members = groups * local
    spread = members - 1.0
    every = range(columns)
    parts = [(c, pl.ds(half, members // 2)) for c in every for half in (0, members // 2)]
    rows = lax.broadcasted_iota(jnp.int32, (members, members), 0)
    cols = lax.broadcasted_iota(jnp.int32, (members, members), 1)
    means, forces, scales, grams = [], [], [], []
    for c in every:
        x = jnp.concatenate([ref[c] for ref in states], axis=0)
        mean = jnp.sum(x, axis=0, keepdims=True) * (1.0 / members)
        anomaly = x - mean
        total = obs_ref[c, 0:1]
        forces.append(obs_ref[c, 1:2] - total * mean)
        means.append(mean)
        grams.append(square_by_rows(split(anomaly * jnp.sqrt(total), 3)))
        ahead[c] = anomaly
        store(w.at[0], c, slice(None), anomaly)
    for c in every:
        gram = grams[c] + jnp.where(rows == cols, spread, 0.0)
        norm = jnp.sum(jnp.sum(gram * gram, axis=0, keepdims=True), axis=1, keepdims=True)
        scales.append(jnp.sqrt(norm))
        gram = gram * (1.0 / scales[c])
        root[c] = gram
        store(s, c, slice(None), gram)

    def advance(step):
        for c, rows in parts:
            x = 2.25 * ahead[c, rows] + multiply(r.at[step % 2], w.at[step % 2], c, rows)
            ahead[c, rows] = x
            if step < PAIRS - 1:
                store(w.at[(step + 1) % 2], c, rows, x)

    for step in range(PAIRS):
        for c, rows in parts:
            x = multiply(s, s, c, rows)
            y = root[c, rows]
            store(p, c, rows, x)
            store(u, c, rows, 0.0625 * x - 0.5625 * y)
            mixed[c, rows] = 1.6875 * x - 2.4375 * y
        if step > 0:
            advance(step - 1)
        for c, rows in parts:
            store(r.at[step % 2], c, rows, mixed[c, rows] + multiply(u, p, c, rows))
        if step < PAIRS - 1:
            for c, rows in parts:
                x = 2.25 * root[c, rows] + multiply(r.at[step % 2], s, c, rows)
                store(t, c, rows, x)
                mixed[c, rows] = 2.25 * x
            for c, rows in parts:
                x = mixed[c, rows] + multiply(t, r.at[step % 2], c, rows)
                root[c, rows] = x
                store(s, c, rows, x)
    advance(PAIRS - 1)
    for c in every:
        x = ahead[c]
        inner = jnp.sum(x * forces[c], axis=1, keepdims=True)
        shift = jnp.sum(x * inner, axis=0, keepdims=True) / scales[c]
        result = means[c] + shift + x * jnp.sqrt(spread / scales[c])
        for k in range(groups):
            outs[k][c] = result[k * local : (k + 1) * local]


def analyse(states, obs, me, after, back):
    groups = len(states)
    columns, local, entries = states[0].shape
    members = groups * local
    block = jax.ShapeDtypeStruct((columns, local, entries), jnp.float32)
    whole = jax.ShapeDtypeStruct((groups, columns, local, entries), jnp.float32)
    token = jax.ShapeDtypeStruct(after.shape, jnp.float32)
    full = pltpu.VMEM((columns, members, members), jnp.float32)
    pair = pltpu.VMEM((2, columns, members, members), jnp.bfloat16)
    two = pltpu.VMEM((2, 2, columns, members, members), jnp.bfloat16)
    ahead = pltpu.VMEM((columns, members, entries), jnp.float32)
    factor = pltpu.VMEM((2, 2, columns, members, entries), jnp.bfloat16)

    def kernel(me_ref, after_ref, obs_ref, *refs):
        *blocks, done_ref = refs[:-SCRATCH]
        if back:
            whole_ref, *outs = blocks
            ins = [whole_ref.at[target(me_ref[0], k, groups)] for k in issue_order(groups)]
        else:
            *ins, whole_ref = blocks
            outs = [whole_ref.at[source(me_ref[0], k, groups)] for k in issue_order(groups)]
        analyse_kernel(after_ref, obs_ref, ins, outs, done_ref, *refs[-SCRATCH:])

    operands = [states] if back else states
    return call(
        kernel,
        [block] * groups + [token] if back else [whole, token],
        columns * 90 * 2 * members * members * entries,
        8 * columns * members * entries,
        in_specs=[SMEM] + [VMEM] * (len(operands) + 2),
        scratch_shapes=[full, full, ahead, pair, pair, pair, pair, two, factor],
    )(me, after, obs, *operands)


def body(background, diffusion, advection, obs_where, obs_count, obs_value, obs_rinv):
    local, columns, entries = background.shape
    groups = lax.axis_size("mem")
    tiles = lax.axis_size("tile")
    last = max(columns // groups // 4, 1)
    main = columns // groups - last
    side = groups * last // 2
    size = background.size
    block = jax.ShapeDtypeStruct((main, local, entries), jnp.float32)
    whole = jax.ShapeDtypeStruct((groups, last, local, entries), jnp.float32)
    rest = jax.ShapeDtypeStruct((2, side + 2, local, entries), jnp.float32)
    edge = jax.ShapeDtypeStruct((2, local, entries), jnp.float32)
    me = lax.axis_index("mem")[None].astype(jnp.int32)
    pieces = len(pieces_of(local))
    width = min(columns, 8)
    seen = [jax.ShapeDtypeStruct((owned, 8, entries), jnp.float32) for owned in (main, last)]
    numbers = jax.ShapeDtypeStruct((8, entries), jnp.float32)

    low, high, numbers, counts = call(
        edge_kernel,
        [edge, edge, numbers, jax.ShapeDtypeStruct(obs_count.shape, jnp.int32)],
        0,
        16 * local * width * entries,
        in_specs=[HBM] * 4,
        scratch_shapes=[
            pltpu.VMEM((2, local, width, entries), jnp.float32),
            pltpu.SemaphoreType.DMA((5,)),
        ],
    )(*(in_hbm(x) for x in (background, diffusion, advection, obs_count)))
    before = lax.ppermute(high, "tile", [(i, (i + 1) % tiles) for i in range(tiles)])
    after = lax.ppermute(low, "tile", [((i + 1) % tiles, i) for i in range(tiles)])
    *inner, rest = call(
        inner_kernel,
        [block] * groups + [rest],
        20 * size,
        8 * size,
        in_specs=[SMEM] + [VMEM] * 2,
        scratch_shapes=[pltpu.VMEM((columns, local, entries), jnp.float32)],
    )(me, background, numbers)
    inner = exchange(inner)
    slots = (counts, obs_where[0], obs_value[0], obs_rinv[0])
    outer, obs = call(
        outer_kernel,
        [whole, seen[0]],
        20 * size,
        8 * size,
        in_specs=[SMEM] + [VMEM] * 8,
    )(me, rest, before, after, numbers, *slots)
    outer = lax.all_to_all(outer, "mem", split_axis=0, concat_axis=0, tiled=True)

    inner, done = analyse(inner, obs, me, obs[0], False)
    inner = lax.all_to_all(inner, "mem", split_axis=0, concat_axis=0, tiled=True)

    def observe_last(*refs):
        observe_kernel(side, *refs)

    obs = call(
        observe_last,
        seen[1],
        last * 2 * 16 * obs_where.shape[2] * entries,
        12 * obs_where.size,
        in_specs=[SMEM] + [VMEM] * 5,
    )(me, done, *slots)
    *outer, _ = analyse(outer, obs, me, done, True)
    outer = exchange(outer)
    return call(
        join_kernel,
        jax.ShapeDtypeStruct(background.shape, jnp.float32),
        size,
        8 * size,
        in_specs=[SMEM] + [VMEM] * (groups + 1),
        out_specs=HBM,
        scratch_shapes=[
            pltpu.VMEM((columns, local, entries), jnp.float32),
            pltpu.VMEM(background.shape, jnp.float32),
            pltpu.SemaphoreType.DMA((pieces,)),
        ],
    )(me, *outer, inner)


def solution(mesh):
    return jax.shard_map(
        body,
        mesh=mesh,
        in_specs=(
            P("mem", "tile", None),
            P(),
            P(),
            P("tile", None, None),
            P("tile", None),
            P("tile", None, None),
            P("tile", None, None),
        ),
        out_specs=P("mem", "tile", None),
        check_vma=False,
    )
```

```python
import jax
import jax.numpy as jnp
from jax import lax
from jax.experimental import pallas as pl
from jax.experimental.pallas import tpu as pltpu
from jax.sharding import PartitionSpec as P

PAIRS = 6
SCRATCH = 9
MIB = 1024 * 1024
SMEM = pl.BlockSpec(memory_space=pltpu.SMEM)
VMEM = pl.BlockSpec(memory_space=pltpu.VMEM)
HBM = pl.BlockSpec(memory_space=pltpu.HBM)


def call(kernel, out_shape, flops, moved, vmem=48 * MIB, **options):
    return pl.pallas_call(
        kernel,
        out_shape=out_shape,
        compiler_params=pltpu.CompilerParams(vmem_limit_bytes=vmem),
        cost_estimate=pl.CostEstimate(flops=flops, bytes_accessed=moved, transcendentals=0),
        **options,
    )


def in_hbm(x):
    return pltpu.with_memory_space_constraint(x, pltpu.HBM)


def target(me, k, groups):
    if groups & (groups - 1) == 0:
        return me ^ k
    return lax.rem(me + k, groups)


def source(me, k, groups):
    if groups & (groups - 1) == 0:
        return me ^ k
    return lax.rem(me + groups - k, groups)


def issue_order(groups):
    return sorted(range(1, groups), key=lambda k: (k != 1, -(k // 2).bit_count(), k)) + [0]


def exchange(blocks):
    groups = len(blocks)
    out = []
    for k, block in zip(issue_order(groups), blocks):
        pairs = [(i, i ^ k if groups & (groups - 1) == 0 else (i + k) % groups) for i in range(groups)]
        out.append(lax.ppermute(block, "mem", pairs) if k else block)
    return out


def split(x, parts):
    out = []
    for _ in range(parts):
        part = x.astype(jnp.bfloat16)
        out.append(part)
        x = x - part.astype(jnp.float32)
    return out


def store(ref, c, rows, x):
    for i, part in enumerate(split(x, 2)):
        ref[i, c, rows] = part


def multiply(a_ref, b_ref, c, rows):
    lhs = jnp.concatenate([a_ref[0, c, rows], a_ref[1, c, rows], a_ref[0, c, rows]], axis=1)
    rhs = jnp.concatenate([b_ref[0, c], b_ref[0, c], b_ref[1, c]], axis=0)
    return jnp.dot(lhs, rhs, preferred_element_type=jnp.float32)


def square_by_rows(parts):
    p0, p1, p2 = parts
    lhs = jnp.concatenate([p2, p0, p1, p1, p0, p0], axis=1)
    rhs = jnp.concatenate([p0, p2, p1, p0, p1, p0], axis=1)
    return lax.dot_general(lhs, rhs, (((1,), (1,)), ((), ())), preferred_element_type=jnp.float32)


def stencil(padded, diffusion, advection):
    middle = padded[1:-1]
    left = padded[:-2]
    right = padded[2:]
    return middle + diffusion * (left - 2.0 * middle + right) + advection * (0.5 * (left - right))


def inner_start(place, quarter):
    return place + quarter


def outer_start(place, quarter):
    return jnp.where(place < quarter, place, place + 2 * quarter)


def pieces_of(members):
    rows = 8 if members % 8 == 0 else members
    return [pl.ds(first, rows) for first in range(0, members, rows)]


def edge_kernel(state_ref, diff_ref, adv_ref, count_ref, low_ref, high_ref, num_ref, counts_ref, held_ref, sems):
    columns = state_ref.shape[1]
    width = held_ref.shape[2]
    reads = [
        pltpu.make_async_copy(state_ref.at[:, pl.ds(first, width)], held_ref.at[i], sems.at[i])
        for i, first in enumerate((0, columns - width))
    ]
    reads.append(pltpu.make_async_copy(diff_ref, num_ref.at[0], sems.at[2]))
    reads.append(pltpu.make_async_copy(adv_ref, num_ref.at[1], sems.at[3]))
    reads.append(pltpu.make_async_copy(count_ref, counts_ref, sems.at[4]))
    for copy in reads:
        copy.start()
    reads[0].wait()
    for i in range(2):
        low_ref[i] = held_ref[0, :, i]
    reads[1].wait()
    for i in range(2):
        high_ref[i] = held_ref[1, :, width - 2 + i]
    for copy in reads[2:]:
        copy.wait()


def inner_kernel(me_ref, state_ref, num_ref, *refs):
    *outs, rest_ref, turned_ref = refs
    groups = len(outs)
    half = outs[0].shape[0]
    columns = state_ref.shape[1]
    quarter = columns // 4
    turned_ref[...] = jnp.swapaxes(state_ref[...], 0, 1)
    diffusion = num_ref[0:1][None]
    advection = num_ref[1:2][None]
    for k, out_ref in zip(issue_order(groups), outs):
        x = turned_ref[pl.ds(target(me_ref[0], k, groups) * half + (quarter - 2), half + 4)]
        out_ref[...] = stencil(stencil(x, diffusion, advection), diffusion, advection)
    rest_ref[0] = turned_ref[: quarter + 2]
    rest_ref[1] = turned_ref[columns - quarter - 2 :]


def outer_kernel(rest_ref, before_ref, after_ref, num_ref, out_ref, done_ref):
    done_ref[...] = jnp.zeros_like(done_ref)
    diffusion = num_ref[0:1][None]
    advection = num_ref[1:2][None]
    low = jnp.concatenate([before_ref[...], rest_ref[0]], axis=0)
    high = jnp.concatenate([rest_ref[1], after_ref[...]], axis=0)
    low = stencil(stencil(low, diffusion, advection), diffusion, advection)
    high = stencil(stencil(high, diffusion, advection), diffusion, advection)
    out_ref[...] = jnp.concatenate([low, high], axis=0).reshape(out_ref.shape)


def inner_join_kernel(after_ref, inner_ref, out_ref, made_ref, sems):
    del after_ref
    members, columns, entries = out_ref.shape
    groups, half, _, _ = inner_ref.shape
    quarter = columns // 4
    writes = []
    for i, part in enumerate(pieces_of(members)):
        x = inner_ref[:, :, part].reshape(groups * half, part.size, entries)
        made_ref[part] = jnp.swapaxes(x, 0, 1)
        copy = pltpu.make_async_copy(
            made_ref.at[part], out_ref.at[part, pl.ds(quarter, columns - 2 * quarter)], sems.at[i]
        )
        copy.start()
        writes.append(copy)
    for copy in writes:
        copy.wait()


def outer_join_kernel(me_ref, held_ref, *refs):
    del held_ref
    *outer, out_ref, turned_ref, made_ref, sems = refs
    members, columns, _ = out_ref.shape
    groups = len(outer)
    half = outer[0].shape[0]
    quarter = columns // 4
    writes = []
    for i, part in enumerate(pieces_of(members)):
        for k, block in zip(issue_order(groups), outer):
            turned_ref[pl.ds(source(me_ref[0], k, groups) * half, half), part] = block[:, part]
        made_ref[part] = jnp.swapaxes(turned_ref[:, part], 0, 1)
        for side in range(2):
            copy = pltpu.make_async_copy(
                made_ref.at[part, pl.ds(side * quarter, quarter)],
                out_ref.at[part, pl.ds(side * (columns - quarter), quarter)],
                sems.at[2 * i + side],
            )
            copy.start()
            writes.append(copy)
    for copy in writes:
        copy.wait()


def observe(first, count_ref, where_ref, value_ref, rinv_ref, out_ref):
    columns, _, entries = out_ref.shape
    slots = where_ref.shape[1]
    column = lax.broadcasted_iota(jnp.int32, count_ref.shape, 1)
    slot = lax.broadcasted_iota(jnp.int32, (1, slots), 1)
    row = lax.broadcasted_iota(jnp.int32, (16, slots), 0)
    entry = lax.broadcasted_iota(jnp.int32, (entries, slots), 0)
    for c in range(columns):
        at = first + c
        count = jnp.sum(jnp.where(column == at, count_ref[...], 0), axis=1, keepdims=True)
        weight = jnp.where(slot < count, rinv_ref[pl.ds(at, 1), :], 0.0)
        lhs = jnp.zeros((16, slots), jnp.float32)
        for line, values in ((0, weight), (3, weight * value_ref[pl.ds(at, 1), :])):
            for k, part in enumerate(split(values, 3)):
                lhs = jnp.where(row == line + k, part.astype(jnp.float32), lhs)
        onehot = (entry == where_ref[pl.ds(at, 1), :]).astype(jnp.float32).astype(jnp.bfloat16)
        sums = lax.dot_general(
            lhs.astype(jnp.bfloat16), onehot, (((1,), (1,)), ((), ())), preferred_element_type=jnp.float32
        )
        out_ref[c, 0:1] = sums[0:1] + (sums[1:2] + sums[2:3])
        out_ref[c, 1:2] = sums[3:4] + (sums[4:5] + sums[5:6])


def analyse_kernel(obs_ref, states, outs, root, mixed, ahead, s, p, u, t, r, w):
    groups = len(outs)
    columns, local, entries = outs[0].shape
    members = groups * local
    spread = members - 1.0
    every = range(columns)
    parts = [(c, pl.ds(half, members // 2)) for c in every for half in (0, members // 2)]
    rows = lax.broadcasted_iota(jnp.int32, (members, members), 0)
    cols = lax.broadcasted_iota(jnp.int32, (members, members), 1)
    means, forces, scales, grams = [], [], [], []
    for c in every:
        x = jnp.concatenate([ref[c] for ref in states], axis=0)
        mean = jnp.sum(x, axis=0, keepdims=True) * (1.0 / members)
        anomaly = x - mean
        total = obs_ref[c, 0:1]
        forces.append(obs_ref[c, 1:2] - total * mean)
        means.append(mean)
        grams.append(square_by_rows(split(anomaly * jnp.sqrt(total), 3)))
        ahead[c] = anomaly
        store(w.at[0], c, slice(None), anomaly)
    for c in every:
        gram = grams[c] + jnp.where(rows == cols, spread, 0.0)
        norm = jnp.sum(jnp.sum(gram * gram, axis=0, keepdims=True), axis=1, keepdims=True)
        scales.append(jnp.sqrt(norm))
        gram = gram * (1.0 / scales[c])
        root[c] = gram
        store(s, c, slice(None), gram)

    def advance(step, some):
        for c, rows in some:
            x = 2.25 * ahead[c, rows] + multiply(r.at[step % 2], w.at[step % 2], c, rows)
            ahead[c, rows] = x
            if step < PAIRS - 1:
                store(w.at[(step + 1) % 2], c, rows, x)

    gaps = [parts[i::4] for i in range(4)]
    for step in range(PAIRS):
        for c, rows in parts:
            x = multiply(s, s, c, rows)
            y = root[c, rows]
            store(p, c, rows, x)
            store(u, c, rows, 0.0625 * x - 0.5625 * y)
            mixed[c, rows] = 1.6875 * x - 2.4375 * y
        if step > 0:
            advance(step - 1, gaps[0])
        for c, rows in parts:
            store(r.at[step % 2], c, rows, mixed[c, rows] + multiply(u, p, c, rows))
        if step > 0:
            advance(step - 1, gaps[1])
        if step < PAIRS - 1:
            for c, rows in parts:
                x = 2.25 * root[c, rows] + multiply(r.at[step % 2], s, c, rows)
                store(t, c, rows, x)
                mixed[c, rows] = 2.25 * x
        if step > 0:
            advance(step - 1, gaps[2])
        if step < PAIRS - 1:
            for c, rows in parts:
                x = mixed[c, rows] + multiply(t, r.at[step % 2], c, rows)
                root[c, rows] = x
                store(s, c, rows, x)
        if step > 0:
            advance(step - 1, gaps[3])
    advance(PAIRS - 1, parts)
    for c in every:
        x = ahead[c]
        inner = jnp.sum(x * forces[c], axis=1, keepdims=True)
        shift = jnp.sum(x * inner, axis=0, keepdims=True) / scales[c]
        result = means[c] + shift + x * jnp.sqrt(spread / scales[c])
        for k in range(groups):
            outs[k][c] = result[k * local : (k + 1) * local]


def sizes_of(columns, local, entries, members):
    full = pltpu.VMEM((columns, members, members), jnp.float32)
    pair = pltpu.VMEM((2, columns, members, members), jnp.bfloat16)
    two = pltpu.VMEM((2, 2, columns, members, members), jnp.bfloat16)
    ahead = pltpu.VMEM((columns, members, entries), jnp.float32)
    factor = pltpu.VMEM((2, 2, columns, members, entries), jnp.bfloat16)
    return [full, full, ahead, pair, pair, pair, pair, two, factor]


def inner_analysis(me_ref, after_ref, count_ref, where_ref, value_ref, rinv_ref, *refs):
    del after_ref
    *ins, whole_ref, done_ref, obs_ref = refs[:-SCRATCH]
    groups = len(ins)
    half = ins[0].shape[0]
    done_ref[...] = jnp.zeros_like(done_ref)
    outs = [whole_ref.at[source(me_ref[0], k, groups)] for k in issue_order(groups)]
    first = inner_start(me_ref[0] * half, where_ref.shape[0] // 4)
    observe(first, count_ref, where_ref, value_ref, rinv_ref, obs_ref)
    analyse_kernel(obs_ref, ins, outs, *refs[-SCRATCH:])


def outer_analysis(me_ref, after_ref, count_ref, where_ref, value_ref, rinv_ref, whole_ref, *refs):
    del after_ref
    *outs, obs_ref = refs[:-SCRATCH]
    groups = len(outs)
    half = outs[0].shape[0]
    ins = [whole_ref.at[target(me_ref[0], k, groups)] for k in issue_order(groups)]
    first = outer_start(me_ref[0] * half, where_ref.shape[0] // 4)
    observe(first, count_ref, where_ref, value_ref, rinv_ref, obs_ref)
    analyse_kernel(obs_ref, ins, outs, *refs[-SCRATCH:])


def body(background, diffusion, advection, obs_where, obs_count, obs_value, obs_rinv):
    local, columns, entries = background.shape
    groups = lax.axis_size("mem")
    tiles = lax.axis_size("tile")
    half = columns // groups // 2
    size = background.size
    block = jax.ShapeDtypeStruct((half, local, entries), jnp.float32)
    whole = jax.ShapeDtypeStruct((groups, half, local, entries), jnp.float32)
    rest = jax.ShapeDtypeStruct((2, columns // 4 + 2, local, entries), jnp.float32)
    edge = jax.ShapeDtypeStruct((2, local, entries), jnp.float32)
    me = lax.axis_index("mem")[None].astype(jnp.int32)
    pieces = len(pieces_of(local))
    width = min(columns, 8)
    token = jax.ShapeDtypeStruct((8, entries), jnp.float32)
    scratch = [pltpu.VMEM((half, 8, entries), jnp.float32)] + sizes_of(half, local, entries, groups * local)
    flops = half * 180 * (groups * local) ** 2 * entries
    numbers = jax.ShapeDtypeStruct((8, entries), jnp.float32)

    low, high, numbers, counts = call(
        edge_kernel,
        [edge, edge, numbers, jax.ShapeDtypeStruct(obs_count.shape, jnp.int32)],
        0,
        16 * local * width * entries,
        in_specs=[HBM] * 4,
        scratch_shapes=[
            pltpu.VMEM((2, local, width, entries), jnp.float32),
            pltpu.SemaphoreType.DMA((5,)),
        ],
    )(*(in_hbm(x) for x in (background, diffusion, advection, obs_count)))
    before = lax.ppermute(high, "tile", [(i, (i + 1) % tiles) for i in range(tiles)])
    after = lax.ppermute(low, "tile", [((i + 1) % tiles, i) for i in range(tiles)])
    *inner, rest = call(
        inner_kernel,
        [block] * groups + [rest],
        20 * size,
        8 * size,
        in_specs=[SMEM] + [VMEM] * 2,
        scratch_shapes=[pltpu.VMEM((columns, local, entries), jnp.float32)],
    )(me, background, numbers)
    inner = exchange(inner)
    slots = (counts, obs_where[0], obs_value[0], obs_rinv[0])
    outer, done = call(
        outer_kernel,
        [whole, token],
        20 * size,
        8 * size,
        in_specs=[VMEM] * 4,
    )(rest, before, after, numbers)
    outer = lax.all_to_all(outer, "mem", split_axis=0, concat_axis=0, tiled=True)

    inner, done = call(
        inner_analysis,
        [whole, token],
        flops,
        4 * size,
        in_specs=[SMEM] + [VMEM] * (groups + 5),
        scratch_shapes=scratch,
    )(me, done, *slots, *inner)
    inner = lax.all_to_all(inner, "mem", split_axis=0, concat_axis=0, tiled=True)
    outer = call(
        outer_analysis,
        [block] * groups,
        flops,
        4 * size,
        in_specs=[SMEM] + [VMEM] * 6,
        scratch_shapes=scratch,
    )(me, done, *slots, outer)
    outer = exchange(outer)
    result = jax.ShapeDtypeStruct(background.shape, jnp.float32)
    made = call(
        inner_join_kernel,
        result,
        size,
        4 * size,
        in_specs=[VMEM, VMEM],
        out_specs=HBM,
        scratch_shapes=[
            pltpu.VMEM((local, groups * half, entries), jnp.float32),
            pltpu.SemaphoreType.DMA((pieces,)),
        ],
    )(outer[2], inner)
    return call(
        outer_join_kernel,
        result,
        size,
        4 * size,
        in_specs=[SMEM, HBM] + [VMEM] * groups,
        out_specs=HBM,
        scratch_shapes=[
            pltpu.VMEM((groups * half, local, entries), jnp.float32),
            pltpu.VMEM((local, groups * half, entries), jnp.float32),
            pltpu.SemaphoreType.DMA((2 * pieces,)),
        ],
        input_output_aliases={1: 0},
    )(me, made, *outer)


def solution(mesh):
    return jax.shard_map(
        body,
        mesh=mesh,
        in_specs=(
            P("mem", "tile", None),
            P(),
            P(),
            P("tile", None, None),
            P("tile", None),
            P("tile", None, None),
            P("tile", None, None),
        ),
        out_specs=P("mem", "tile", None),
        check_vma=False,
    )
```

```python
import jax
import jax.numpy as jnp
from jax import lax
from jax.experimental import pallas as pl
from jax.experimental.pallas import tpu as pltpu
from jax.sharding import PartitionSpec as P

PAIRS = 6
SCRATCH = 9
MIB = 1024 * 1024
SMEM = pl.BlockSpec(memory_space=pltpu.SMEM)
VMEM = pl.BlockSpec(memory_space=pltpu.VMEM)
HBM = pl.BlockSpec(memory_space=pltpu.HBM)


def call(kernel, out_shape, flops, moved, vmem=48 * MIB, **options):
    return pl.pallas_call(
        kernel,
        out_shape=out_shape,
        compiler_params=pltpu.CompilerParams(vmem_limit_bytes=vmem),
        cost_estimate=pl.CostEstimate(flops=flops, bytes_accessed=moved, transcendentals=0),
        **options,
    )


def in_hbm(x):
    return pltpu.with_memory_space_constraint(x, pltpu.HBM)


def chips_from(chip, step, chips):
    if chips & (chips - 1) == 0:
        return chip ^ step
    return (chip + step) % chips if isinstance(chip, int) else lax.rem(chip + step, chips)


def step_of(core, round, chips):
    steps = sorted(range(1, chips), key=lambda step: (-step.bit_count(), step))
    near, far = steps[round - 1], steps[round % len(steps)]
    if isinstance(core, int):
        return far if core else near
    return jnp.where(core == 1, far, near)


def target(me, block, groups):
    round, other = block
    chip = chips_from(me // 2, step_of(me & 1, round, groups // 2), groups // 2) if round else me // 2
    return 2 * chip + (me & 1 ^ other)


def source(me, block, groups):
    round, other = block
    chips = groups // 2
    core = me & 1 ^ other
    if not round:
        return 2 * (me // 2) + core
    step = step_of(core, round, chips)
    return 2 * chips_from(me // 2, step if chips & (chips - 1) == 0 else chips - step, chips) + core


def issue_order(groups):
    return [(0, 1)] + [(round, other) for round in range(1, groups // 2) for other in range(2)] + [(0, 0)]


def exchange(blocks):
    groups = len(blocks)
    out = []
    for k, block in zip(issue_order(groups), blocks):
        pairs = [(i, target(i, k, groups)) for i in range(groups)]
        out.append(lax.ppermute(block, "mem", pairs) if k != (0, 0) else block)
    return out


def split(x, parts):
    out = []
    for _ in range(parts):
        part = x.astype(jnp.bfloat16)
        out.append(part)
        x = x - part.astype(jnp.float32)
    return out


def store(ref, c, rows, x):
    for i, part in enumerate(split(x, 2)):
        ref[i, c, rows] = part


def multiply(a_ref, b_ref, c, rows):
    lhs = jnp.concatenate([a_ref[0, c, rows], a_ref[1, c, rows], a_ref[0, c, rows]], axis=1)
    rhs = jnp.concatenate([b_ref[0, c], b_ref[0, c], b_ref[1, c]], axis=0)
    return jnp.dot(lhs, rhs, preferred_element_type=jnp.float32)


def square_by_rows(parts):
    p0, p1, p2 = parts
    lhs = jnp.concatenate([p2, p0, p1, p1, p0, p0], axis=1)
    rhs = jnp.concatenate([p0, p2, p1, p0, p1, p0], axis=1)
    return lax.dot_general(lhs, rhs, (((1,), (1,)), ((), ())), preferred_element_type=jnp.float32)


def stencil(padded, diffusion, advection):
    middle = padded[1:-1]
    left = padded[:-2]
    right = padded[2:]
    return middle + diffusion * (left - 2.0 * middle + right) + advection * (0.5 * (left - right))


def inner_start(place, quarter):
    return place + quarter


def outer_start(place, quarter):
    return jnp.where(place < quarter, place, place + 2 * quarter)


def pieces_of(members):
    rows = 8 if members % 8 == 0 else members
    return [pl.ds(first, rows) for first in range(0, members, rows)]


def edge_kernel(state_ref, diff_ref, adv_ref, count_ref, low_ref, high_ref, num_ref, counts_ref, held_ref, sems):
    columns = state_ref.shape[1]
    width = held_ref.shape[2]
    reads = [
        pltpu.make_async_copy(state_ref.at[:, pl.ds(first, width)], held_ref.at[i], sems.at[i])
        for i, first in enumerate((0, columns - width))
    ]
    reads.append(pltpu.make_async_copy(diff_ref, num_ref.at[0], sems.at[2]))
    reads.append(pltpu.make_async_copy(adv_ref, num_ref.at[1], sems.at[3]))
    reads.append(pltpu.make_async_copy(count_ref, counts_ref, sems.at[4]))
    for copy in reads:
        copy.start()
    reads[0].wait()
    for i in range(2):
        low_ref[i] = held_ref[0, :, i]
    reads[1].wait()
    for i in range(2):
        high_ref[i] = held_ref[1, :, width - 2 + i]
    for copy in reads[2:]:
        copy.wait()


def inner_kernel(me_ref, state_ref, num_ref, *refs):
    *outs, rest_ref, turned_ref = refs
    groups = len(outs)
    half = outs[0].shape[0]
    columns = state_ref.shape[1]
    quarter = columns // 4
    turned_ref[...] = jnp.swapaxes(state_ref[...], 0, 1)
    diffusion = num_ref[0:1][None]
    advection = num_ref[1:2][None]
    for k, out_ref in zip(issue_order(groups), outs):
        x = turned_ref[pl.ds(target(me_ref[0], k, groups) * half + (quarter - 2), half + 4)]
        out_ref[...] = stencil(stencil(x, diffusion, advection), diffusion, advection)
    rest_ref[0] = turned_ref[: quarter + 2]
    rest_ref[1] = turned_ref[columns - quarter - 2 :]


def outer_kernel(rest_ref, before_ref, after_ref, num_ref, out_ref, done_ref):
    done_ref[...] = jnp.zeros_like(done_ref)
    diffusion = num_ref[0:1][None]
    advection = num_ref[1:2][None]
    low = jnp.concatenate([before_ref[...], rest_ref[0]], axis=0)
    high = jnp.concatenate([rest_ref[1], after_ref[...]], axis=0)
    low = stencil(stencil(low, diffusion, advection), diffusion, advection)
    high = stencil(stencil(high, diffusion, advection), diffusion, advection)
    out_ref[...] = jnp.concatenate([low, high], axis=0).reshape(out_ref.shape)


def inner_join_kernel(after_ref, inner_ref, out_ref, made_ref, sems):
    del after_ref
    members, columns, entries = out_ref.shape
    groups, half, _, _ = inner_ref.shape
    quarter = columns // 4
    writes = []
    for i, part in enumerate(pieces_of(members)):
        x = inner_ref[:, :, part].reshape(groups * half, part.size, entries)
        made_ref[part] = jnp.swapaxes(x, 0, 1)
        copy = pltpu.make_async_copy(
            made_ref.at[part], out_ref.at[part, pl.ds(quarter, columns - 2 * quarter)], sems.at[i]
        )
        copy.start()
        writes.append(copy)
    for copy in writes:
        copy.wait()


def outer_join_kernel(me_ref, held_ref, *refs):
    del held_ref
    *outer, out_ref, turned_ref, made_ref, sems = refs
    members, columns, _ = out_ref.shape
    groups = len(outer)
    half = outer[0].shape[0]
    quarter = columns // 4
    writes = []
    for i, part in enumerate(pieces_of(members)):
        for k, block in zip(issue_order(groups), outer):
            turned_ref[pl.ds(source(me_ref[0], k, groups) * half, half), part] = block[:, part]
        made_ref[part] = jnp.swapaxes(turned_ref[:, part], 0, 1)
        for side in range(2):
            copy = pltpu.make_async_copy(
                made_ref.at[part, pl.ds(side * quarter, quarter)],
                out_ref.at[part, pl.ds(side * (columns - quarter), quarter)],
                sems.at[2 * i + side],
            )
            copy.start()
            writes.append(copy)
    for copy in writes:
        copy.wait()


def observe(first, count_ref, where_ref, value_ref, rinv_ref, out_ref):
    columns, _, entries = out_ref.shape
    slots = where_ref.shape[1]
    column = lax.broadcasted_iota(jnp.int32, count_ref.shape, 1)
    slot = lax.broadcasted_iota(jnp.int32, (1, slots), 1)
    row = lax.broadcasted_iota(jnp.int32, (16, slots), 0)
    entry = lax.broadcasted_iota(jnp.int32, (entries, slots), 0)
    for c in range(columns):
        at = first + c
        count = jnp.sum(jnp.where(column == at, count_ref[...], 0), axis=1, keepdims=True)
        weight = jnp.where(slot < count, rinv_ref[pl.ds(at, 1), :], 0.0)
        lhs = jnp.zeros((16, slots), jnp.float32)
        for line, values in ((0, weight), (3, weight * value_ref[pl.ds(at, 1), :])):
            for k, part in enumerate(split(values, 3)):
                lhs = jnp.where(row == line + k, part.astype(jnp.float32), lhs)
        onehot = (entry == where_ref[pl.ds(at, 1), :]).astype(jnp.float32).astype(jnp.bfloat16)
        sums = lax.dot_general(
            lhs.astype(jnp.bfloat16), onehot, (((1,), (1,)), ((), ())), preferred_element_type=jnp.float32
        )
        out_ref[c, 0:1] = sums[0:1] + (sums[1:2] + sums[2:3])
        out_ref[c, 1:2] = sums[3:4] + (sums[4:5] + sums[5:6])


def analyse_kernel(obs_ref, states, outs, root, mixed, ahead, s, p, u, t, r, w):
    groups = len(outs)
    columns, local, entries = outs[0].shape
    members = groups * local
    spread = members - 1.0
    every = range(columns)
    parts = [(c, pl.ds(half, members // 2)) for c in every for half in (0, members // 2)]
    rows = lax.broadcasted_iota(jnp.int32, (members, members), 0)
    cols = lax.broadcasted_iota(jnp.int32, (members, members), 1)
    means, forces, scales, grams = [], [], [], []
    for c in every:
        x = jnp.concatenate([ref[c] for ref in states], axis=0)
        mean = jnp.sum(x, axis=0, keepdims=True) * (1.0 / members)
        anomaly = x - mean
        total = obs_ref[c, 0:1]
        forces.append(obs_ref[c, 1:2] - total * mean)
        means.append(mean)
        grams.append(square_by_rows(split(anomaly * jnp.sqrt(total), 3)))
        ahead[c] = anomaly
        store(w.at[0], c, slice(None), anomaly)
    for c in every:
        gram = grams[c] + jnp.where(rows == cols, spread, 0.0)
        norm = jnp.sum(jnp.sum(gram * gram, axis=0, keepdims=True), axis=1, keepdims=True)
        scales.append(jnp.sqrt(norm))
        gram = gram * (1.0 / scales[c])
        root[c] = gram
        store(s, c, slice(None), gram)

    def advance(step, some):
        for c, rows in some:
            x = 2.25 * ahead[c, rows] + multiply(r.at[step % 2], w.at[step % 2], c, rows)
            ahead[c, rows] = x
            if step < PAIRS - 1:
                store(w.at[(step + 1) % 2], c, rows, x)

    gaps = [parts[i::4] for i in range(4)]
    for step in range(PAIRS):
        for c, rows in parts:
            x = multiply(s, s, c, rows)
            y = root[c, rows]
            store(p, c, rows, x)
            store(u, c, rows, 0.0625 * x - 0.5625 * y)
            mixed[c, rows] = 1.6875 * x - 2.4375 * y
        if step > 0:
            advance(step - 1, gaps[0])
        for c, rows in parts:
            store(r.at[step % 2], c, rows, mixed[c, rows] + multiply(u, p, c, rows))
        if step > 0:
            advance(step - 1, gaps[1])
        if step < PAIRS - 1:
            for c, rows in parts:
                x = 2.25 * root[c, rows] + multiply(r.at[step % 2], s, c, rows)
                store(t, c, rows, x)
                mixed[c, rows] = 2.25 * x
        if step > 0:
            advance(step - 1, gaps[2])
        if step < PAIRS - 1:
            for c, rows in parts:
                x = mixed[c, rows] + multiply(t, r.at[step % 2], c, rows)
                root[c, rows] = x
                store(s, c, rows, x)
        if step > 0:
            advance(step - 1, gaps[3])
    advance(PAIRS - 1, parts)
    for c in every:
        x = ahead[c]
        inner = jnp.sum(x * forces[c], axis=1, keepdims=True)
        shift = jnp.sum(x * inner, axis=0, keepdims=True) / scales[c]
        result = means[c] + shift + x * jnp.sqrt(spread / scales[c])
        for k in range(groups):
            outs[k][c] = result[k * local : (k + 1) * local]


def sizes_of(columns, local, entries, members):
    full = pltpu.VMEM((columns, members, members), jnp.float32)
    pair = pltpu.VMEM((2, columns, members, members), jnp.bfloat16)
    two = pltpu.VMEM((2, 2, columns, members, members), jnp.bfloat16)
    ahead = pltpu.VMEM((columns, members, entries), jnp.float32)
    factor = pltpu.VMEM((2, 2, columns, members, entries), jnp.bfloat16)
    return [full, full, ahead, pair, pair, pair, pair, two, factor]


def inner_analysis(me_ref, after_ref, count_ref, where_ref, value_ref, rinv_ref, *refs):
    del after_ref
    *ins, whole_ref, done_ref, obs_ref = refs[:-SCRATCH]
    groups = len(ins)
    half = ins[0].shape[0]
    done_ref[...] = jnp.zeros_like(done_ref)
    outs = [whole_ref.at[source(me_ref[0], k, groups)] for k in issue_order(groups)]
    first = inner_start(me_ref[0] * half, where_ref.shape[0] // 4)
    observe(first, count_ref, where_ref, value_ref, rinv_ref, obs_ref)
    analyse_kernel(obs_ref, ins, outs, *refs[-SCRATCH:])


def outer_analysis(me_ref, after_ref, count_ref, where_ref, value_ref, rinv_ref, whole_ref, *refs):
    del after_ref
    *outs, obs_ref = refs[:-SCRATCH]
    groups = len(outs)
    half = outs[0].shape[0]
    ins = [whole_ref.at[target(me_ref[0], k, groups)] for k in issue_order(groups)]
    first = outer_start(me_ref[0] * half, where_ref.shape[0] // 4)
    observe(first, count_ref, where_ref, value_ref, rinv_ref, obs_ref)
    analyse_kernel(obs_ref, ins, outs, *refs[-SCRATCH:])


def body(background, diffusion, advection, obs_where, obs_count, obs_value, obs_rinv):
    local, columns, entries = background.shape
    groups = lax.axis_size("mem")
    tiles = lax.axis_size("tile")
    half = columns // groups // 2
    size = background.size
    block = jax.ShapeDtypeStruct((half, local, entries), jnp.float32)
    whole = jax.ShapeDtypeStruct((groups, half, local, entries), jnp.float32)
    rest = jax.ShapeDtypeStruct((2, columns // 4 + 2, local, entries), jnp.float32)
    edge = jax.ShapeDtypeStruct((2, local, entries), jnp.float32)
    me = lax.axis_index("mem")[None].astype(jnp.int32)
    pieces = len(pieces_of(local))
    width = min(columns, 8)
    token = jax.ShapeDtypeStruct((8, entries), jnp.float32)
    scratch = [pltpu.VMEM((half, 8, entries), jnp.float32)] + sizes_of(half, local, entries, groups * local)
    flops = half * 180 * (groups * local) ** 2 * entries
    numbers = jax.ShapeDtypeStruct((8, entries), jnp.float32)

    low, high, numbers, counts = call(
        edge_kernel,
        [edge, edge, numbers, jax.ShapeDtypeStruct(obs_count.shape, jnp.int32)],
        0,
        16 * local * width * entries,
        in_specs=[HBM] * 4,
        scratch_shapes=[
            pltpu.VMEM((2, local, width, entries), jnp.float32),
            pltpu.SemaphoreType.DMA((5,)),
        ],
    )(*(in_hbm(x) for x in (background, diffusion, advection, obs_count)))
    before = lax.ppermute(high, "tile", [(i, (i + 1) % tiles) for i in range(tiles)])
    after = lax.ppermute(low, "tile", [((i + 1) % tiles, i) for i in range(tiles)])
    *inner, rest = call(
        inner_kernel,
        [block] * groups + [rest],
        20 * size,
        8 * size,
        in_specs=[SMEM] + [VMEM] * 2,
        scratch_shapes=[pltpu.VMEM((columns, local, entries), jnp.float32)],
    )(me, background, numbers)
    inner = exchange(inner)
    slots = (counts, obs_where[0], obs_value[0], obs_rinv[0])
    outer, done = call(
        outer_kernel,
        [whole, token],
        20 * size,
        8 * size,
        in_specs=[VMEM] * 4,
    )(rest, before, after, numbers)
    outer = lax.all_to_all(outer, "mem", split_axis=0, concat_axis=0, tiled=True)

    inner, done = call(
        inner_analysis,
        [whole, token],
        flops,
        4 * size,
        in_specs=[SMEM] + [VMEM] * (groups + 5),
        scratch_shapes=scratch,
    )(me, done, *slots, *inner)
    inner = lax.all_to_all(inner, "mem", split_axis=0, concat_axis=0, tiled=True)
    outer = call(
        outer_analysis,
        [block] * groups,
        flops,
        4 * size,
        in_specs=[SMEM] + [VMEM] * 6,
        scratch_shapes=scratch,
    )(me, done, *slots, outer)
    outer = exchange(outer)
    result = jax.ShapeDtypeStruct(background.shape, jnp.float32)
    made = call(
        inner_join_kernel,
        result,
        size,
        4 * size,
        in_specs=[VMEM, VMEM],
        out_specs=HBM,
        scratch_shapes=[
            pltpu.VMEM((local, groups * half, entries), jnp.float32),
            pltpu.SemaphoreType.DMA((pieces,)),
        ],
    )(outer[2], inner)
    return call(
        outer_join_kernel,
        result,
        size,
        4 * size,
        in_specs=[SMEM, HBM] + [VMEM] * groups,
        out_specs=HBM,
        scratch_shapes=[
            pltpu.VMEM((groups * half, local, entries), jnp.float32),
            pltpu.VMEM((local, groups * half, entries), jnp.float32),
            pltpu.SemaphoreType.DMA((2 * pieces,)),
        ],
        input_output_aliases={1: 0},
    )(me, made, *outer)


def solution(mesh):
    return jax.shard_map(
        body,
        mesh=mesh,
        in_specs=(
            P("mem", "tile", None),
            P(),
            P(),
            P("tile", None, None),
            P("tile", None),
            P("tile", None, None),
            P("tile", None, None),
        ),
        out_specs=P("mem", "tile", None),
        check_vma=False,
    )
```

```python
import jax
import jax.numpy as jnp
from jax import lax
from jax.experimental import pallas as pl
from jax.experimental.pallas import tpu as pltpu
from jax.sharding import PartitionSpec as P

PAIRS = 6
SCRATCH = 9
MIB = 1024 * 1024
SMEM = pl.BlockSpec(memory_space=pltpu.SMEM)
VMEM = pl.BlockSpec(memory_space=pltpu.VMEM)
HBM = pl.BlockSpec(memory_space=pltpu.HBM)


def call(kernel, out_shape, flops, moved, vmem=48 * MIB, **options):
    return pl.pallas_call(
        kernel,
        out_shape=out_shape,
        compiler_params=pltpu.CompilerParams(vmem_limit_bytes=vmem),
        cost_estimate=pl.CostEstimate(flops=flops, bytes_accessed=moved, transcendentals=0),
        **options,
    )


def in_hbm(x):
    return pltpu.with_memory_space_constraint(x, pltpu.HBM)


def target(me, k, groups):
    if groups & (groups - 1) == 0:
        return me ^ k
    return lax.rem(me + k, groups)


def source(me, k, groups):
    if groups & (groups - 1) == 0:
        return me ^ k
    return lax.rem(me + groups - k, groups)


def issue_order(groups):
    return sorted(range(1, groups), key=lambda k: (k != 1, -(k // 2).bit_count(), k)) + [0]


def exchange(blocks):
    groups = len(blocks)
    out = []
    for k, block in zip(issue_order(groups), blocks):
        pairs = [(i, i ^ k if groups & (groups - 1) == 0 else (i + k) % groups) for i in range(groups)]
        out.append(lax.ppermute(block, "mem", pairs) if k else block)
    return out


def split(x, parts):
    out = []
    for _ in range(parts):
        part = x.astype(jnp.bfloat16)
        out.append(part)
        x = x - part.astype(jnp.float32)
    return out


def store(ref, c, rows, x):
    for i, part in enumerate(split(x, 2)):
        ref[i, c, rows] = part


def multiply(a_ref, b_ref, c, rows):
    lhs = jnp.concatenate([a_ref[0, c, rows], a_ref[1, c, rows], a_ref[0, c, rows]], axis=1)
    rhs = jnp.concatenate([b_ref[0, c], b_ref[0, c], b_ref[1, c]], axis=0)
    return jnp.dot(lhs, rhs, preferred_element_type=jnp.float32)


def square_by_rows(parts):
    p0, p1, p2 = parts
    lhs = jnp.concatenate([p2, p0, p1, p1, p0, p0], axis=1)
    rhs = jnp.concatenate([p0, p2, p1, p0, p1, p0], axis=1)
    return lax.dot_general(lhs, rhs, (((1,), (1,)), ((), ())), preferred_element_type=jnp.float32)


def stencil(padded, diffusion, advection):
    middle = padded[1:-1]
    left = padded[:-2]
    right = padded[2:]
    return middle + diffusion * (left - 2.0 * middle + right) + advection * (0.5 * (left - right))


def inner_start(place, quarter):
    return place + quarter


def outer_start(place, quarter):
    return jnp.where(place < quarter, place, place + 2 * quarter)


def pieces_of(members):
    rows = 8 if members % 8 == 0 else members
    return [pl.ds(first, rows) for first in range(0, members, rows)]


def edge_kernel(state_ref, diff_ref, adv_ref, count_ref, low_ref, high_ref, num_ref, counts_ref, held_ref, sems):
    columns = state_ref.shape[1]
    width = held_ref.shape[2]
    reads = [
        pltpu.make_async_copy(state_ref.at[:, pl.ds(first, width)], held_ref.at[i], sems.at[i])
        for i, first in enumerate((0, columns - width))
    ]
    reads.append(pltpu.make_async_copy(diff_ref, num_ref.at[0], sems.at[2]))
    reads.append(pltpu.make_async_copy(adv_ref, num_ref.at[1], sems.at[3]))
    reads.append(pltpu.make_async_copy(count_ref, counts_ref, sems.at[4]))
    for copy in reads:
        copy.start()
    reads[0].wait()
    for i in range(2):
        low_ref[i] = held_ref[0, :, i]
    reads[1].wait()
    for i in range(2):
        high_ref[i] = held_ref[1, :, width - 2 + i]
    for copy in reads[2:]:
        copy.wait()


def inner_kernel(me_ref, state_ref, num_ref, *refs):
    *outs, rest_ref, turned_ref = refs
    groups = len(outs)
    half = outs[0].shape[0]
    columns = state_ref.shape[1]
    quarter = columns // 4
    turned_ref[...] = jnp.swapaxes(state_ref[...], 0, 1)
    diffusion = num_ref[0:1][None]
    advection = num_ref[1:2][None]
    for k, out_ref in zip(issue_order(groups), outs):
        x = turned_ref[pl.ds(target(me_ref[0], k, groups) * half + (quarter - 2), half + 4)]
        out_ref[...] = stencil(stencil(x, diffusion, advection), diffusion, advection)
    rest_ref[0] = turned_ref[: quarter + 2]
    rest_ref[1] = turned_ref[columns - quarter - 2 :]


def outer_kernel(rest_ref, before_ref, after_ref, num_ref, out_ref, done_ref, made_ref, sems):
    done_ref[...] = jnp.zeros_like(done_ref)
    groups, half, members, entries = out_ref.shape
    quarter = groups * half // 2
    owners = groups // sems.shape[0]
    diffusion = num_ref[0:1][None]
    advection = num_ref[1:2][None]
    low = jnp.concatenate([before_ref[...], rest_ref[0]], axis=0)
    high = jnp.concatenate([rest_ref[1], after_ref[...]], axis=0)
    writes = []
    for i in range(sems.shape[0]):
        first = i * owners * half
        padded, first = (low, first) if first < quarter else (high, first - quarter)
        x = padded[first : first + owners * half + 4]
        x = stencil(stencil(x, diffusion, advection), diffusion, advection)
        part = pl.ds(i * owners, owners)
        made_ref[part] = x.reshape(owners, half, members, entries)
        copy = pltpu.make_async_copy(made_ref.at[part], out_ref.at[part], sems.at[i])
        copy.start()
        writes.append(copy)
    for copy in writes:
        copy.wait()


def inner_join_kernel(after_ref, inner_ref, out_ref, made_ref, sems):
    del after_ref
    members, columns, entries = out_ref.shape
    groups, half, _, _ = inner_ref.shape
    quarter = columns // 4
    writes = []
    for i, part in enumerate(pieces_of(members)):
        x = inner_ref[:, :, part].reshape(groups * half, part.size, entries)
        made_ref[part] = jnp.swapaxes(x, 0, 1)
        copy = pltpu.make_async_copy(
            made_ref.at[part], out_ref.at[part, pl.ds(quarter, columns - 2 * quarter)], sems.at[i]
        )
        copy.start()
        writes.append(copy)
    for copy in writes:
        copy.wait()


def outer_join_kernel(me_ref, held_ref, *refs):
    del held_ref
    *outer, out_ref, turned_ref, made_ref, sems = refs
    members, columns, _ = out_ref.shape
    groups = len(outer)
    half = outer[0].shape[0]
    quarter = columns // 4
    writes = []
    for i, part in enumerate(pieces_of(members)):
        for k, block in zip(issue_order(groups), outer):
            turned_ref[pl.ds(source(me_ref[0], k, groups) * half, half), part] = block[:, part]
        made_ref[part] = jnp.swapaxes(turned_ref[:, part], 0, 1)
        for side in range(2):
            copy = pltpu.make_async_copy(
                made_ref.at[part, pl.ds(side * quarter, quarter)],
                out_ref.at[part, pl.ds(side * (columns - quarter), quarter)],
                sems.at[2 * i + side],
            )
            copy.start()
            writes.append(copy)
    for copy in writes:
        copy.wait()


def observe(first, count_ref, where_ref, value_ref, rinv_ref, out_ref):
    columns, _, entries = out_ref.shape
    slots = where_ref.shape[1]
    column = lax.broadcasted_iota(jnp.int32, count_ref.shape, 1)
    slot = lax.broadcasted_iota(jnp.int32, (1, slots), 1)
    row = lax.broadcasted_iota(jnp.int32, (16, slots), 0)
    entry = lax.broadcasted_iota(jnp.int32, (entries, slots), 0)
    for c in range(columns):
        at = first + c
        count = jnp.sum(jnp.where(column == at, count_ref[...], 0), axis=1, keepdims=True)
        weight = jnp.where(slot < count, rinv_ref[pl.ds(at, 1), :], 0.0)
        lhs = jnp.zeros((16, slots), jnp.float32)
        for line, values in ((0, weight), (3, weight * value_ref[pl.ds(at, 1), :])):
            for k, part in enumerate(split(values, 3)):
                lhs = jnp.where(row == line + k, part.astype(jnp.float32), lhs)
        onehot = (entry == where_ref[pl.ds(at, 1), :]).astype(jnp.float32).astype(jnp.bfloat16)
        sums = lax.dot_general(
            lhs.astype(jnp.bfloat16), onehot, (((1,), (1,)), ((), ())), preferred_element_type=jnp.float32
        )
        out_ref[c, 0:1] = sums[0:1] + (sums[1:2] + sums[2:3])
        out_ref[c, 1:2] = sums[3:4] + (sums[4:5] + sums[5:6])


def analyse_kernel(obs_ref, states, outs, root, mixed, ahead, s, p, u, t, r, w):
    groups = len(outs)
    columns, local, entries = outs[0].shape
    members = groups * local
    spread = members - 1.0
    every = range(columns)
    parts = [(c, pl.ds(half, members // 2)) for c in every for half in (0, members // 2)]
    rows = lax.broadcasted_iota(jnp.int32, (members, members), 0)
    cols = lax.broadcasted_iota(jnp.int32, (members, members), 1)
    means, forces, scales, grams = [], [], [], []
    for c in every:
        x = jnp.concatenate([ref[c] for ref in states], axis=0)
        mean = jnp.sum(x, axis=0, keepdims=True) * (1.0 / members)
        anomaly = x - mean
        total = obs_ref[c, 0:1]
        forces.append(obs_ref[c, 1:2] - total * mean)
        means.append(mean)
        grams.append(square_by_rows(split(anomaly * jnp.sqrt(total), 3)))
        ahead[c] = anomaly
        store(w.at[0], c, slice(None), anomaly)
    for c in every:
        gram = grams[c] + jnp.where(rows == cols, spread, 0.0)
        norm = jnp.sum(jnp.sum(gram * gram, axis=0, keepdims=True), axis=1, keepdims=True)
        scales.append(jnp.sqrt(norm))
        gram = gram * (1.0 / scales[c])
        root[c] = gram
        store(s, c, slice(None), gram)

    def advance(step, some):
        for c, rows in some:
            x = 2.25 * ahead[c, rows] + multiply(r.at[step % 2], w.at[step % 2], c, rows)
            ahead[c, rows] = x
            if step < PAIRS - 1:
                store(w.at[(step + 1) % 2], c, rows, x)

    gaps = [parts[i::4] for i in range(4)]
    for step in range(PAIRS):
        for c, rows in parts:
            x = multiply(s, s, c, rows)
            y = root[c, rows]
            store(p, c, rows, x)
            store(u, c, rows, 0.0625 * x - 0.5625 * y)
            mixed[c, rows] = 1.6875 * x - 2.4375 * y
        if step > 0:
            advance(step - 1, gaps[0])
        for c, rows in parts:
            store(r.at[step % 2], c, rows, mixed[c, rows] + multiply(u, p, c, rows))
        if step > 0:
            advance(step - 1, gaps[1])
        if step < PAIRS - 1:
            for c, rows in parts:
                x = 2.25 * root[c, rows] + multiply(r.at[step % 2], s, c, rows)
                store(t, c, rows, x)
                mixed[c, rows] = 2.25 * x
        if step > 0:
            advance(step - 1, gaps[2])
        if step < PAIRS - 1:
            for c, rows in parts:
                x = mixed[c, rows] + multiply(t, r.at[step % 2], c, rows)
                root[c, rows] = x
                store(s, c, rows, x)
        if step > 0:
            advance(step - 1, gaps[3])
    advance(PAIRS - 1, parts)
    for c in every:
        x = ahead[c]
        inner = jnp.sum(x * forces[c], axis=1, keepdims=True)
        shift = jnp.sum(x * inner, axis=0, keepdims=True) / scales[c]
        result = means[c] + shift + x * jnp.sqrt(spread / scales[c])
        for k in range(groups):
            outs[k][c] = result[k * local : (k + 1) * local]


def sizes_of(columns, local, entries, members):
    full = pltpu.VMEM((columns, members, members), jnp.float32)
    pair = pltpu.VMEM((2, columns, members, members), jnp.bfloat16)
    two = pltpu.VMEM((2, 2, columns, members, members), jnp.bfloat16)
    ahead = pltpu.VMEM((columns, members, entries), jnp.float32)
    factor = pltpu.VMEM((2, 2, columns, members, entries), jnp.bfloat16)
    return [full, full, ahead, pair, pair, pair, pair, two, factor]


def inner_analysis(me_ref, after_ref, count_ref, where_ref, value_ref, rinv_ref, *refs):
    del after_ref
    *ins, whole_ref, done_ref, obs_ref = refs[:-SCRATCH]
    groups = len(ins)
    half = ins[0].shape[0]
    done_ref[...] = jnp.zeros_like(done_ref)
    outs = [whole_ref.at[source(me_ref[0], k, groups)] for k in issue_order(groups)]
    first = inner_start(me_ref[0] * half, where_ref.shape[0] // 4)
    observe(first, count_ref, where_ref, value_ref, rinv_ref, obs_ref)
    analyse_kernel(obs_ref, ins, outs, *refs[-SCRATCH:])


def outer_analysis(me_ref, after_ref, count_ref, where_ref, value_ref, rinv_ref, whole_ref, *refs):
    del after_ref
    *outs, obs_ref = refs[:-SCRATCH]
    groups = len(outs)
    half = outs[0].shape[0]
    ins = [whole_ref.at[target(me_ref[0], k, groups)] for k in issue_order(groups)]
    first = outer_start(me_ref[0] * half, where_ref.shape[0] // 4)
    observe(first, count_ref, where_ref, value_ref, rinv_ref, obs_ref)
    analyse_kernel(obs_ref, ins, outs, *refs[-SCRATCH:])


def body(background, diffusion, advection, obs_where, obs_count, obs_value, obs_rinv):
    local, columns, entries = background.shape
    groups = lax.axis_size("mem")
    tiles = lax.axis_size("tile")
    half = columns // groups // 2
    size = background.size
    block = jax.ShapeDtypeStruct((half, local, entries), jnp.float32)
    whole = jax.ShapeDtypeStruct((groups, half, local, entries), jnp.float32)
    rest = jax.ShapeDtypeStruct((2, columns // 4 + 2, local, entries), jnp.float32)
    edge = jax.ShapeDtypeStruct((2, local, entries), jnp.float32)
    me = lax.axis_index("mem")[None].astype(jnp.int32)
    pieces = len(pieces_of(local))
    width = min(columns, 8)
    token = jax.ShapeDtypeStruct((8, entries), jnp.float32)
    scratch = [pltpu.VMEM((half, 8, entries), jnp.float32)] + sizes_of(half, local, entries, groups * local)
    flops = half * 180 * (groups * local) ** 2 * entries
    numbers = jax.ShapeDtypeStruct((8, entries), jnp.float32)

    low, high, numbers, counts = call(
        edge_kernel,
        [edge, edge, numbers, jax.ShapeDtypeStruct(obs_count.shape, jnp.int32)],
        0,
        16 * local * width * entries,
        in_specs=[HBM] * 4,
        scratch_shapes=[
            pltpu.VMEM((2, local, width, entries), jnp.float32),
            pltpu.SemaphoreType.DMA((5,)),
        ],
    )(*(in_hbm(x) for x in (background, diffusion, advection, obs_count)))
    before = lax.ppermute(high, "tile", [(i, (i + 1) % tiles) for i in range(tiles)])
    after = lax.ppermute(low, "tile", [((i + 1) % tiles, i) for i in range(tiles)])
    *inner, rest = call(
        inner_kernel,
        [block] * groups + [rest],
        20 * size,
        8 * size,
        in_specs=[SMEM] + [VMEM] * 2,
        scratch_shapes=[pltpu.VMEM((columns, local, entries), jnp.float32)],
    )(me, background, numbers)
    inner = exchange(inner)
    slots = (counts, obs_where[0], obs_value[0], obs_rinv[0])
    outer, done = call(
        outer_kernel,
        [whole, token],
        20 * size,
        8 * size,
        in_specs=[VMEM] * 4,
        out_specs=[HBM, VMEM],
        scratch_shapes=[
            pltpu.VMEM(whole.shape, jnp.float32),
            pltpu.SemaphoreType.DMA((4 if groups % 4 == 0 else 2,)),
        ],
    )(rest, before, after, numbers)
    outer = lax.all_to_all(outer, "mem", split_axis=0, concat_axis=0, tiled=True)

    inner, done = call(
        inner_analysis,
        [whole, token],
        flops,
        4 * size,
        in_specs=[SMEM] + [VMEM] * (groups + 5),
        scratch_shapes=scratch,
    )(me, done, *slots, *inner)
    inner = lax.all_to_all(inner, "mem", split_axis=0, concat_axis=0, tiled=True)
    outer = call(
        outer_analysis,
        [block] * groups,
        flops,
        4 * size,
        in_specs=[SMEM] + [VMEM] * 6,
        scratch_shapes=scratch,
    )(me, done, *slots, outer)
    outer = exchange(outer)
    result = jax.ShapeDtypeStruct(background.shape, jnp.float32)
    made = call(
        inner_join_kernel,
        result,
        size,
        4 * size,
        in_specs=[VMEM, VMEM],
        out_specs=HBM,
        scratch_shapes=[
            pltpu.VMEM((local, groups * half, entries), jnp.float32),
            pltpu.SemaphoreType.DMA((pieces,)),
        ],
    )(outer[2], inner)
    return call(
        outer_join_kernel,
        result,
        size,
        4 * size,
        in_specs=[SMEM, HBM] + [VMEM] * groups,
        out_specs=HBM,
        scratch_shapes=[
            pltpu.VMEM((groups * half, local, entries), jnp.float32),
            pltpu.VMEM((local, groups * half, entries), jnp.float32),
            pltpu.SemaphoreType.DMA((2 * pieces,)),
        ],
        input_output_aliases={1: 0},
    )(me, made, *outer)


def solution(mesh):
    return jax.shard_map(
        body,
        mesh=mesh,
        in_specs=(
            P("mem", "tile", None),
            P(),
            P(),
            P("tile", None, None),
            P("tile", None),
            P("tile", None, None),
            P("tile", None, None),
        ),
        out_specs=P("mem", "tile", None),
        check_vma=False,
    )
```

```python
import jax
import jax.numpy as jnp
from jax import lax
from jax.experimental import pallas as pl
from jax.experimental.pallas import tpu as pltpu
from jax.sharding import PartitionSpec as P

PAIRS = 6
SCRATCH = 9
MIB = 1024 * 1024
SMEM = pl.BlockSpec(memory_space=pltpu.SMEM)
VMEM = pl.BlockSpec(memory_space=pltpu.VMEM)
HBM = pl.BlockSpec(memory_space=pltpu.HBM)


def call(kernel, out_shape, flops, moved, vmem=48 * MIB, **options):
    return pl.pallas_call(
        kernel,
        out_shape=out_shape,
        compiler_params=pltpu.CompilerParams(vmem_limit_bytes=vmem),
        cost_estimate=pl.CostEstimate(flops=flops, bytes_accessed=moved, transcendentals=0),
        **options,
    )


def in_hbm(x):
    return pltpu.with_memory_space_constraint(x, pltpu.HBM)


def target(me, k, groups):
    if groups & (groups - 1) == 0:
        return me ^ k
    return lax.rem(me + k, groups)


def source(me, k, groups):
    if groups & (groups - 1) == 0:
        return me ^ k
    return lax.rem(me + groups - k, groups)


def issue_order(groups):
    return sorted(range(1, groups), key=lambda k: (k != 1, -(k // 2).bit_count(), k)) + [0]


def exchange(blocks):
    groups = len(blocks)
    out = []
    for k, block in zip(issue_order(groups), blocks):
        pairs = [(i, i ^ k if groups & (groups - 1) == 0 else (i + k) % groups) for i in range(groups)]
        out.append(lax.ppermute(block, "mem", pairs) if k else block)
    return out


def split(x, parts):
    out = []
    for _ in range(parts):
        part = x.astype(jnp.bfloat16)
        out.append(part)
        x = x - part.astype(jnp.float32)
    return out


def store(ref, c, rows, x):
    for i, part in enumerate(split(x, 2)):
        ref[i, c, rows] = part


def multiply(a_ref, b_ref, c, rows):
    lhs = jnp.concatenate([a_ref[0, c, rows], a_ref[1, c, rows], a_ref[0, c, rows]], axis=1)
    rhs = jnp.concatenate([b_ref[0, c], b_ref[0, c], b_ref[1, c]], axis=0)
    return jnp.dot(lhs, rhs, preferred_element_type=jnp.float32)


def square_by_rows(parts):
    p0, p1, p2 = parts
    lhs = jnp.concatenate([p2, p0, p1, p1, p0, p0], axis=1)
    rhs = jnp.concatenate([p0, p2, p1, p0, p1, p0], axis=1)
    return lax.dot_general(lhs, rhs, (((1,), (1,)), ((), ())), preferred_element_type=jnp.float32)


def stencil(padded, diffusion, advection):
    middle = padded[1:-1]
    left = padded[:-2]
    right = padded[2:]
    return middle + diffusion * (left - 2.0 * middle + right) + advection * (0.5 * (left - right))


def inner_start(place, quarter):
    return place + quarter


def outer_start(place, quarter):
    return jnp.where(place < quarter, place, place + 2 * quarter)


def pieces_of(members):
    rows = 8 if members % 8 == 0 else members
    return [pl.ds(first, rows) for first in range(0, members, rows)]


def edge_kernel(state_ref, diff_ref, adv_ref, count_ref, low_ref, high_ref, num_ref, counts_ref, held_ref, sems):
    columns = state_ref.shape[1]
    width = held_ref.shape[2]
    reads = [
        pltpu.make_async_copy(state_ref.at[:, pl.ds(first, width)], held_ref.at[i], sems.at[i])
        for i, first in enumerate((0, columns - width))
    ]
    reads.append(pltpu.make_async_copy(diff_ref, num_ref.at[0], sems.at[2]))
    reads.append(pltpu.make_async_copy(adv_ref, num_ref.at[1], sems.at[3]))
    reads.append(pltpu.make_async_copy(count_ref, counts_ref, sems.at[4]))
    for copy in reads:
        copy.start()
    reads[0].wait()
    for i in range(2):
        low_ref[i] = held_ref[0, :, i]
    reads[1].wait()
    for i in range(2):
        high_ref[i] = held_ref[1, :, width - 2 + i]
    for copy in reads[2:]:
        copy.wait()


def inner_kernel(me_ref, state_ref, num_ref, *refs):
    *outs, rest_ref, turned_ref = refs
    groups = len(outs)
    half = outs[0].shape[0]
    columns = state_ref.shape[1]
    quarter = columns // 4
    turned_ref[...] = jnp.swapaxes(state_ref[...], 0, 1)
    diffusion = num_ref[0:1][None]
    advection = num_ref[1:2][None]
    for k, out_ref in zip(issue_order(groups), outs):
        x = turned_ref[pl.ds(target(me_ref[0], k, groups) * half + (quarter - 2), half + 4)]
        out_ref[...] = stencil(stencil(x, diffusion, advection), diffusion, advection)
    rest_ref[0] = turned_ref[: quarter + 2]
    rest_ref[1] = turned_ref[columns - quarter - 2 :]


def outer_kernel(rest_ref, before_ref, after_ref, num_ref, out_ref, done_ref, made_ref, sems):
    done_ref[...] = jnp.zeros_like(done_ref)
    groups, half, members, entries = out_ref.shape
    quarter = groups * half // 2
    owners = groups // sems.shape[0]
    diffusion = num_ref[0:1][None]
    advection = num_ref[1:2][None]
    low = jnp.concatenate([before_ref[...], rest_ref[0]], axis=0)
    high = jnp.concatenate([rest_ref[1], after_ref[...]], axis=0)
    writes = []
    for i in range(sems.shape[0]):
        first = i * owners * half
        padded, first = (low, first) if first < quarter else (high, first - quarter)
        x = padded[first : first + owners * half + 4]
        x = stencil(stencil(x, diffusion, advection), diffusion, advection)
        part = pl.ds(i * owners, owners)
        made_ref[part] = x.reshape(owners, half, members, entries)
        copy = pltpu.make_async_copy(made_ref.at[part], out_ref.at[part], sems.at[i])
        copy.start()
        writes.append(copy)
    for copy in writes:
        copy.wait()


def inner_join_kernel(after_ref, inner_ref, out_ref, made_ref, sems):
    del after_ref
    members, columns, entries = out_ref.shape
    groups, half, _, _ = inner_ref.shape
    quarter = columns // 4
    writes = []
    for i, part in enumerate(pieces_of(members)):
        x = inner_ref[:, :, part].reshape(groups * half, part.size, entries)
        made_ref[part] = jnp.swapaxes(x, 0, 1)
        copy = pltpu.make_async_copy(
            made_ref.at[part], out_ref.at[part, pl.ds(quarter, columns - 2 * quarter)], sems.at[i]
        )
        copy.start()
        writes.append(copy)
    for copy in writes:
        copy.wait()


def outer_join_kernel(me_ref, held_ref, *refs):
    del held_ref
    *outer, out_ref, turned_ref, made_ref, sems = refs
    members, columns, _ = out_ref.shape
    groups = len(outer)
    half = outer[0].shape[0]
    quarter = columns // 4
    writes = []
    for i, part in enumerate(pieces_of(members)):
        for k, block in zip(issue_order(groups), outer):
            turned_ref[pl.ds(source(me_ref[0], k, groups) * half, half), part] = block[:, part]
        made_ref[part] = jnp.swapaxes(turned_ref[:, part], 0, 1)
        for side in range(2):
            copy = pltpu.make_async_copy(
                made_ref.at[part, pl.ds(side * quarter, quarter)],
                out_ref.at[part, pl.ds(side * (columns - quarter), quarter)],
                sems.at[2 * i + side],
            )
            copy.start()
            writes.append(copy)
    for copy in writes:
        copy.wait()


def observe(first, count_ref, where_ref, value_ref, rinv_ref, out_ref):
    columns, _, entries = out_ref.shape
    slots = where_ref.shape[1]
    column = lax.broadcasted_iota(jnp.int32, count_ref.shape, 1)
    slot = lax.broadcasted_iota(jnp.int32, (1, slots), 1)
    row = lax.broadcasted_iota(jnp.int32, (16, slots), 0)
    entry = lax.broadcasted_iota(jnp.int32, (entries, slots), 0)
    for c in range(columns):
        at = first + c
        count = jnp.sum(jnp.where(column == at, count_ref[...], 0), axis=1, keepdims=True)
        weight = jnp.where(slot < count, rinv_ref[pl.ds(at, 1), :], 0.0)
        lhs = jnp.zeros((16, slots), jnp.float32)
        for line, values in ((0, weight), (3, weight * value_ref[pl.ds(at, 1), :])):
            for k, part in enumerate(split(values, 3)):
                lhs = jnp.where(row == line + k, part.astype(jnp.float32), lhs)
        onehot = (entry == where_ref[pl.ds(at, 1), :]).astype(jnp.float32).astype(jnp.bfloat16)
        sums = lax.dot_general(
            lhs.astype(jnp.bfloat16), onehot, (((1,), (1,)), ((), ())), preferred_element_type=jnp.float32
        )
        out_ref[c, 0:1] = sums[0:1] + (sums[1:2] + sums[2:3])
        out_ref[c, 1:2] = sums[3:4] + (sums[4:5] + sums[5:6])


def analyse_kernel(obs_ref, states, outs, root, mixed, ahead, s, p, u, t, r, w):
    groups = len(outs)
    columns, local, entries = outs[0].shape
    members = groups * local
    spread = members - 1.0
    every = range(columns)
    parts = [(c, pl.ds(half, members // 2)) for c in every for half in (0, members // 2)]
    rows = lax.broadcasted_iota(jnp.int32, (members, members), 0)
    cols = lax.broadcasted_iota(jnp.int32, (members, members), 1)
    means, forces, scales, grams = [], [], [], []
    for c in every:
        x = jnp.concatenate([ref[c] for ref in states], axis=0)
        mean = jnp.sum(x, axis=0, keepdims=True) * (1.0 / members)
        anomaly = x - mean
        total = obs_ref[c, 0:1]
        forces.append(obs_ref[c, 1:2] - total * mean)
        means.append(mean)
        grams.append(square_by_rows(split(anomaly * jnp.sqrt(total), 3)))
        ahead[c] = anomaly
        store(w.at[0], c, slice(None), anomaly)
    for c in every:
        gram = grams[c] + jnp.where(rows == cols, spread, 0.0)
        norm = jnp.sum(jnp.sum(gram * gram, axis=0, keepdims=True), axis=1, keepdims=True)
        scales.append(jnp.sqrt(norm))
        gram = gram * (1.0 / scales[c])
        root[c] = gram
        store(s, c, slice(None), gram)

    def advance(step, some):
        for c, rows in some:
            x = 2.25 * ahead[c, rows] + multiply(r.at[step % 2], w.at[step % 2], c, rows)
            ahead[c, rows] = x
            if step < PAIRS - 1:
                store(w.at[(step + 1) % 2], c, rows, x)

    gaps = [parts[i::4] for i in range(4)]
    for step in range(PAIRS):
        for c, rows in parts:
            x = multiply(s, s, c, rows)
            y = root[c, rows]
            store(p, c, rows, x)
            store(u, c, rows, 0.0625 * x - 0.5625 * y)
            mixed[c, rows] = 1.6875 * x - 2.4375 * y
        if step > 0:
            advance(step - 1, gaps[0])
        for c, rows in parts:
            store(r.at[step % 2], c, rows, mixed[c, rows] + multiply(u, p, c, rows))
        if step > 0:
            advance(step - 1, gaps[1])
        if step < PAIRS - 1:
            for c, rows in parts:
                x = 2.25 * root[c, rows] + multiply(r.at[step % 2], s, c, rows)
                store(t, c, rows, x)
                mixed[c, rows] = 2.25 * x
        if step > 0:
            advance(step - 1, gaps[2])
        if step < PAIRS - 1:
            for c, rows in parts:
                x = mixed[c, rows] + multiply(t, r.at[step % 2], c, rows)
                root[c, rows] = x
                store(s, c, rows, x)
        if step > 0:
            advance(step - 1, gaps[3])
    advance(PAIRS - 1, parts)
    for c in every:
        x = ahead[c]
        inner = jnp.sum(x * forces[c], axis=1, keepdims=True)
        shift = jnp.sum(x * inner, axis=0, keepdims=True) / scales[c]
        result = means[c] + shift + x * jnp.sqrt(spread / scales[c])
        for k in range(groups):
            outs[k][c] = result[k * local : (k + 1) * local]


def sizes_of(columns, local, entries, members):
    full = pltpu.VMEM((columns, members, members), jnp.float32)
    pair = pltpu.VMEM((2, columns, members, members), jnp.bfloat16)
    two = pltpu.VMEM((2, 2, columns, members, members), jnp.bfloat16)
    ahead = pltpu.VMEM((columns, members, entries), jnp.float32)
    factor = pltpu.VMEM((2, 2, columns, members, entries), jnp.bfloat16)
    return [full, full, ahead, pair, pair, pair, pair, two, factor]


def inner_analysis(me_ref, after_ref, count_ref, where_ref, value_ref, rinv_ref, *refs):
    del after_ref
    *ins, whole_ref, done_ref, obs_ref = refs[:-SCRATCH]
    groups = len(ins)
    half = ins[0].shape[0]
    done_ref[...] = jnp.zeros_like(done_ref)
    outs = [whole_ref.at[source(me_ref[0], k, groups)] for k in issue_order(groups)]
    first = inner_start(me_ref[0] * half, where_ref.shape[0] // 4)
    observe(first, count_ref, where_ref, value_ref, rinv_ref, obs_ref)
    analyse_kernel(obs_ref, ins, outs, *refs[-SCRATCH:])


def outer_observations(me_ref, after_ref, count_ref, where_ref, value_ref, rinv_ref, out_ref):
    del after_ref
    first = outer_start(me_ref[0] * out_ref.shape[0], where_ref.shape[0] // 4)
    observe(first, count_ref, where_ref, value_ref, rinv_ref, out_ref)


def outer_analysis(me_ref, obs_ref, whole_ref, *refs):
    outs = refs[:-SCRATCH]
    groups = len(outs)
    ins = [whole_ref.at[target(me_ref[0], k, groups)] for k in issue_order(groups)]
    analyse_kernel(obs_ref, ins, outs, *refs[-SCRATCH:])


def body(background, diffusion, advection, obs_where, obs_count, obs_value, obs_rinv):
    local, columns, entries = background.shape
    groups = lax.axis_size("mem")
    tiles = lax.axis_size("tile")
    half = columns // groups // 2
    size = background.size
    block = jax.ShapeDtypeStruct((half, local, entries), jnp.float32)
    whole = jax.ShapeDtypeStruct((groups, half, local, entries), jnp.float32)
    rest = jax.ShapeDtypeStruct((2, columns // 4 + 2, local, entries), jnp.float32)
    edge = jax.ShapeDtypeStruct((2, local, entries), jnp.float32)
    me = lax.axis_index("mem")[None].astype(jnp.int32)
    pieces = len(pieces_of(local))
    width = min(columns, 8)
    token = jax.ShapeDtypeStruct((8, entries), jnp.float32)
    scratch = [pltpu.VMEM((half, 8, entries), jnp.float32)] + sizes_of(half, local, entries, groups * local)
    flops = half * 180 * (groups * local) ** 2 * entries
    numbers = jax.ShapeDtypeStruct((8, entries), jnp.float32)

    low, high, numbers, counts = call(
        edge_kernel,
        [edge, edge, numbers, jax.ShapeDtypeStruct(obs_count.shape, jnp.int32)],
        0,
        16 * local * width * entries,
        in_specs=[HBM] * 4,
        scratch_shapes=[
            pltpu.VMEM((2, local, width, entries), jnp.float32),
            pltpu.SemaphoreType.DMA((5,)),
        ],
    )(*(in_hbm(x) for x in (background, diffusion, advection, obs_count)))
    before = lax.ppermute(high, "tile", [(i, (i + 1) % tiles) for i in range(tiles)])
    after = lax.ppermute(low, "tile", [((i + 1) % tiles, i) for i in range(tiles)])
    *inner, rest = call(
        inner_kernel,
        [block] * groups + [rest],
        20 * size,
        8 * size,
        in_specs=[SMEM] + [VMEM] * 2,
        scratch_shapes=[pltpu.VMEM((columns, local, entries), jnp.float32)],
    )(me, background, numbers)
    inner = exchange(inner)
    slots = (counts, obs_where[0], obs_value[0], obs_rinv[0])
    outer, done = call(
        outer_kernel,
        [whole, token],
        20 * size,
        8 * size,
        in_specs=[VMEM] * 4,
        out_specs=[HBM, VMEM],
        scratch_shapes=[
            pltpu.VMEM(whole.shape, jnp.float32),
            pltpu.SemaphoreType.DMA((4 if groups % 4 == 0 else 2,)),
        ],
    )(rest, before, after, numbers)
    outer = lax.all_to_all(outer, "mem", split_axis=0, concat_axis=0, tiled=True)

    inner, done = call(
        inner_analysis,
        [whole, token],
        flops,
        4 * size,
        in_specs=[SMEM] + [VMEM] * (groups + 5),
        scratch_shapes=scratch,
    )(me, done, *slots, *inner)
    inner = lax.all_to_all(inner, "mem", split_axis=0, concat_axis=0, tiled=True)
    obs = call(
        outer_observations,
        jax.ShapeDtypeStruct((half, 8, entries), jnp.float32),
        half * 32 * obs_where.shape[2] * entries,
        12 * obs_where.size,
        in_specs=[SMEM] + [VMEM] * 5,
    )(me, done, *slots)
    outer = call(
        outer_analysis,
        [block] * groups,
        flops,
        4 * size,
        in_specs=[SMEM] + [VMEM] * 2,
        scratch_shapes=scratch[1:],
    )(me, obs, outer)
    outer = exchange(outer)
    result = jax.ShapeDtypeStruct(background.shape, jnp.float32)
    made = call(
        inner_join_kernel,
        result,
        size,
        4 * size,
        in_specs=[VMEM, VMEM],
        out_specs=HBM,
        scratch_shapes=[
            pltpu.VMEM((local, groups * half, entries), jnp.float32),
            pltpu.SemaphoreType.DMA((pieces,)),
        ],
    )(outer[2], inner)
    return call(
        outer_join_kernel,
        result,
        size,
        4 * size,
        in_specs=[SMEM, HBM] + [VMEM] * groups,
        out_specs=HBM,
        scratch_shapes=[
            pltpu.VMEM((groups * half, local, entries), jnp.float32),
            pltpu.VMEM((local, groups * half, entries), jnp.float32),
            pltpu.SemaphoreType.DMA((2 * pieces,)),
        ],
        input_output_aliases={1: 0},
    )(me, made, *outer)


def solution(mesh):
    return jax.shard_map(
        body,
        mesh=mesh,
        in_specs=(
            P("mem", "tile", None),
            P(),
            P(),
            P("tile", None, None),
            P("tile", None),
            P("tile", None, None),
            P("tile", None, None),
        ),
        out_specs=P("mem", "tile", None),
        check_vma=False,
    )
```

```python
import jax
import jax.numpy as jnp
from jax import lax
from jax.experimental import pallas as pl
from jax.experimental.pallas import tpu as pltpu
from jax.sharding import PartitionSpec as P

PAIRS = 6
SCRATCH = 9
MIB = 1024 * 1024
SMEM = pl.BlockSpec(memory_space=pltpu.SMEM)
VMEM = pl.BlockSpec(memory_space=pltpu.VMEM)
HBM = pl.BlockSpec(memory_space=pltpu.HBM)


def call(kernel, out_shape, flops, moved, vmem=48 * MIB, **options):
    return pl.pallas_call(
        kernel,
        out_shape=out_shape,
        compiler_params=pltpu.CompilerParams(vmem_limit_bytes=vmem),
        cost_estimate=pl.CostEstimate(flops=flops, bytes_accessed=moved, transcendentals=0),
        **options,
    )


def in_hbm(x):
    return pltpu.with_memory_space_constraint(x, pltpu.HBM)


def target(me, k, groups):
    if groups & (groups - 1) == 0:
        return me ^ k
    return lax.rem(me + k, groups)


def source(me, k, groups):
    if groups & (groups - 1) == 0:
        return me ^ k
    return lax.rem(me + groups - k, groups)


def issue_order(groups):
    return sorted(range(1, groups), key=lambda k: (k != 1, -(k // 2).bit_count(), k)) + [0]


def exchange(blocks):
    groups = len(blocks)
    out = []
    for k, block in zip(issue_order(groups), blocks):
        pairs = [(i, i ^ k if groups & (groups - 1) == 0 else (i + k) % groups) for i in range(groups)]
        out.append(lax.ppermute(block, "mem", pairs) if k else block)
    return out


def split(x, parts):
    out = []
    for _ in range(parts):
        part = x.astype(jnp.bfloat16)
        out.append(part)
        x = x - part.astype(jnp.float32)
    return out


def store(ref, c, rows, x):
    for i, part in enumerate(split(x, 2)):
        ref[i, c, rows] = part


def multiply(a_ref, b_ref, c, rows):
    lhs = jnp.concatenate([a_ref[0, c, rows], a_ref[1, c, rows], a_ref[0, c, rows]], axis=1)
    rhs = jnp.concatenate([b_ref[0, c], b_ref[0, c], b_ref[1, c]], axis=0)
    return jnp.dot(lhs, rhs, preferred_element_type=jnp.float32)


def square_by_rows(parts):
    p0, p1, p2 = parts
    lhs = jnp.concatenate([p2, p0, p1, p1, p0, p0], axis=1)
    rhs = jnp.concatenate([p0, p2, p1, p0, p1, p0], axis=1)
    return lax.dot_general(lhs, rhs, (((1,), (1,)), ((), ())), preferred_element_type=jnp.float32)


def stencil(padded, diffusion, advection):
    middle = padded[1:-1]
    left = padded[:-2]
    right = padded[2:]
    return middle + diffusion * (left - 2.0 * middle + right) + advection * (0.5 * (left - right))


def inner_start(place, quarter):
    return place + quarter


def outer_start(place, quarter):
    return jnp.where(place < quarter, place, place + 2 * quarter)


def pieces_of(members):
    rows = 8 if members % 8 == 0 else members
    return [pl.ds(first, rows) for first in range(0, members, rows)]


def edge_kernel(state_ref, diff_ref, adv_ref, count_ref, low_ref, high_ref, num_ref, counts_ref, held_ref, sems):
    columns = state_ref.shape[1]
    width = held_ref.shape[2]
    reads = [
        pltpu.make_async_copy(state_ref.at[:, pl.ds(first, width)], held_ref.at[i], sems.at[i])
        for i, first in enumerate((0, columns - width))
    ]
    reads.append(pltpu.make_async_copy(diff_ref, num_ref.at[0], sems.at[2]))
    reads.append(pltpu.make_async_copy(adv_ref, num_ref.at[1], sems.at[3]))
    reads.append(pltpu.make_async_copy(count_ref, counts_ref, sems.at[4]))
    for copy in reads:
        copy.start()
    reads[0].wait()
    for i in range(2):
        low_ref[i] = held_ref[0, :, i]
    reads[1].wait()
    for i in range(2):
        high_ref[i] = held_ref[1, :, width - 2 + i]
    for copy in reads[2:]:
        copy.wait()


def inner_kernel(me_ref, state_ref, num_ref, *refs):
    *outs, rest_ref, turned_ref = refs
    groups = len(outs)
    half = outs[0].shape[0]
    columns = state_ref.shape[1]
    quarter = columns // 4
    turned_ref[...] = jnp.swapaxes(state_ref[...], 0, 1)
    diffusion = num_ref[0:1][None]
    advection = num_ref[1:2][None]
    for k, out_ref in zip(issue_order(groups), outs):
        x = turned_ref[pl.ds(target(me_ref[0], k, groups) * half + (quarter - 2), half + 4)]
        out_ref[...] = stencil(stencil(x, diffusion, advection), diffusion, advection)
    rest_ref[0] = turned_ref[: quarter + 2]
    rest_ref[1] = turned_ref[columns - quarter - 2 :]


def outer_kernel(rest_ref, before_ref, after_ref, num_ref, out_ref, done_ref, made_ref, sems):
    done_ref[...] = jnp.zeros_like(done_ref)
    groups, half, members, entries = out_ref.shape
    quarter = groups * half // 2
    owners = groups // sems.shape[0]
    diffusion = num_ref[0:1][None]
    advection = num_ref[1:2][None]
    low = jnp.concatenate([before_ref[...], rest_ref[0]], axis=0)
    high = jnp.concatenate([rest_ref[1], after_ref[...]], axis=0)
    writes = []
    for i in range(sems.shape[0]):
        first = i * owners * half
        padded, first = (low, first) if first < quarter else (high, first - quarter)
        x = padded[first : first + owners * half + 4]
        x = stencil(stencil(x, diffusion, advection), diffusion, advection)
        part = pl.ds(i * owners, owners)
        made_ref[part] = x.reshape(owners, half, members, entries)
        copy = pltpu.make_async_copy(made_ref.at[part], out_ref.at[part], sems.at[i])
        copy.start()
        writes.append(copy)
    for copy in writes:
        copy.wait()


def inner_join_kernel(after_ref, inner_ref, out_ref, made_ref, sems):
    del after_ref
    members, columns, entries = out_ref.shape
    groups, half, _, _ = inner_ref.shape
    quarter = columns // 4
    writes = []
    for i, part in enumerate(pieces_of(members)):
        x = inner_ref[:, :, part].reshape(groups * half, part.size, entries)
        made_ref[part] = jnp.swapaxes(x, 0, 1)
        copy = pltpu.make_async_copy(
            made_ref.at[part], out_ref.at[part, pl.ds(quarter, columns - 2 * quarter)], sems.at[i]
        )
        copy.start()
        writes.append(copy)
    for copy in writes:
        copy.wait()


def outer_join_kernel(me_ref, held_ref, *refs):
    del held_ref
    *outer, out_ref, turned_ref, made_ref, sems = refs
    members, columns, _ = out_ref.shape
    groups = len(outer)
    half = outer[0].shape[0]
    quarter = columns // 4
    writes = []
    for i, part in enumerate(pieces_of(members)):
        for k, block in zip(issue_order(groups), outer):
            turned_ref[pl.ds(source(me_ref[0], k, groups) * half, half), part] = block[:, part]
        made_ref[part] = jnp.swapaxes(turned_ref[:, part], 0, 1)
        for side in range(2):
            copy = pltpu.make_async_copy(
                made_ref.at[part, pl.ds(side * quarter, quarter)],
                out_ref.at[part, pl.ds(side * (columns - quarter), quarter)],
                sems.at[2 * i + side],
            )
            copy.start()
            writes.append(copy)
    for copy in writes:
        copy.wait()


def observe(first, count_ref, where_ref, value_ref, rinv_ref, out_ref):
    columns, _, entries = out_ref.shape
    slots = where_ref.shape[1]
    column = lax.broadcasted_iota(jnp.int32, count_ref.shape, 1)
    slot = lax.broadcasted_iota(jnp.int32, (1, slots), 1)
    row = lax.broadcasted_iota(jnp.int32, (16, slots), 0)
    entry = lax.broadcasted_iota(jnp.int32, (entries, slots), 0)
    for c in range(columns):
        at = first + c
        count = jnp.sum(jnp.where(column == at, count_ref[...], 0), axis=1, keepdims=True)
        weight = jnp.where(slot < count, rinv_ref[pl.ds(at, 1), :], 0.0)
        lhs = jnp.zeros((16, slots), jnp.float32)
        for line, values in ((0, weight), (3, weight * value_ref[pl.ds(at, 1), :])):
            for k, part in enumerate(split(values, 3)):
                lhs = jnp.where(row == line + k, part.astype(jnp.float32), lhs)
        onehot = (entry == where_ref[pl.ds(at, 1), :]).astype(jnp.float32).astype(jnp.bfloat16)
        sums = lax.dot_general(
            lhs.astype(jnp.bfloat16), onehot, (((1,), (1,)), ((), ())), preferred_element_type=jnp.float32
        )
        out_ref[c, 0:1] = sums[0:1] + (sums[1:2] + sums[2:3])
        out_ref[c, 1:2] = sums[3:4] + (sums[4:5] + sums[5:6])


def analyse_kernel(obs_ref, states, outs, root, mixed, ahead, s, p, u, t, r, w):
    groups = len(outs)
    columns, local, entries = outs[0].shape
    members = groups * local
    spread = members - 1.0
    every = range(columns)
    parts = [(c, pl.ds(half, members // 2)) for c in every for half in (0, members // 2)]
    rows = lax.broadcasted_iota(jnp.int32, (members, members), 0)
    cols = lax.broadcasted_iota(jnp.int32, (members, members), 1)
    means, forces, scales, grams = [], [], [], []
    for c in every:
        x = jnp.concatenate([ref[c] for ref in states], axis=0)
        mean = jnp.sum(x, axis=0, keepdims=True) * (1.0 / members)
        anomaly = x - mean
        total = obs_ref[c, 0:1]
        forces.append(obs_ref[c, 1:2] - total * mean)
        means.append(mean)
        grams.append(square_by_rows(split(anomaly * jnp.sqrt(total), 3)))
        ahead[c] = anomaly
        store(w.at[0], c, slice(None), anomaly)
    for c in every:
        gram = grams[c] + jnp.where(rows == cols, spread, 0.0)
        norm = jnp.sum(jnp.sum(gram * gram, axis=0, keepdims=True), axis=1, keepdims=True)
        scales.append(jnp.sqrt(norm))
        gram = gram * (1.0 / scales[c])
        root[c] = gram
        store(s, c, slice(None), gram)

    def advance(step, some):
        for c, rows in some:
            x = 2.25 * ahead[c, rows] + multiply(r.at[step % 2], w.at[step % 2], c, rows)
            ahead[c, rows] = x
            if step < PAIRS - 1:
                store(w.at[(step + 1) % 2], c, rows, x)

    gaps = [parts[::2], [], [], parts[1::2]]
    for step in range(PAIRS):
        for c, rows in parts:
            x = multiply(s, s, c, rows)
            y = root[c, rows]
            store(p, c, rows, x)
            store(u, c, rows, 0.0625 * x - 0.5625 * y)
            mixed[c, rows] = 1.6875 * x - 2.4375 * y
        if step > 0:
            advance(step - 1, gaps[0])
        for c, rows in parts:
            store(r.at[step % 2], c, rows, mixed[c, rows] + multiply(u, p, c, rows))
        if step > 0:
            advance(step - 1, gaps[1])
        if step < PAIRS - 1:
            for c, rows in parts:
                x = 2.25 * root[c, rows] + multiply(r.at[step % 2], s, c, rows)
                store(t, c, rows, x)
                mixed[c, rows] = 2.25 * x
        if step > 0:
            advance(step - 1, gaps[2])
        if step < PAIRS - 1:
            for c, rows in parts:
                x = mixed[c, rows] + multiply(t, r.at[step % 2], c, rows)
                root[c, rows] = x
                store(s, c, rows, x)
        if step > 0:
            advance(step - 1, gaps[3])
    advance(PAIRS - 1, parts)
    for c in every:
        x = ahead[c]
        inner = jnp.sum(x * forces[c], axis=1, keepdims=True)
        shift = jnp.sum(x * inner, axis=0, keepdims=True) / scales[c]
        result = means[c] + shift + x * jnp.sqrt(spread / scales[c])
        for k in range(groups):
            outs[k][c] = result[k * local : (k + 1) * local]


def sizes_of(columns, local, entries, members):
    full = pltpu.VMEM((columns, members, members), jnp.float32)
    pair = pltpu.VMEM((2, columns, members, members), jnp.bfloat16)
    two = pltpu.VMEM((2, 2, columns, members, members), jnp.bfloat16)
    ahead = pltpu.VMEM((columns, members, entries), jnp.float32)
    factor = pltpu.VMEM((2, 2, columns, members, entries), jnp.bfloat16)
    return [full, full, ahead, pair, pair, pair, pair, two, factor]


def inner_analysis(me_ref, after_ref, count_ref, where_ref, value_ref, rinv_ref, *refs):
    del after_ref
    *ins, whole_ref, done_ref, obs_ref = refs[:-SCRATCH]
    groups = len(ins)
    half = ins[0].shape[0]
    done_ref[...] = jnp.zeros_like(done_ref)
    outs = [whole_ref.at[source(me_ref[0], k, groups)] for k in issue_order(groups)]
    first = inner_start(me_ref[0] * half, where_ref.shape[0] // 4)
    observe(first, count_ref, where_ref, value_ref, rinv_ref, obs_ref)
    analyse_kernel(obs_ref, ins, outs, *refs[-SCRATCH:])


def outer_observations(me_ref, after_ref, count_ref, where_ref, value_ref, rinv_ref, out_ref):
    del after_ref
    first = outer_start(me_ref[0] * out_ref.shape[0], where_ref.shape[0] // 4)
    observe(first, count_ref, where_ref, value_ref, rinv_ref, out_ref)


def outer_analysis(me_ref, obs_ref, whole_ref, *refs):
    outs = refs[:-SCRATCH]
    groups = len(outs)
    ins = [whole_ref.at[target(me_ref[0], k, groups)] for k in issue_order(groups)]
    analyse_kernel(obs_ref, ins, outs, *refs[-SCRATCH:])


def body(background, diffusion, advection, obs_where, obs_count, obs_value, obs_rinv):
    local, columns, entries = background.shape
    groups = lax.axis_size("mem")
    tiles = lax.axis_size("tile")
    half = columns // groups // 2
    size = background.size
    block = jax.ShapeDtypeStruct((half, local, entries), jnp.float32)
    whole = jax.ShapeDtypeStruct((groups, half, local, entries), jnp.float32)
    rest = jax.ShapeDtypeStruct((2, columns // 4 + 2, local, entries), jnp.float32)
    edge = jax.ShapeDtypeStruct((2, local, entries), jnp.float32)
    me = lax.axis_index("mem")[None].astype(jnp.int32)
    pieces = len(pieces_of(local))
    width = min(columns, 8)
    token = jax.ShapeDtypeStruct((8, entries), jnp.float32)
    scratch = [pltpu.VMEM((half, 8, entries), jnp.float32)] + sizes_of(half, local, entries, groups * local)
    flops = half * 180 * (groups * local) ** 2 * entries
    numbers = jax.ShapeDtypeStruct((8, entries), jnp.float32)

    low, high, numbers, counts = call(
        edge_kernel,
        [edge, edge, numbers, jax.ShapeDtypeStruct(obs_count.shape, jnp.int32)],
        0,
        16 * local * width * entries,
        in_specs=[HBM] * 4,
        scratch_shapes=[
            pltpu.VMEM((2, local, width, entries), jnp.float32),
            pltpu.SemaphoreType.DMA((5,)),
        ],
    )(*(in_hbm(x) for x in (background, diffusion, advection, obs_count)))
    before = lax.ppermute(high, "tile", [(i, (i + 1) % tiles) for i in range(tiles)])
    after = lax.ppermute(low, "tile", [((i + 1) % tiles, i) for i in range(tiles)])
    *inner, rest = call(
        inner_kernel,
        [block] * groups + [rest],
        20 * size,
        8 * size,
        in_specs=[SMEM] + [VMEM] * 2,
        scratch_shapes=[pltpu.VMEM((columns, local, entries), jnp.float32)],
    )(me, background, numbers)
    inner = exchange(inner)
    slots = (counts, obs_where[0], obs_value[0], obs_rinv[0])
    outer, done = call(
        outer_kernel,
        [whole, token],
        20 * size,
        8 * size,
        in_specs=[VMEM] * 4,
        out_specs=[HBM, VMEM],
        scratch_shapes=[
            pltpu.VMEM(whole.shape, jnp.float32),
            pltpu.SemaphoreType.DMA((4 if groups % 4 == 0 else 2,)),
        ],
    )(rest, before, after, numbers)
    outer = lax.all_to_all(outer, "mem", split_axis=0, concat_axis=0, tiled=True)

    inner, done = call(
        inner_analysis,
        [whole, token],
        flops,
        4 * size,
        in_specs=[SMEM] + [VMEM] * (groups + 5),
        scratch_shapes=scratch,
    )(me, done, *slots, *inner)
    inner = lax.all_to_all(inner, "mem", split_axis=0, concat_axis=0, tiled=True)
    obs = call(
        outer_observations,
        jax.ShapeDtypeStruct((half, 8, entries), jnp.float32),
        half * 32 * obs_where.shape[2] * entries,
        12 * obs_where.size,
        in_specs=[SMEM] + [VMEM] * 5,
    )(me, done, *slots)
    outer = call(
        outer_analysis,
        [block] * groups,
        flops,
        4 * size,
        in_specs=[SMEM] + [VMEM] * 2,
        scratch_shapes=scratch[1:],
    )(me, obs, outer)
    outer = exchange(outer)
    result = jax.ShapeDtypeStruct(background.shape, jnp.float32)
    made = call(
        inner_join_kernel,
        result,
        size,
        4 * size,
        in_specs=[VMEM, VMEM],
        out_specs=HBM,
        scratch_shapes=[
            pltpu.VMEM((local, groups * half, entries), jnp.float32),
            pltpu.SemaphoreType.DMA((pieces,)),
        ],
    )(outer[2], inner)
    return call(
        outer_join_kernel,
        result,
        size,
        4 * size,
        in_specs=[SMEM, HBM] + [VMEM] * groups,
        out_specs=HBM,
        scratch_shapes=[
            pltpu.VMEM((groups * half, local, entries), jnp.float32),
            pltpu.VMEM((local, groups * half, entries), jnp.float32),
            pltpu.SemaphoreType.DMA((2 * pieces,)),
        ],
        input_output_aliases={1: 0},
    )(me, made, *outer)


def solution(mesh):
    return jax.shard_map(
        body,
        mesh=mesh,
        in_specs=(
            P("mem", "tile", None),
            P(),
            P(),
            P("tile", None, None),
            P("tile", None),
            P("tile", None, None),
            P("tile", None, None),
        ),
        out_specs=P("mem", "tile", None),
        check_vma=False,
    )
```
